32 devices in a mesh: head: 2 (over y), leaf: 16 (over z, x, core).
Axes of the slice: x: 2, y: 2, z: 4, core: 2. Of those that a mesh axis runs over, the one named last changes fastest.
Arguments:
- queries: bfloat16 [32, 128, 8192], P('leaf', None, 'head'), may hold values from -6 to 6
- keys: bfloat16 [32, 128, 1024], P('leaf', 'head'), may hold values from -6 to 6
- values: bfloat16 [32, 128, 1024], P('leaf', 'head'), may hold values from -6 to 6
- output_gradient: bfloat16 [32, 128, 8192], P('leaf', None, 'head'), may hold values from -6 to 6
- parents: int32 [32], P('leaf'), may hold values from -1 to 31, as said below
Outputs:
- grad_queries: bfloat16 [32, 128, 8192], P('leaf', None, 'head')
- key_gradient: bfloat16 [32, 128, 1024], P('leaf', 'head')
- value_gradient: bfloat16 [32, 128, 1024], P('leaf', 'head')
The draws below stay inside these ranges and needn't reach their ends.
Inputs may be any that keep to these rules, and one draw needn't show every extreme that they name: `parents`: block b is in tree b % 2 and its parent is in the same tree. In the tree of even blocks the parent lies below b and only block 0 is a root; in the tree of odd blocks the parent lies above b and only block 31 is a root. Every block has at most 2 ancestors, and some block has exactly 2.
All inputs are finite; a program needn't handle non-finite values.
Results may differ from the reference program's by a relative error of at most 0.012.
Values may be sent and summed in bfloat16 or wider, within the bound.
No kernel may reach another device: no remote copies, remote signals or barrier semaphores. Data moves between devices by JAX's collectives and lax.ppermute only.
A program may use at most 64 MiB of HBM per device.

```python
import jax
import jax.numpy as jnp
from jax import lax

QUERY_HEAD_COUNT = 64
KEY_VALUE_HEADS = 8
HEAD_DIM = 128
BLOCK_TOKENS = 128
NODE_BLOCKS = 32
MAX_ANCESTORS = 2


def grow_tree(key, count):
    hops = jax.random.randint(jax.random.fold_in(key, 1), (count,), 1, 3).astype(jnp.int32)

    def visit(state, index):
        depths, links = state
        near = (index - 1).astype(jnp.int32)

        def climb(step, node):
            return jnp.where(step < hops[index], links[node], node).astype(jnp.int32)
        lifted = lax.fori_loop(0, 2, climb, near)
        chosen = jnp.where(depths[near] < MAX_ANCESTORS, near, lifted).astype(jnp.int32)
        depths = depths.at[index].set(depths[chosen] + 1)
        links = links.at[index].set(chosen)
        return ((depths, links), chosen)
    start = (jnp.zeros((count,), jnp.int32), jnp.full((count,), -1, jnp.int32))
    _, chosen_all = lax.scan(visit, start, jnp.arange(1, count, dtype=jnp.int32))
    return jnp.concatenate([jnp.full((1,), -1, jnp.int32), chosen_all.astype(jnp.int32)])


def draw_parents(key, part):
    ranks = NODE_BLOCKS // 2
    lower = grow_tree(jax.random.fold_in(key, 31), ranks)
    upper = grow_tree(jax.random.fold_in(key, 37), ranks)
    lower_blocks = jnp.where(lower >= 0, 2 * lower, -1)
    mirrored = upper[::-1]
    upper_blocks = jnp.where(mirrored >= 0, 2 * (ranks - 1 - mirrored) + 1, -1)
    return jnp.stack([lower_blocks, upper_blocks], 1).reshape(NODE_BLOCKS).astype(jnp.int32)


def draw_queries(key, part):
    array_shape = (NODE_BLOCKS, BLOCK_TOKENS, QUERY_HEAD_COUNT * HEAD_DIM)
    draws = jnp.clip(jax.random.normal(jax.random.fold_in(key, 11), array_shape, jnp.float32), -6.0, 6.0)
    return draws.astype(jnp.bfloat16)


def draw_keys(key, part):
    array_shape = (NODE_BLOCKS, BLOCK_TOKENS, KEY_VALUE_HEADS * HEAD_DIM)
    draws = jnp.clip(jax.random.normal(jax.random.fold_in(key, 12), array_shape, jnp.float32), -6.0, 6.0)
    return draws.astype(jnp.bfloat16)


def level_of(own_key, extent, split, smallest, largest):
    factor_of, own = 1.0, jax.random.fold_in(own_key, 6)
    for position, blocks in split:
        steps = jnp.exp(jax.random.uniform(jax.random.fold_in(own, position), (blocks,), jnp.float32, smallest / len(split), largest / len(split)))
        factor_of = factor_of * jnp.repeat(steps, extent[position] // blocks).reshape([-1 if axis == position else 1 for axis in range(len(extent))])
    return factor_of


def normal_values(stream_key, dims, deviation, most, split=(), kind=jnp.bfloat16):
    values = jax.random.normal(stream_key, dims, jnp.float32) * deviation
    if len(split) > 0:
        values = level_of(stream_key, dims, split, -0.22, 0.18) * values
    return jnp.clip(values, min=-most, max=most).astype(kind)


def setup_inputs(seed: int = 0) -> dict:
    arg_keys = jax.random.split(jax.random.key(seed), 6)
    queries = draw_queries(jax.random.fold_in(arg_keys[5], 71), 0)
    keys = draw_keys(jax.random.fold_in(arg_keys[5], 71), 0)
    values = normal_values(arg_keys[2], (NODE_BLOCKS, BLOCK_TOKENS, KEY_VALUE_HEADS * HEAD_DIM), 1.0, 6.0, ((0, 16), (1, 2)))
    output_gradient = normal_values(arg_keys[3], (NODE_BLOCKS, BLOCK_TOKENS, QUERY_HEAD_COUNT * HEAD_DIM), 1.0, 6.0, ((0, 16), (2, 2)))
    parents = draw_parents(jax.random.fold_in(arg_keys[5], 71), 0)
    return {"queries": queries, "keys": keys, "values": values, "output_gradient": output_gradient, "parents": parents}


masked_score = -1.0e30


def follow_links(parent_table, chain_len):
    def extend(link_no, carry_in):
        current, ancestry = carry_in
        ancestry = ancestry.at[:, link_no].set(current)
        upward = jnp.where(current >= 0, parent_table[jnp.maximum(current, 0)], -1)
        return upward.astype(jnp.int32), ancestry
    start = jnp.full((parent_table.shape[0], chain_len), -1, jnp.int32)
    return lax.fori_loop(0, chain_len, extend, (parent_table.astype(jnp.int32), start))[1]


def reference(queries, keys, values, output_gradient, parents):
    heads_per_group = QUERY_HEAD_COUNT // KEY_VALUE_HEADS
    softmax_scale = HEAD_DIM ** -0.5
    ancestry = follow_links(parents, MAX_ANCESTORS)
    query_full = queries.astype(jnp.float32).reshape(NODE_BLOCKS, BLOCK_TOKENS, KEY_VALUE_HEADS, heads_per_group, HEAD_DIM)
    gradient_total = output_gradient.astype(jnp.float32).reshape(NODE_BLOCKS, BLOCK_TOKENS, KEY_VALUE_HEADS, heads_per_group, HEAD_DIM)
    key_full = keys.astype(jnp.float32).reshape(NODE_BLOCKS, BLOCK_TOKENS, KEY_VALUE_HEADS, HEAD_DIM)
    value_full = values.astype(jnp.float32).reshape(NODE_BLOCKS, BLOCK_TOKENS, KEY_VALUE_HEADS, HEAD_DIM)
    token_span = (MAX_ANCESTORS + 1) * BLOCK_TOKENS
    row_pos = jnp.arange(BLOCK_TOKENS, dtype=jnp.int32)[:, None]
    col_pos = jnp.arange(token_span, dtype=jnp.int32)[None, :]
    col_block = col_pos // BLOCK_TOKENS
    col_inner = col_pos % BLOCK_TOKENS

    def one_block(carry_in, index):
        key_running, value_running = carry_in
        chain = jnp.concatenate([index[None], ancestry[index]]).astype(jnp.int32)
        active = chain >= 0
        safe_value = jnp.maximum(chain, 0)
        block_keys = key_full[safe_value].reshape(token_span, KEY_VALUE_HEADS, HEAD_DIM)
        block_values = value_full[safe_value].reshape(token_span, KEY_VALUE_HEADS, HEAD_DIM)
        query_rows = query_full[index]
        grad_rows = gradient_total[index]
        visible = active[col_block] & ((col_block > 0) | (col_inner <= row_pos))
        scores = jnp.einsum("igrd,jgd->grij", query_rows, block_keys) * softmax_scale
        scores = jnp.where(visible, scores, masked_score)
        row_peak = jnp.max(scores, -1, keepdims=True)
        row_level = row_peak + jnp.log(jnp.sum(jnp.exp(scores - row_peak), -1, keepdims=True))
        weights = jnp.exp(scores - row_level)
        slopes = jnp.einsum("igrd,jgd->grij", grad_rows, block_values)
        row_mean = jnp.sum(weights * slopes, -1, keepdims=True)
        dscore = lax.optimization_barrier((weights * (slopes - row_mean)).astype(jnp.bfloat16)).astype(jnp.float32)
        rounded = lax.optimization_barrier(weights.astype(jnp.bfloat16)).astype(jnp.float32)
        query_grad = (softmax_scale * jnp.einsum("grij,jgd->igrd", dscore, block_keys)).astype(jnp.bfloat16)
        key_portion = softmax_scale * jnp.einsum("grij,igrd->jgd", dscore, query_rows)
        value_portion = jnp.einsum("grij,igrd->jgd", rounded, grad_rows)
        gate_flag = active.astype(jnp.float32)[:, None, None, None]
        key_running = key_running.at[safe_value].add(key_portion.reshape(MAX_ANCESTORS + 1, BLOCK_TOKENS, KEY_VALUE_HEADS, HEAD_DIM) * gate_flag)
        value_running = value_running.at[safe_value].add(value_portion.reshape(MAX_ANCESTORS + 1, BLOCK_TOKENS, KEY_VALUE_HEADS, HEAD_DIM) * gate_flag)
        return (key_running, value_running), query_grad.reshape(BLOCK_TOKENS, QUERY_HEAD_COUNT * HEAD_DIM)

    zero_running = jnp.zeros((NODE_BLOCKS, BLOCK_TOKENS, KEY_VALUE_HEADS, HEAD_DIM), jnp.float32)
    (key_running, value_running), query_grads = lax.scan(one_block, (zero_running, zero_running), jnp.arange(NODE_BLOCKS, dtype=jnp.int32))
    key_gradient = key_running.reshape(NODE_BLOCKS, BLOCK_TOKENS, KEY_VALUE_HEADS * HEAD_DIM).astype(jnp.bfloat16)
    value_gradient = value_running.reshape(NODE_BLOCKS, BLOCK_TOKENS, KEY_VALUE_HEADS * HEAD_DIM).astype(jnp.bfloat16)
    return query_grads, key_gradient, value_gradient
```

```python
import functools
import math

import jax
import jax.numpy as jnp
from jax import lax
from jax.experimental import pallas as pl
from jax.experimental.pallas import tpu as pltpu
from jax.sharding import PartitionSpec as P

QUERY_HEAD_COUNT = 64
KEY_VALUE_HEADS = 8
HEAD_DIM = 128

NT = (((1,), (1,)), ((), ()))
F32 = jnp.float32
BF16 = jnp.bfloat16


def dot(a, b, dims=(((1,), (0,)), ((), ()))):
    return lax.dot_general(a, b, dims, preferred_element_type=F32)


def attend_kernel(parents, rank, q_ref, do_ref, self_ref, anc_ref, dq_ref, dself_ref, danc_ref, qs, dos, ps, ds):
    depth = anc_ref.shape[1]
    rows = q_ref.shape[1]
    heads = q_ref.shape[2] // HEAD_DIM
    scale = HEAD_DIM ** (-0.5)
    c = scale * math.log2(math.e)
    block = 2 * rank[0] + pl.program_id(0)
    valid = []
    for _ in range(depth):
        block = jnp.where(block >= 0, parents[jnp.maximum(block, 0)], -1)
        valid.append(block >= 0)

    def whole(ref, *at):
        tile = ref[(slice(None),) + at]
        return tile.reshape(rows, HEAD_DIM)

    keys = jnp.concatenate([whole(self_ref, 0, 0)] + [whole(anc_ref, k, 0) for k in range(depth)], 0)
    values = jnp.concatenate([whole(self_ref, 1, 0)] + [whole(anc_ref, k, 1) for k in range(depth)], 0)
    keys_t = keys.T
    for h in range(heads):
        qs[h * rows : (h + 1) * rows, :] = q_ref[0, :, h * HEAD_DIM : (h + 1) * HEAD_DIM]
        dos[h * rows : (h + 1) * rows, :] = do_ref[0, :, h * HEAD_DIM : (h + 1) * HEAD_DIM]
    hidden = lax.broadcasted_iota(jnp.int32, (rows, rows), 0) > lax.broadcasted_iota(jnp.int32, (rows, rows), 1)
    for h in range(heads):
        part = slice(h * rows, (h + 1) * rows)
        scores = dot(keys, qs[part, :], NT)
        slopes = dot(values, dos[part, :], NT)
        s = [scores[k * rows : (k + 1) * rows] for k in range(depth + 1)]
        d = [slopes[k * rows : (k + 1) * rows] for k in range(depth + 1)]
        s[0] = jnp.where(hidden, -1e30, s[0])
        peak = jnp.max(s[0], 0, keepdims=True)
        for k in range(depth):
            peak = jnp.maximum(peak, jnp.where(valid[k], jnp.max(s[k + 1], 0, keepdims=True), -1e30))
        peak = peak * c
        e = [jnp.exp2(s[0] * c - peak)]
        for k in range(depth):
            e.append(jnp.exp2(s[k + 1] * c - jnp.where(valid[k], peak, 1e30)))
        total = functools.reduce(jnp.add, [jnp.sum(x, 0, keepdims=True) for x in e])
        weighted = functools.reduce(jnp.add, [jnp.sum(x * y, 0, keepdims=True) for x, y in zip(e, d)])
        inverse = 1.0 / total
        mean = weighted * inverse
        for k in range(depth + 1):
            p = e[k] * inverse
            ps[k * rows : (k + 1) * rows, part] = p.astype(BF16)
            ds[k * rows : (k + 1) * rows, part] = (p * (d[k] - mean)).astype(BF16)
        dq_t = dot(keys_t, ds[:, part])
        dq_ref[0, :, h * HEAD_DIM : (h + 1) * HEAD_DIM] = (dq_t * scale).T.astype(BF16)
    dkey = (dot(ds[...], qs[...]) * scale).astype(BF16)
    dvalue = dot(ps[...], dos[...]).astype(BF16)
    hubs, pieces = self_ref.shape[0], self_ref.shape[3]

    def piece(x, k):
        return x[k * rows : (k + 1) * rows].reshape(hubs, pieces, HEAD_DIM)

    dself_ref[:, 0, 0] = piece(dkey, 0)
    dself_ref[:, 1, 0] = piece(dvalue, 0)
    for k in range(depth):
        danc_ref[:, k, 0] = piece(dkey, k + 1)
        danc_ref[:, k, 1] = piece(dvalue, k + 1)


def attend(parents, rank, queries, output_gradient, own, foreign):
    trees, rows, width = queries.shape
    hubs, _, _, pieces, kv_width = own.shape
    depth = foreign.shape[1] // trees
    groups = kv_width // HEAD_DIM
    heads = width // groups // HEAD_DIM
    span = (depth + 1) * rows
    smem = pl.BlockSpec(memory_space=pltpu.SMEM)
    q_spec = pl.BlockSpec((1, rows, heads * HEAD_DIM), lambda t, g: (t, 0, g))
    own_spec = pl.BlockSpec((hubs, 2, 1, pieces, HEAD_DIM), lambda t, g: (0, 0, t, 0, g))
    anc_spec = pl.BlockSpec((hubs, depth, 2, pieces, HEAD_DIM), lambda t, g: (0, t, 0, 0, g))
    return pl.pallas_call(
        attend_kernel,
        grid=(trees, groups),
        in_specs=[smem, smem, q_spec, q_spec, own_spec, anc_spec],
        out_specs=[q_spec, own_spec, anc_spec],
        out_shape=[
            jax.ShapeDtypeStruct(queries.shape, BF16),
            jax.ShapeDtypeStruct(own.shape, BF16),
            jax.ShapeDtypeStruct(foreign.shape, BF16),
        ],
        scratch_shapes=[
            pltpu.VMEM((heads * rows, HEAD_DIM), BF16),
            pltpu.VMEM((heads * rows, HEAD_DIM), BF16),
            pltpu.VMEM((span, heads * rows), BF16),
            pltpu.VMEM((span, heads * rows), BF16),
        ],
        compiler_params=pltpu.CompilerParams(vmem_limit_bytes=40 * 1024 * 1024),
    )(parents, rank, queries, output_gradient, own, foreign)


def each_need(parents, rank, half, depth, act):
    base = (rank[0] // half) * half

    def leaf(d, _):
        for t in range(2):
            block = 2 * (base + d) + t
            for k in range(depth):
                block = jnp.where(block >= 0, parents[jnp.maximum(block, 0)], -1)
                p = block // 2
                here = (p >= base) & (p < base + half)
                act(d, t * depth + k, block >= 0, here, p % half, t)
        return 0

    lax.fori_loop(0, half, leaf, 0)


def pick_kernel(depth, parents, rank, own_ref, cross_ref, out_ref):
    half = own_ref.shape[0]

    def act(d, slot, valid, here, p, t):
        @pl.when(here | ~valid)
        def _():
            out_ref[d, slot] = own_ref[p, :, t]

        @pl.when(valid & ~here)
        def _():
            out_ref[d, slot] = cross_ref[p]

    each_need(parents, rank, half, depth, act)


def collect_kernel(depth, parents, rank, in_ref, own_ref, cross_ref, cross_sum):
    half = own_ref.shape[0]
    own_ref[...] = jnp.zeros_like(own_ref)
    cross_sum[...] = jnp.zeros_like(cross_sum)

    def act(d, slot, valid, here, p, t):
        @pl.when(valid & here)
        def _():
            own_ref[p, :, t] += in_ref[d, slot].astype(F32)

        @pl.when(valid & ~here)
        def _():
            cross_sum[p] += in_ref[d, slot].astype(F32)

    each_need(parents, rank, half, depth, act)
    cross_ref[...] = cross_sum[...].astype(BF16)


def body(queries, keys, values, output_gradient, parents):
    leaf_count = lax.axis_size("leaf")
    head_count = lax.axis_size("head")
    half = leaf_count // 2
    depth = leaf_count // 4 - 2
    leaf_rank = lax.axis_index("leaf")
    rank = leaf_rank.astype(jnp.int32).reshape(1)
    upper = leaf_rank >= half
    groups = [[half * i + j for j in range(half)] for i in range(2)]
    swap = [(i, (i + half) % leaf_count) for i in range(leaf_count)]
    trees, part_rows, kv_all = keys.shape
    kv_width = kv_all // head_count
    rows = part_rows * head_count
    pieces = rows // half
    share = half // head_count
    vmem = pl.BlockSpec(memory_space=pltpu.VMEM)
    smem = pl.BlockSpec(memory_space=pltpu.SMEM)
    params = pltpu.CompilerParams(vmem_limit_bytes=40 * 1024 * 1024)

    def exchange(x):
        return lax.all_to_all(x, "leaf", 0, 0, tiled=True, axis_index_groups=groups)

    all_parents = lax.all_gather(parents, "leaf", axis=0, tiled=True)

    pair = jnp.stack([keys, values]).reshape(2, trees, share, pieces, head_count, kv_width)
    pair = pair.transpose(4, 2, 0, 1, 3, 5)
    if head_count > 1:
        pair = lax.all_to_all(pair, "head", 0, 0, tiled=True)
    mine = pair.reshape(half, 2, trees, pieces, kv_width)
    hub_own = exchange(mine)
    hub_cross = lax.ppermute(jnp.where(upper, hub_own[:, :, 1], hub_own[:, :, 0]), "leaf", swap)
    picked = pl.pallas_call(
        functools.partial(pick_kernel, depth),
        in_specs=[smem, smem, vmem, vmem],
        out_specs=vmem,
        out_shape=jax.ShapeDtypeStruct((half, trees * depth, 2, pieces, kv_width), BF16),
        compiler_params=params,
    )(all_parents, rank, hub_own, hub_cross)
    foreign = exchange(picked)

    if pieces % 16:
        mine_rows = mine.transpose(1, 2, 0, 3, 4).reshape(1, 2, trees, rows, kv_width)
        foreign_rows = foreign.transpose(1, 2, 0, 3, 4).reshape(1, trees * depth, 2, rows, kv_width)
    else:
        mine_rows, foreign_rows = mine, foreign
    query_grad, self_grad, foreign_grad = attend(
        all_parents, rank, queries, output_gradient, mine_rows, foreign_rows
    )
    if pieces % 16:
        def split(x):
            return x.reshape(x.shape[1:3] + (half, pieces, kv_width)).transpose(2, 0, 1, 3, 4)
        self_grad, foreign_grad = split(self_grad), split(foreign_grad)

    back = exchange(foreign_grad)
    own_sum, cross_sum = pl.pallas_call(
        functools.partial(collect_kernel, depth),
        in_specs=[smem, smem, vmem],
        out_specs=[vmem, vmem],
        out_shape=[
            jax.ShapeDtypeStruct((half, 2, trees, pieces, kv_width), F32),
            jax.ShapeDtypeStruct((half, 2, pieces, kv_width), BF16),
        ],
        scratch_shapes=[pltpu.VMEM((half, 2, pieces, kv_width), F32)],
        compiler_params=params,
    )(all_parents, rank, back)
    crossed = lax.ppermute(cross_sum, "leaf", swap).astype(F32)
    is_left = (jnp.arange(trees) == jnp.where(upper, 1, 0))[None, None, :, None, None]
    hub_total = (own_sum + jnp.where(is_left, crossed[:, :, None], 0.0)).astype(BF16)
    returned = exchange(hub_total)
    total = (returned.astype(F32) + self_grad.astype(F32)).astype(BF16)
    total = total.reshape(head_count, share, 2, trees, pieces, kv_width)
    if head_count > 1:
        total = lax.all_to_all(total, "head", 0, 0, tiled=True)
    total = total.transpose(2, 3, 1, 4, 0, 5).reshape(2, trees, part_rows, kv_all)
    return query_grad, total[0], total[1]


def solution(mesh):
    in_specs = (
        P("leaf", None, "head"),
        P("leaf", "head", None),
        P("leaf", "head", None),
        P("leaf", None, "head"),
        P("leaf"),
    )
    out_specs = (P("leaf", None, "head"), P("leaf", "head", None), P("leaf", "head", None))
    return jax.shard_map(body, mesh=mesh, in_specs=in_specs, out_specs=out_specs, check_vma=False)
```

```python
import functools
import math

import jax
import jax.numpy as jnp
from jax import lax
from jax.experimental import pallas as pl
from jax.experimental.pallas import tpu as pltpu
from jax.sharding import PartitionSpec as P

HEAD_DIM = 128

NT = (((1,), (1,)), ((), ()))
NN = (((1,), (0,)), ((), ()))
F32 = jnp.float32
BF16 = jnp.bfloat16
VMEM = pl.BlockSpec(memory_space=pltpu.VMEM)
SMEM = pl.BlockSpec(memory_space=pltpu.SMEM)
PARAMS = pltpu.CompilerParams(vmem_limit_bytes=40 * 1024 * 1024)


def dot(a, b, dims=NN):
    return lax.dot_general(a, b, dims, preferred_element_type=F32)


def attend_kernel(
    place, parents, q_ref, do_ref, self_ref, anc_ref, _, dq_ref, dself_ref, danc_ref, qs, dos, ps, ds
):
    hubs, depth, _, pieces, _ = anc_ref.shape
    rows = q_ref.shape[1]
    heads = q_ref.shape[2] // HEAD_DIM
    scale = HEAD_DIM ** (-0.5)
    c = scale * math.log2(math.e)
    block = 2 * place[0] + place[1]
    valid = []
    for _ in range(depth):
        block = jnp.where(block >= 0, parents[jnp.maximum(block, 0)], -1)
        valid.append(block >= 0)

    def seen(which):
        tiles = [anc_ref[:, k, which].reshape(rows, HEAD_DIM) for k in range(depth)]
        return jnp.concatenate([self_ref[which, 0]] + tiles, 0)

    keys, values = seen(0), seen(1)
    for h in range(heads):
        qs[h * rows : (h + 1) * rows, :] = q_ref[0, :, h * HEAD_DIM : (h + 1) * HEAD_DIM]
        dos[h * rows : (h + 1) * rows, :] = do_ref[0, :, h * HEAD_DIM : (h + 1) * HEAD_DIM]
    hidden = lax.broadcasted_iota(jnp.int32, (rows, rows), 0) > lax.broadcasted_iota(jnp.int32, (rows, rows), 1)
    scores = dot(keys, qs[...], NT)
    slopes = dot(values, dos[...], NT)
    for h in range(heads):
        part = slice(h * rows, (h + 1) * rows)
        s = [scores[k * rows : (k + 1) * rows, part] for k in range(depth + 1)]
        d = [slopes[k * rows : (k + 1) * rows, part] for k in range(depth + 1)]
        s[0] = jnp.where(hidden, -1e30, s[0])
        peak = jnp.max(s[0], 0, keepdims=True)
        for k in range(depth):
            peak = jnp.maximum(peak, jnp.where(valid[k], jnp.max(s[k + 1], 0, keepdims=True), -1e30))
        peak = peak * c
        e = [jnp.exp2(s[0] * c - peak)]
        for k in range(depth):
            e.append(jnp.exp2(s[k + 1] * c - jnp.where(valid[k], peak, 1e30)))
        total = functools.reduce(jnp.add, [jnp.sum(x, 0, keepdims=True) for x in e])
        weighted = functools.reduce(jnp.add, [jnp.sum(x * y, 0, keepdims=True) for x, y in zip(e, d)])
        inverse = 1.0 / total
        mean = weighted * inverse
        for k in range(depth + 1):
            p = e[k] * inverse
            ps[k * rows : (k + 1) * rows, part] = p.astype(BF16)
            ds[k * rows : (k + 1) * rows, part] = (p * (d[k] - mean)).astype(BF16)
    dq_t = dot(keys.T, ds[...]) * scale
    for h in range(heads):
        dq_ref[0, :, h * HEAD_DIM : (h + 1) * HEAD_DIM] = dq_t[:, h * rows : (h + 1) * rows].T.astype(BF16)
    grads = [dot(ds[...], qs[...]) * scale, dot(ps[...], dos[...])]
    for which in range(2):
        dself_ref[which] = grads[which][:rows].astype(BF16)
        for k in range(depth):
            grad = grads[which][(k + 1) * rows : (k + 2) * rows].astype(BF16)
            danc_ref[:, k, which] = grad.reshape(hubs, pieces, HEAD_DIM)


def attend(place, parents, queries, output_gradient, own, foreign, query_grad):
    _, rows, width = queries.shape
    hubs, depth, _, pieces, kv_width = foreign.shape
    groups = kv_width // HEAD_DIM
    heads = width // groups // HEAD_DIM
    span = (depth + 1) * rows
    q_spec = pl.BlockSpec((1, rows, heads * HEAD_DIM), lambda g, place, _: (place[1], 0, g))
    own_spec = pl.BlockSpec((2, 1, rows, HEAD_DIM), lambda g, place, _: (0, place[1], 0, g))
    dself_spec = pl.BlockSpec((2, rows, HEAD_DIM), lambda g, place, _: (0, 0, g))
    anc_spec = pl.BlockSpec((hubs, depth, 2, pieces, HEAD_DIM), lambda g, place, _: (0, 0, 0, 0, g))
    hbm = pl.BlockSpec(memory_space=pl.ANY)
    first = query_grad is None
    return pl.pallas_call(
        attend_kernel,
        grid_spec=pltpu.PrefetchScalarGridSpec(
            num_scalar_prefetch=2,
            grid=(groups,),
            in_specs=[q_spec, q_spec, own_spec, anc_spec, SMEM if first else hbm],
            out_specs=[q_spec, dself_spec, anc_spec],
            scratch_shapes=[
                pltpu.VMEM((heads * rows, HEAD_DIM), BF16),
                pltpu.VMEM((heads * rows, HEAD_DIM), BF16),
                pltpu.VMEM((span, heads * rows), BF16),
                pltpu.VMEM((span, heads * rows), BF16),
            ],
        ),
        out_shape=[
            jax.ShapeDtypeStruct(queries.shape, BF16),
            jax.ShapeDtypeStruct((2, rows, kv_width), BF16),
            jax.ShapeDtypeStruct(foreign.shape, BF16),
        ],
        input_output_aliases={} if first else {6: 0},
        compiler_params=PARAMS,
        cost_estimate=pl.CostEstimate(
            flops=10 * groups * heads * span * rows * HEAD_DIM,
            bytes_accessed=6 * rows * width,
            transcendentals=groups * heads * span * rows,
        ),
    )(place, parents, queries, output_gradient, own, foreign, place if first else query_grad)


def each_need(place, parents, half, depth, which, act):
    base = (place[0] // half) * half
    t = place[1 + which]

    def leaf(d, _):
        block = 2 * (base + d) + t
        for k in range(depth):
            block = jnp.where(block >= 0, parents[jnp.maximum(block, 0)], -1)
            p = block // 2
            act(d, k, block >= 0, (p >= base) & (p < base + half), p % half, t)
        return 0

    lax.fori_loop(0, half, leaf, 0)


def pick_near_kernel(place, parents, own_ref, out_ref):
    half, depth = out_ref.shape[:2]

    def act(d, slot, valid, here, p, t):
        out_ref[d, slot] = own_ref[p, :, t]

    each_need(place, parents, half, depth, 0, act)


def pick_far_kernel(place, parents, own_ref, cross_ref, out_ref):
    half, depth = out_ref.shape[:2]

    def act(d, slot, valid, here, p, t):
        @pl.when(here | ~valid)
        def _():
            out_ref[d, slot] = own_ref[p, :, t]

        @pl.when(valid & ~here)
        def _():
            out_ref[d, slot] = cross_ref[p]

    each_need(place, parents, half, depth, 1, act)


def collect_near_kernel(place, parents, in_ref, own_ref):
    half, depth = in_ref.shape[:2]
    own_ref[...] = jnp.zeros_like(own_ref)

    def act(d, slot, valid, here, p, t):
        @pl.when(valid)
        def _():
            own_ref[p] += in_ref[d, slot].astype(F32)

    each_need(place, parents, half, depth, 0, act)


def collect_far_kernel(place, parents, in_ref, own_ref, cross_ref, sums):
    half, depth = in_ref.shape[:2]
    sums[...] = jnp.zeros_like(sums)

    def act(d, slot, valid, here, p, t):
        @pl.when(valid)
        def _():
            sums[jnp.where(here, 0, half) + p] += in_ref[d, slot].astype(F32)

    each_need(place, parents, half, depth, 1, act)
    own_ref[...] = sums[:half].astype(BF16)
    cross_ref[...] = sums[half:].astype(BF16)


def body(queries, keys, values, output_gradient, parents):
    leaf_count = lax.axis_size("leaf")
    head_count = lax.axis_size("head")
    half = leaf_count // 2
    depth = leaf_count // 4 - 2
    leaf_rank = lax.axis_index("leaf")
    head_rank = lax.axis_index("head")
    upper = leaf_rank >= half
    near = jnp.where(upper, 1, 0)
    place = jnp.stack([leaf_rank, near, 1 - near]).astype(jnp.int32)
    far_place = jnp.stack([leaf_rank, 1 - near]).astype(jnp.int32)
    sides = [[half * i + j for j in range(half)] for i in range(2)]
    both = [[leaf_count * h + j for h in range(head_count) for j in side] for side in sides]
    swap = [(i, (i + half) % leaf_count) for i in range(leaf_count)]
    trees, part_rows, kv_all = keys.shape
    kv_width = kv_all // head_count
    rows = part_rows * head_count
    pieces = rows // half
    merged = head_count == 2 and part_rows % half == 0
    bits = part_rows // half if merged else 0

    def exchange(x):
        return lax.all_to_all(x, "leaf", 0, 0, tiled=True, axis_index_groups=sides)

    def exchange_both(x):
        return lax.all_to_all(x, ("head", "leaf"), 0, 0, tiled=True, axis_index_groups=both)

    def to_other_head(x):
        return lax.ppermute(x, "head", [(0, 1), (1, 0)])

    def other(x, axis):
        return lax.dynamic_index_in_dim(x, 1 - head_rank, axis, keepdims=False)

    def this(x, axis):
        return lax.dynamic_index_in_dim(x, head_rank, axis, keepdims=False)

    def by_head(mine, theirs, axis):
        low = jnp.where(head_rank == 0, mine, theirs)
        high = jnp.where(head_rank == 0, theirs, mine)
        return jnp.stack([low, high], axis)

    all_parents = lax.all_gather(parents, "leaf", axis=0, tiled=True)

    pair = jnp.stack([keys, values]).reshape(2, trees, part_rows, head_count, kv_width)
    if merged:
        pair = jnp.moveaxis(pair, 3, 0)
        send = pair.reshape(2, 2, trees, half, bits, kv_width).transpose(0, 3, 1, 2, 4, 5)
        arrived = exchange_both(send.reshape(2 * half, 2, trees, bits, kv_width))
        arrived = arrived.reshape(2, half, 2, trees, bits, kv_width).transpose(1, 2, 3, 0, 4, 5)
        hub_own = arrived.reshape(half, 2, trees, pieces, kv_width)
        theirs = to_other_head(other(pair, 0))
        mine = by_head(this(pair, 0), theirs, 2).reshape(2, trees, rows, kv_width)
    else:
        pair = jnp.moveaxis(pair, 3, 0)
        if head_count > 1:
            pair = lax.all_to_all(pair, "head", 0, 0, tiled=True)
        mine = pair.transpose(1, 2, 0, 3, 4).reshape(2, trees, rows, kv_width)
        hub_own = exchange(mine.reshape(2, trees, half, pieces, kv_width).transpose(2, 0, 1, 3, 4))

    hub_cross = lax.ppermute(jnp.where(upper, hub_own[:, :, 1], hub_own[:, :, 0]), "leaf", swap)
    picked_shape = jax.ShapeDtypeStruct((half, depth, 2, pieces, kv_width), BF16)
    picked_near = pl.pallas_call(
        pick_near_kernel,
        in_specs=[SMEM, SMEM, VMEM],
        out_specs=VMEM,
        out_shape=picked_shape,
        compiler_params=PARAMS,
    )(place, all_parents, hub_own)
    foreign_near = exchange(picked_near)
    picked_far = pl.pallas_call(
        pick_far_kernel,
        in_specs=[SMEM, SMEM, VMEM, VMEM],
        out_specs=VMEM,
        out_shape=picked_shape,
        compiler_params=PARAMS,
    )(place, all_parents, hub_own, hub_cross)
    foreign_far = exchange(picked_far)

    def gather_rows(x):
        if pieces % 16 == 0:
            return x
        return x.transpose(1, 2, 0, 3, 4).reshape(1, depth, 2, rows, kv_width)

    def spread_rows(x):
        if pieces % 16 == 0:
            return x
        return x.reshape(depth, 2, half, pieces, kv_width).transpose(2, 0, 1, 3, 4)

    query_grad, self_near, grad_near = attend(
        place, all_parents, queries, output_gradient, mine, gather_rows(foreign_near), None
    )
    query_grad, self_far, grad_far = attend(
        far_place, all_parents, queries, output_gradient, mine, gather_rows(foreign_far), query_grad
    )
    back_near = exchange(spread_rows(grad_near))
    back_far = exchange(spread_rows(grad_far))

    sum_shape = (half, 2, pieces, kv_width)
    far_sum, cross_sum = pl.pallas_call(
        collect_far_kernel,
        in_specs=[SMEM, SMEM, VMEM],
        out_specs=[VMEM, VMEM],
        out_shape=[jax.ShapeDtypeStruct(sum_shape, BF16)] * 2,
        scratch_shapes=[pltpu.VMEM((2 * half,) + sum_shape[1:], F32)],
        compiler_params=PARAMS,
    )(place, all_parents, back_far)
    near_sum = pl.pallas_call(
        collect_near_kernel,
        in_specs=[SMEM, SMEM, VMEM],
        out_specs=VMEM,
        out_shape=jax.ShapeDtypeStruct(sum_shape, F32),
        compiler_params=PARAMS,
    )(place, all_parents, back_near)
    crossed = lax.ppermute(cross_sum, "leaf", swap)
    near_sum = (near_sum + crossed.astype(F32)).astype(BF16)
    hub_sum = jnp.stack([near_sum, far_sum], 1)
    self_sum = jnp.stack([self_near, self_far])
    if merged:
        hub_sum = hub_sum.reshape(half, 2, 2, 2, bits, kv_width).transpose(3, 0, 1, 2, 4, 5)
        returned = exchange_both(hub_sum.reshape(2 * half, 2, 2, bits, kv_width))
        returned = returned.reshape(2, half, 2, 2, bits, kv_width).transpose(0, 2, 3, 1, 4, 5)
        returned = returned.reshape(2, 2, 2, part_rows, kv_width)
        self_sum = self_sum.reshape(2, 2, 2, part_rows, kv_width)
        theirs = to_other_head(other(self_sum, 2))
        total = returned.astype(F32) + by_head(this(self_sum, 2), theirs, 0).astype(F32)
        total = total.astype(BF16)
    else:
        returned = exchange(hub_sum).transpose(1, 2, 0, 3, 4).reshape(2, 2, rows, kv_width)
        total = (returned.astype(F32) + self_sum.astype(F32)).astype(BF16)
        total = jnp.moveaxis(total.reshape(2, 2, head_count, part_rows, kv_width), 2, 0)
        if head_count > 1:
            total = lax.all_to_all(total, "head", 0, 0, tiled=True)
    total = total.transpose(2, 1, 3, 0, 4).reshape(2, 2, part_rows, kv_all)
    total = jnp.where(upper, total[:, ::-1], total)
    return query_grad, total[0], total[1]


def solution(mesh):
    in_specs = (
        P("leaf", None, "head"),
        P("leaf", "head", None),
        P("leaf", "head", None),
        P("leaf", None, "head"),
        P("leaf"),
    )
    out_specs = (P("leaf", None, "head"), P("leaf", "head", None), P("leaf", "head", None))
    return jax.shard_map(body, mesh=mesh, in_specs=in_specs, out_specs=out_specs, check_vma=False)
```

```python
import functools
import math

import jax
import jax.numpy as jnp
from jax import lax
from jax.experimental import pallas as pl
from jax.experimental.pallas import tpu as pltpu
from jax.sharding import PartitionSpec as P

HEAD_DIM = 128

NT = (((1,), (1,)), ((), ()))
NN = (((1,), (0,)), ((), ()))
F32 = jnp.float32
BF16 = jnp.bfloat16
VMEM = pl.BlockSpec(memory_space=pltpu.VMEM)
SMEM = pl.BlockSpec(memory_space=pltpu.SMEM)
PARAMS = pltpu.CompilerParams(vmem_limit_bytes=40 * 1024 * 1024)


def dot(a, b, dims=NN):
    return lax.dot_general(a, b, dims, preferred_element_type=F32)


def attend_kernel(parts, first, place, parents, q_ref, do_ref, *refs):
    own_refs, anc_ref = refs[:parts], refs[parts]
    refs = refs[parts + (1 if first else 2) :]
    dq_ref, dself_refs, danc_ref = refs[0], refs[1 : 1 + parts], refs[1 + parts]
    qs, dos, ps, ds = refs[2 + parts :]
    hubs, depth, _, pieces, _ = anc_ref.shape
    rows = q_ref.shape[1]
    heads = q_ref.shape[2] // HEAD_DIM
    scale = HEAD_DIM ** (-0.5)
    c = scale * math.log2(math.e)
    block = 2 * place[0] + place[1]
    valid = []
    for _ in range(depth):
        block = jnp.where(block >= 0, parents[jnp.maximum(block, 0)], -1)
        valid.append(block >= 0)

    def seen(which):
        tiles = [anc_ref[:, k, which].reshape(rows, HEAD_DIM) for k in range(depth)]
        return jnp.concatenate([ref[which, 0] for ref in own_refs] + tiles, 0)

    keys, values = seen(0), seen(1)
    for h in range(heads):
        qs[h * rows : (h + 1) * rows, :] = q_ref[0, :, h * HEAD_DIM : (h + 1) * HEAD_DIM]
        dos[h * rows : (h + 1) * rows, :] = do_ref[0, :, h * HEAD_DIM : (h + 1) * HEAD_DIM]
    token = lax.rem(lax.broadcasted_iota(jnp.int32, (rows, rows), 0) + place[2], rows)
    hidden = token > lax.broadcasted_iota(jnp.int32, (rows, rows), 1)
    scores = dot(keys, qs[...], NT)
    slopes = dot(values, dos[...], NT)
    for h in range(heads):
        part = slice(h * rows, (h + 1) * rows)
        s = [scores[k * rows : (k + 1) * rows, part] for k in range(depth + 1)]
        d = [slopes[k * rows : (k + 1) * rows, part] for k in range(depth + 1)]
        s[0] = jnp.where(hidden, -1e30, s[0])
        peak = jnp.max(s[0], 0, keepdims=True)
        for k in range(depth):
            peak = jnp.maximum(peak, jnp.where(valid[k], jnp.max(s[k + 1], 0, keepdims=True), -1e30))
        peak = peak * c
        e = [jnp.exp2(s[0] * c - peak)]
        for k in range(depth):
            e.append(jnp.exp2(s[k + 1] * c - jnp.where(valid[k], peak, 1e30)))
        total = functools.reduce(jnp.add, [jnp.sum(x, 0, keepdims=True) for x in e])
        weighted = functools.reduce(jnp.add, [jnp.sum(x * y, 0, keepdims=True) for x, y in zip(e, d)])
        inverse = 1.0 / total
        mean = weighted * inverse
        for k in range(depth + 1):
            p = e[k] * inverse
            ps[k * rows : (k + 1) * rows, part] = p.astype(BF16)
            ds[k * rows : (k + 1) * rows, part] = (p * (d[k] - mean)).astype(BF16)
    dq_t = dot(keys.T, ds[...]) * scale
    for h in range(heads):
        dq_ref[0, :, h * HEAD_DIM : (h + 1) * HEAD_DIM] = dq_t[:, h * rows : (h + 1) * rows].T.astype(BF16)
    grads = [dot(ds[...], qs[...]) * scale, dot(ps[...], dos[...])]
    for which in range(2):
        start = 0
        for ref in dself_refs:
            ref[which] = grads[which][start : start + ref.shape[1]].astype(BF16)
            start += ref.shape[1]
        for k in range(depth):
            grad = grads[which][(k + 1) * rows : (k + 2) * rows].astype(BF16)
            danc_ref[:, k, which] = grad.reshape(hubs, pieces, HEAD_DIM)


def attend(place, parents, queries, output_gradient, owns, foreign, query_grad):
    _, rows, width = queries.shape
    hubs, depth, _, pieces, kv_width = foreign.shape
    groups = kv_width // HEAD_DIM
    heads = width // groups // HEAD_DIM
    span = (depth + 1) * rows
    q_spec = pl.BlockSpec((1, rows, heads * HEAD_DIM), lambda g, place, _: (place[1], 0, g))
    own_specs = [pl.BlockSpec((2, 1, x.shape[2], HEAD_DIM), lambda g, place, _: (0, place[1], 0, g)) for x in owns]
    dself_specs = [pl.BlockSpec((2, x.shape[2], HEAD_DIM), lambda g, place, _: (0, 0, g)) for x in owns]
    anc_spec = pl.BlockSpec((hubs, depth, 2, pieces, HEAD_DIM), lambda g, place, _: (0, 0, 0, 0, g))
    first = query_grad is None
    return pl.pallas_call(
        functools.partial(attend_kernel, len(owns), first),
        grid_spec=pltpu.PrefetchScalarGridSpec(
            num_scalar_prefetch=2,
            grid=(groups,),
            in_specs=[q_spec, q_spec, *own_specs, anc_spec] + ([] if first else [pl.BlockSpec(memory_space=pl.ANY)]),
            out_specs=[q_spec, *dself_specs, anc_spec],
            scratch_shapes=[
                pltpu.VMEM((heads * rows, HEAD_DIM), BF16),
                pltpu.VMEM((heads * rows, HEAD_DIM), BF16),
                pltpu.VMEM((span, heads * rows), BF16),
                pltpu.VMEM((span, heads * rows), BF16),
            ],
        ),
        out_shape=[
            jax.ShapeDtypeStruct(queries.shape, BF16),
            *[jax.ShapeDtypeStruct((2, x.shape[2], kv_width), BF16) for x in owns],
            jax.ShapeDtypeStruct(foreign.shape, BF16),
        ],
        input_output_aliases={} if first else {5 + len(owns): 0},
        compiler_params=pltpu.CompilerParams(vmem_limit_bytes=56 * 1024 * 1024),
        cost_estimate=pl.CostEstimate(
            flops=10 * groups * heads * span * rows * HEAD_DIM,
            bytes_accessed=6 * rows * width,
            transcendentals=groups * heads * span * rows,
        ),
    )(place, parents, queries, output_gradient, *owns, foreign, *([] if first else [query_grad]))


def pack_kernel(place, keys_ref, values_ref, send_ref, keep_ref, give_ref):
    heads, width = send_ref.shape[0] // (keys_ref.shape[1] // 8), keep_ref.shape[3]
    leaves = send_ref.shape[0] // heads
    for kv, ref in enumerate((keys_ref, values_ref)):
        for h in range(heads):
            for j in range(0, leaves, 2):
                tiles = [ref[t, 8 * j : 8 * j + 16, h * width : (h + 1) * width] for t in range(2)]
                send_ref[h * leaves + j, kv] = jnp.concatenate([x[:8] for x in tiles], 0)
                send_ref[h * leaves + j + 1, kv] = jnp.concatenate([x[8:] for x in tiles], 0)
        keep_ref[kv] = ref[:, :, pl.ds(pl.multiple_of(place[3] * width, width), width)]
        give_ref[kv] = ref[:, :, pl.ds(pl.multiple_of((1 - place[3]) * width, width), width)]


def finish_kernel(place, got_ref, near_ref, near_got_ref, far_ref, far_got_ref, keys_ref, values_ref):
    width = near_ref.shape[2]
    leaves = near_ref.shape[1] // 8
    upper = place[1] == 1
    for kv, out_ref in enumerate((keys_ref, values_ref)):
        for own in range(2):
            h = place[3] if own else 1 - place[3]
            refs = (near_ref, far_ref) if own else (near_got_ref, far_got_ref)
            lanes = pl.ds(pl.multiple_of(h * width, width), width)
            for j in range(0, leaves, 2):
                rows = slice(8 * j, 8 * j + 16)
                a, b = got_ref[h * leaves + j, kv], got_ref[h * leaves + j + 1, kv]
                near = jnp.concatenate([a[:8], b[:8]], 0).astype(F32) + refs[0][kv, rows].astype(F32)
                far = jnp.concatenate([a[8:], b[8:]], 0).astype(F32) + refs[1][kv, rows].astype(F32)
                out_ref[0, rows, lanes] = jnp.where(upper, far, near).astype(BF16)
                out_ref[1, rows, lanes] = jnp.where(upper, near, far).astype(BF16)


def each_need(place, parents, half, depth, which, act):
    base = (place[0] // half) * half
    t = place[1 + which]

    def leaf(d, _):
        block = 2 * (base + d) + t
        for k in range(depth):
            block = jnp.where(block >= 0, parents[jnp.maximum(block, 0)], -1)
            p = block // 2
            act(d, k, block >= 0, (p >= base) & (p < base + half), p % half, t)
        return 0

    lax.fori_loop(0, half, leaf, 0)


def pick_near_kernel(place, parents, own_ref, out_ref):
    half, depth = out_ref.shape[:2]

    def act(d, slot, valid, here, p, t):
        out_ref[d, slot] = own_ref[p, :, t]

    each_need(place, parents, half, depth, 0, act)


def pick_far_kernel(place, parents, own_ref, cross_ref, out_ref):
    half, depth = out_ref.shape[:2]

    def act(d, slot, valid, here, p, t):
        @pl.when(here | ~valid)
        def _():
            out_ref[d, slot] = own_ref[p, :, t]

        @pl.when(valid & ~here)
        def _():
            out_ref[d, slot] = cross_ref[p]

    each_need(place, parents, half, depth, 1, act)


def collect_near_kernel(place, parents, in_ref, own_ref):
    half, depth = in_ref.shape[:2]
    own_ref[...] = jnp.zeros_like(own_ref)

    def act(d, slot, valid, here, p, t):
        @pl.when(valid)
        def _():
            own_ref[p] += in_ref[d, slot].astype(F32)

    each_need(place, parents, half, depth, 0, act)


def collect_far_kernel(place, parents, in_ref, own_ref, cross_ref, sums):
    half, depth = in_ref.shape[:2]
    sums[...] = jnp.zeros_like(sums)

    def act(d, slot, valid, here, p, t):
        @pl.when(valid)
        def _():
            sums[jnp.where(here, 0, half) + p] += in_ref[d, slot].astype(F32)

    each_need(place, parents, half, depth, 1, act)
    own_ref[...] = sums[:half].astype(BF16)
    cross_ref[...] = sums[half:].astype(BF16)


def body(queries, keys, values, output_gradient, parents):
    leaf_count = lax.axis_size("leaf")
    head_count = lax.axis_size("head")
    half = leaf_count // 2
    depth = leaf_count // 4 - 2
    leaf_rank = lax.axis_index("leaf")
    head_rank = lax.axis_index("head")
    upper = leaf_rank >= half
    near = jnp.where(upper, 1, 0)
    token = head_rank * keys.shape[1] if head_count == 2 else 0
    place = jnp.stack([leaf_rank, near, 1 - near, head_rank]).astype(jnp.int32)
    near_place = jnp.stack([leaf_rank, near, token]).astype(jnp.int32)
    far_place = jnp.stack([leaf_rank, 1 - near, token]).astype(jnp.int32)
    sides = [[half * i + j for j in range(half)] for i in range(2)]
    both = [[leaf_count * h + j for h in range(head_count) for j in side] for side in sides]
    swap = [(i, (i + half) % leaf_count) for i in range(leaf_count)]
    trees, part_rows, kv_all = keys.shape
    kv_width = kv_all // head_count
    rows = part_rows * head_count
    pieces = rows // half
    merged = head_count == 2 and part_rows == 8 * half and half % 2 == 0

    def exchange(x):
        return lax.all_to_all(x, "leaf", 0, 0, tiled=True, axis_index_groups=sides)

    def exchange_both(x):
        return lax.all_to_all(x, ("head", "leaf"), 0, 0, tiled=True, axis_index_groups=both)

    def to_other_head(x):
        return lax.ppermute(x, "head", [(0, 1), (1, 0)])

    all_parents = lax.all_gather(parents, "leaf", axis=0, tiled=True)

    if merged:
        send, keep, give = pl.pallas_call(
            pack_kernel,
            in_specs=[SMEM, VMEM, VMEM],
            out_specs=[VMEM, VMEM, VMEM],
            out_shape=[
                jax.ShapeDtypeStruct((2 * half, 2, 16, kv_width), BF16),
                *[jax.ShapeDtypeStruct((2, trees, part_rows, kv_width), BF16)] * 2,
            ],
            compiler_params=PARAMS,
        )(place, keys, values)
        arrived, theirs, all_parents = lax.optimization_barrier(
            (exchange_both(send), to_other_head(give), all_parents)
        )
        arrived = arrived.reshape(2, half, 2, trees, 8, kv_width).transpose(1, 2, 3, 0, 4, 5)
        hub_own = arrived.reshape(half, 2, trees, pieces, kv_width)
        owns = [keep, theirs]
    else:
        pair = jnp.stack([keys, values]).reshape(2, trees, part_rows, head_count, kv_width)
        pair = jnp.moveaxis(pair, 3, 0)
        if head_count > 1:
            pair = lax.all_to_all(pair, "head", 0, 0, tiled=True)
        mine = pair.transpose(1, 2, 0, 3, 4).reshape(2, trees, rows, kv_width)
        hub_own = exchange(mine.reshape(2, trees, half, pieces, kv_width).transpose(2, 0, 1, 3, 4))
        owns = [mine]

    hub_cross = lax.ppermute(jnp.where(upper, hub_own[:, :, 1], hub_own[:, :, 0]), "leaf", swap)
    picked_shape = jax.ShapeDtypeStruct((half, depth, 2, pieces, kv_width), BF16)
    picked_near = pl.pallas_call(
        pick_near_kernel,
        in_specs=[SMEM, SMEM, VMEM],
        out_specs=VMEM,
        out_shape=picked_shape,
        compiler_params=PARAMS,
    )(place, all_parents, hub_own)
    foreign_near = exchange(picked_near)
    picked_far = pl.pallas_call(
        pick_far_kernel,
        in_specs=[SMEM, SMEM, VMEM, VMEM],
        out_specs=VMEM,
        out_shape=picked_shape,
        compiler_params=PARAMS,
    )(place, all_parents, hub_own, hub_cross)
    foreign_far = exchange(picked_far)

    def gather_rows(x):
        if pieces % 16 == 0:
            return x
        return x.transpose(1, 2, 0, 3, 4).reshape(1, depth, 2, rows, kv_width)

    def spread_rows(x):
        if pieces % 16 == 0:
            return x
        return x.reshape(depth, 2, half, pieces, kv_width).transpose(2, 0, 1, 3, 4)

    query_grad, *self_near, grad_near = attend(
        near_place, all_parents, queries, output_gradient, owns, gather_rows(foreign_near), None
    )
    query_grad, *self_far, grad_far = attend(
        far_place, all_parents, queries, output_gradient, owns, gather_rows(foreign_far), query_grad
    )
    back_near, grad_far = lax.optimization_barrier((exchange(spread_rows(grad_near)), grad_far))
    back_far = exchange(spread_rows(grad_far))

    sum_shape = (half, 2, pieces, kv_width)
    far_sum, cross_sum = pl.pallas_call(
        collect_far_kernel,
        in_specs=[SMEM, SMEM, VMEM],
        out_specs=[VMEM, VMEM],
        out_shape=[jax.ShapeDtypeStruct(sum_shape, BF16)] * 2,
        scratch_shapes=[pltpu.VMEM((2 * half,) + sum_shape[1:], F32)],
        compiler_params=PARAMS,
    )(place, all_parents, back_far)
    near_sum = pl.pallas_call(
        collect_near_kernel,
        in_specs=[SMEM, SMEM, VMEM],
        out_specs=VMEM,
        out_shape=jax.ShapeDtypeStruct(sum_shape, F32),
        compiler_params=PARAMS,
    )(place, all_parents, back_near)
    crossed = lax.ppermute(cross_sum, "leaf", swap)
    near_sum = (near_sum + crossed.astype(F32)).astype(BF16)
    hub_sum = jnp.stack([near_sum, far_sum], 1)
    if merged:
        hub_sum = hub_sum.reshape(half, 2, 2, 2, 8, kv_width).transpose(3, 0, 2, 1, 4, 5)
        returned = exchange_both(hub_sum.reshape(2 * half, 2, 16, kv_width))
        near_got, far_got = to_other_head(self_near[1]), to_other_head(self_far[1])
        key_gradient, value_gradient = pl.pallas_call(
            finish_kernel,
            in_specs=[SMEM] + [VMEM] * 5,
            out_specs=[VMEM, VMEM],
            out_shape=[jax.ShapeDtypeStruct(keys.shape, BF16)] * 2,
            compiler_params=PARAMS,
        )(place, returned, self_near[0], near_got, self_far[0], far_got)
        return query_grad, key_gradient, value_gradient
    self_sum = jnp.stack([self_near[0], self_far[0]])
    returned = exchange(hub_sum).transpose(1, 2, 0, 3, 4).reshape(2, 2, rows, kv_width)
    total = (returned.astype(F32) + self_sum.astype(F32)).astype(BF16)
    total = jnp.moveaxis(total.reshape(2, 2, head_count, part_rows, kv_width), 2, 0)
    if head_count > 1:
        total = lax.all_to_all(total, "head", 0, 0, tiled=True)
    total = total.transpose(2, 1, 3, 0, 4).reshape(2, 2, part_rows, kv_all)
    total = jnp.where(upper, total[:, ::-1], total)
    return query_grad, total[0], total[1]


def solution(mesh):
    in_specs = (
        P("leaf", None, "head"),
        P("leaf", "head", None),
        P("leaf", "head", None),
        P("leaf", None, "head"),
        P("leaf"),
    )
    out_specs = (P("leaf", None, "head"), P("leaf", "head", None), P("leaf", "head", None))
    return jax.shard_map(body, mesh=mesh, in_specs=in_specs, out_specs=out_specs, check_vma=False)
```

```python
import functools
import math

import jax
import jax.numpy as jnp
from jax import lax
from jax.experimental import pallas as pl
from jax.experimental.pallas import tpu as pltpu
from jax.sharding import PartitionSpec as P

HEAD_DIM = 128

NT = (((1,), (1,)), ((), ()))
NN = (((1,), (0,)), ((), ()))
F32 = jnp.float32
BF16 = jnp.bfloat16
VMEM = pl.BlockSpec(memory_space=pltpu.VMEM)
SMEM = pl.BlockSpec(memory_space=pltpu.SMEM)
PARAMS = pltpu.CompilerParams(vmem_limit_bytes=40 * 1024 * 1024)


def dot(a, b, dims=NN):
    return lax.dot_general(a, b, dims, preferred_element_type=F32)


def attend_kernel(parts, first, place, parents, q_ref, do_ref, *refs):
    own_refs, anc_ref = refs[:parts], refs[parts]
    refs = refs[parts + (1 if first else 2) :]
    dq_ref, dself_refs, danc_ref = refs[0], refs[1 : 1 + parts], refs[1 + parts]
    hubs, depth, _, pieces, _ = anc_ref.shape
    rows = q_ref.shape[1]
    heads = q_ref.shape[2] // HEAD_DIM
    scale = HEAD_DIM ** (-0.5)
    c = scale * math.log2(math.e)
    block = 2 * place[0] + place[1]
    valid = []
    for _ in range(depth):
        block = jnp.where(block >= 0, parents[jnp.maximum(block, 0)], -1)
        valid.append(block >= 0)

    def seen(which):
        tiles = [anc_ref[:, k, which].reshape(rows, HEAD_DIM) for k in range(depth)]
        return jnp.concatenate([ref[which, 0] for ref in own_refs] + tiles, 0)

    keys, values = seen(0), seen(1)
    keys_t = keys.T
    token = lax.rem(lax.broadcasted_iota(jnp.int32, (rows, rows), 0) + place[2], rows)
    hidden = token > lax.broadcasted_iota(jnp.int32, (rows, rows), 1)

    def products(h):
        q, do = (
            jnp.concatenate([ref[0, :, i * HEAD_DIM : (i + 1) * HEAD_DIM] for i in range(h, h + 2)], 0)
            for ref in (q_ref, do_ref)
        )
        return h, q, do, dot(keys, q, NT), dot(values, do, NT)

    def soften(scores, slopes):
        s = [scores[k * rows : (k + 1) * rows] for k in range(depth + 1)]
        d = [slopes[k * rows : (k + 1) * rows] for k in range(depth + 1)]
        s[0] = jnp.where(hidden, -1e30, s[0])
        peak = jnp.max(s[0], 0, keepdims=True)
        for k in range(depth):
            peak = jnp.maximum(peak, jnp.where(valid[k], jnp.max(s[k + 1], 0, keepdims=True), -1e30))
        peak = peak * c
        e = [jnp.exp2(s[0] * c - peak)]
        for k in range(depth):
            e.append(jnp.exp2(s[k + 1] * c - jnp.where(valid[k], peak, 1e30)))
        total = functools.reduce(jnp.add, [jnp.sum(x, 0, keepdims=True) for x in e])
        weighted = functools.reduce(jnp.add, [jnp.sum(x * y, 0, keepdims=True) for x, y in zip(e, d)])
        inverse = 1.0 / total
        mean = weighted * inverse
        p = [x * inverse for x in e]
        ds = [(x * (y - mean)).astype(BF16) for x, y in zip(p, d)]
        return jnp.concatenate([x.astype(BF16) for x in p], 0), jnp.concatenate(ds, 0)

    def gradients(h, q, do, ps, ds):
        dq_t = dot(keys_t, ds) * scale
        for i in range(2):
            lanes = slice((h + i) * HEAD_DIM, (h + i + 1) * HEAD_DIM)
            dq_ref[0, :, lanes] = dq_t[:, i * rows : (i + 1) * rows].T.astype(BF16)
        return dot(ds, q), dot(ps, do)

    grads = None
    stage = products(0)
    ready = None
    for h in range(0, heads + 2, 2):
        following = products(h + 2) if h + 2 < heads else None
        soft = None
        if stage is not None:
            i, q, do, scores, slopes = stage
            halves = [soften(scores[:, x * rows : (x + 1) * rows], slopes[:, x * rows : (x + 1) * rows]) for x in range(2)]
            soft = (i, q, do, jnp.concatenate([x[0] for x in halves], 1), jnp.concatenate([x[1] for x in halves], 1))
        if ready is not None:
            more = gradients(*ready)
            grads = more if grads is None else (grads[0] + more[0], grads[1] + more[1])
        stage, ready = following, soft
    grads = (grads[0] * scale, grads[1])
    for which in range(2):
        start = 0
        for ref in dself_refs:
            ref[which] = grads[which][start : start + ref.shape[1]].astype(BF16)
            start += ref.shape[1]
        for k in range(depth):
            grad = grads[which][(k + 1) * rows : (k + 2) * rows].astype(BF16)
            danc_ref[:, k, which] = grad.reshape(hubs, pieces, HEAD_DIM)


def attend(place, parents, queries, output_gradient, owns, foreign, query_grad):
    _, rows, width = queries.shape
    hubs, depth, _, pieces, kv_width = foreign.shape
    groups = kv_width // HEAD_DIM
    heads = width // groups // HEAD_DIM
    span = (depth + 1) * rows
    q_spec = pl.BlockSpec((1, rows, heads * HEAD_DIM), lambda g, place, _: (place[1], 0, g))
    own_specs = [pl.BlockSpec((2, 1, x.shape[2], HEAD_DIM), lambda g, place, _: (0, place[1], 0, g)) for x in owns]
    dself_specs = [pl.BlockSpec((2, x.shape[2], HEAD_DIM), lambda g, place, _: (0, 0, g)) for x in owns]
    anc_spec = pl.BlockSpec((hubs, depth, 2, pieces, HEAD_DIM), lambda g, place, _: (0, 0, 0, 0, g))
    first = query_grad is None
    return pl.pallas_call(
        functools.partial(attend_kernel, len(owns), first),
        grid_spec=pltpu.PrefetchScalarGridSpec(
            num_scalar_prefetch=2,
            grid=(groups,),
            in_specs=[q_spec, q_spec, *own_specs, anc_spec] + ([] if first else [pl.BlockSpec(memory_space=pl.ANY)]),
            out_specs=[q_spec, *dself_specs, anc_spec],
        ),
        out_shape=[
            jax.ShapeDtypeStruct(queries.shape, BF16),
            *[jax.ShapeDtypeStruct((2, x.shape[2], kv_width), BF16) for x in owns],
            jax.ShapeDtypeStruct(foreign.shape, BF16),
        ],
        input_output_aliases={} if first else {5 + len(owns): 0},
        compiler_params=pltpu.CompilerParams(vmem_limit_bytes=56 * 1024 * 1024),
        cost_estimate=pl.CostEstimate(
            flops=10 * groups * heads * span * rows * HEAD_DIM,
            bytes_accessed=6 * rows * width,
            transcendentals=groups * heads * span * rows,
        ),
    )(place, parents, queries, output_gradient, *owns, foreign, *([] if first else [query_grad]))


def pack_kernel(place, keys_ref, values_ref, send_ref, keep_ref, give_ref):
    heads, width = send_ref.shape[0] // (keys_ref.shape[1] // 8), keep_ref.shape[3]
    leaves = send_ref.shape[0] // heads
    for kv, ref in enumerate((keys_ref, values_ref)):
        for h in range(heads):
            for j in range(0, leaves, 2):
                tiles = [ref[t, 8 * j : 8 * j + 16, h * width : (h + 1) * width] for t in range(2)]
                send_ref[h * leaves + j, kv] = jnp.concatenate([x[:8] for x in tiles], 0)
                send_ref[h * leaves + j + 1, kv] = jnp.concatenate([x[8:] for x in tiles], 0)
        keep_ref[kv] = ref[:, :, pl.ds(pl.multiple_of(place[3] * width, width), width)]
        give_ref[kv] = ref[:, :, pl.ds(pl.multiple_of((1 - place[3]) * width, width), width)]


def finish_kernel(place, got_ref, near_ref, near_got_ref, far_ref, far_got_ref, keys_ref, values_ref):
    width = near_ref.shape[2]
    leaves = near_ref.shape[1] // 8
    upper = place[1] == 1
    for kv, out_ref in enumerate((keys_ref, values_ref)):
        for own in range(2):
            h = place[3] if own else 1 - place[3]
            refs = (near_ref, far_ref) if own else (near_got_ref, far_got_ref)
            lanes = pl.ds(pl.multiple_of(h * width, width), width)
            for j in range(0, leaves, 2):
                rows = slice(8 * j, 8 * j + 16)
                a, b = got_ref[h * leaves + j, kv], got_ref[h * leaves + j + 1, kv]
                near = jnp.concatenate([a[:8], b[:8]], 0).astype(F32) + refs[0][kv, rows].astype(F32)
                far = jnp.concatenate([a[8:], b[8:]], 0).astype(F32) + refs[1][kv, rows].astype(F32)
                out_ref[0, rows, lanes] = jnp.where(upper, far, near).astype(BF16)
                out_ref[1, rows, lanes] = jnp.where(upper, near, far).astype(BF16)


def each_need(place, parents, half, depth, which, act):
    base = (place[0] // half) * half
    t = place[1 + which]

    def leaf(d, _):
        block = 2 * (base + d) + t
        for k in range(depth):
            block = jnp.where(block >= 0, parents[jnp.maximum(block, 0)], -1)
            p = block // 2
            act(d, k, block >= 0, (p >= base) & (p < base + half), p % half, t)
        return 0

    lax.fori_loop(0, half, leaf, 0)


def pick_near_kernel(place, parents, own_ref, out_ref):
    half, depth = out_ref.shape[:2]

    def act(d, slot, valid, here, p, t):
        out_ref[d, slot] = own_ref[p, :, t]

    each_need(place, parents, half, depth, 0, act)


def pick_far_kernel(place, parents, own_ref, cross_ref, out_ref):
    half, depth = out_ref.shape[:2]

    def act(d, slot, valid, here, p, t):
        @pl.when(here | ~valid)
        def _():
            out_ref[d, slot] = own_ref[p, :, t]

        @pl.when(valid & ~here)
        def _():
            out_ref[d, slot] = cross_ref[p]

    each_need(place, parents, half, depth, 1, act)


def collect_near_kernel(place, parents, in_ref, own_ref):
    half, depth = in_ref.shape[:2]
    own_ref[...] = jnp.zeros_like(own_ref)

    def act(d, slot, valid, here, p, t):
        @pl.when(valid)
        def _():
            own_ref[p] += in_ref[d, slot].astype(F32)

    each_need(place, parents, half, depth, 0, act)


def collect_far_kernel(place, parents, in_ref, own_ref, cross_ref, sums):
    half, depth = in_ref.shape[:2]
    sums[...] = jnp.zeros_like(sums)

    def act(d, slot, valid, here, p, t):
        @pl.when(valid)
        def _():
            sums[jnp.where(here, 0, half) + p] += in_ref[d, slot].astype(F32)

    each_need(place, parents, half, depth, 1, act)
    own_ref[...] = sums[:half].astype(BF16)
    cross_ref[...] = sums[half:].astype(BF16)


def body(queries, keys, values, output_gradient, parents):
    leaf_count = lax.axis_size("leaf")
    head_count = lax.axis_size("head")
    half = leaf_count // 2
    depth = leaf_count // 4 - 2
    leaf_rank = lax.axis_index("leaf")
    head_rank = lax.axis_index("head")
    upper = leaf_rank >= half
    near = jnp.where(upper, 1, 0)
    token = head_rank * keys.shape[1] if head_count == 2 else 0
    place = jnp.stack([leaf_rank, near, 1 - near, head_rank]).astype(jnp.int32)
    near_place = jnp.stack([leaf_rank, near, token]).astype(jnp.int32)
    far_place = jnp.stack([leaf_rank, 1 - near, token]).astype(jnp.int32)
    sides = [[half * i + j for j in range(half)] for i in range(2)]
    both = [[leaf_count * h + j for h in range(head_count) for j in side] for side in sides]
    swap = [(i, (i + half) % leaf_count) for i in range(leaf_count)]
    trees, part_rows, kv_all = keys.shape
    kv_width = kv_all // head_count
    rows = part_rows * head_count
    pieces = rows // half
    merged = head_count == 2 and part_rows == 8 * half and half % 2 == 0

    def exchange(x):
        return lax.all_to_all(x, "leaf", 0, 0, tiled=True, axis_index_groups=sides)

    def exchange_both(x):
        return lax.all_to_all(x, ("head", "leaf"), 0, 0, tiled=True, axis_index_groups=both)

    def to_other_head(x):
        return lax.ppermute(x, "head", [(0, 1), (1, 0)])

    all_parents = lax.all_gather(parents, "leaf", axis=0, tiled=True)

    if merged:
        send, keep, give = pl.pallas_call(
            pack_kernel,
            in_specs=[SMEM, VMEM, VMEM],
            out_specs=[VMEM, VMEM, VMEM],
            out_shape=[
                jax.ShapeDtypeStruct((2 * half, 2, 16, kv_width), BF16),
                *[jax.ShapeDtypeStruct((2, trees, part_rows, kv_width), BF16)] * 2,
            ],
            compiler_params=PARAMS,
        )(place, keys, values)
        arrived, all_parents, give = lax.optimization_barrier((exchange_both(send), all_parents, give))
        arrived = arrived.reshape(2, half, 2, trees, 8, kv_width).transpose(1, 2, 3, 0, 4, 5)
        hub_own = arrived.reshape(half, 2, trees, pieces, kv_width)
    else:
        pair = jnp.stack([keys, values]).reshape(2, trees, part_rows, head_count, kv_width)
        pair = jnp.moveaxis(pair, 3, 0)
        if head_count > 1:
            pair = lax.all_to_all(pair, "head", 0, 0, tiled=True)
        mine = pair.transpose(1, 2, 0, 3, 4).reshape(2, trees, rows, kv_width)
        hub_own = exchange(mine.reshape(2, trees, half, pieces, kv_width).transpose(2, 0, 1, 3, 4))
        owns = [mine]

    picked_shape = jax.ShapeDtypeStruct((half, depth, 2, pieces, kv_width), BF16)
    picked_near = pl.pallas_call(
        pick_near_kernel,
        in_specs=[SMEM, SMEM, VMEM],
        out_specs=VMEM,
        out_shape=picked_shape,
        compiler_params=PARAMS,
    )(place, all_parents, hub_own)
    foreign_near = exchange(picked_near)
    crossing = jnp.where(upper, hub_own[:, :, 1], hub_own[:, :, 0])
    if merged:
        foreign_near, theirs, crossing = lax.optimization_barrier((foreign_near, to_other_head(give), crossing))
        owns = [keep, theirs]
    else:
        foreign_near, crossing = lax.optimization_barrier((foreign_near, crossing))
    hub_cross = lax.ppermute(crossing, "leaf", swap)
    picked_far = pl.pallas_call(
        pick_far_kernel,
        in_specs=[SMEM, SMEM, VMEM, VMEM],
        out_specs=VMEM,
        out_shape=picked_shape,
        compiler_params=PARAMS,
    )(place, all_parents, hub_own, hub_cross)
    foreign_far = exchange(picked_far)

    def gather_rows(x):
        if pieces % 16 == 0:
            return x
        return x.transpose(1, 2, 0, 3, 4).reshape(1, depth, 2, rows, kv_width)

    def spread_rows(x):
        if pieces % 16 == 0:
            return x
        return x.reshape(depth, 2, half, pieces, kv_width).transpose(2, 0, 1, 3, 4)

    query_grad, *self_near, grad_near = attend(
        near_place, all_parents, queries, output_gradient, owns, gather_rows(foreign_near), None
    )
    query_grad, *self_far, grad_far = attend(
        far_place, all_parents, queries, output_gradient, owns, gather_rows(foreign_far), query_grad
    )
    if merged:
        back_near, near_got, grad_far, give = lax.optimization_barrier(
            (exchange(grad_near), to_other_head(self_near[1]), grad_far, self_far[1])
        )
        back_far, far_got = lax.optimization_barrier((exchange(grad_far), to_other_head(give)))
    else:
        back_near, grad_far = lax.optimization_barrier((exchange(spread_rows(grad_near)), grad_far))
        back_far = exchange(spread_rows(grad_far))

    sum_shape = (half, 2, pieces, kv_width)
    far_sum, cross_sum = pl.pallas_call(
        collect_far_kernel,
        in_specs=[SMEM, SMEM, VMEM],
        out_specs=[VMEM, VMEM],
        out_shape=[jax.ShapeDtypeStruct(sum_shape, BF16)] * 2,
        scratch_shapes=[pltpu.VMEM((2 * half,) + sum_shape[1:], F32)],
        compiler_params=PARAMS,
    )(place, all_parents, back_far)
    near_sum = pl.pallas_call(
        collect_near_kernel,
        in_specs=[SMEM, SMEM, VMEM],
        out_specs=VMEM,
        out_shape=jax.ShapeDtypeStruct(sum_shape, F32),
        compiler_params=PARAMS,
    )(place, all_parents, back_near)
    crossed = lax.ppermute(cross_sum, "leaf", swap)
    near_sum = (near_sum + crossed.astype(F32)).astype(BF16)
    hub_sum = jnp.stack([near_sum, far_sum], 1)
    if merged:
        hub_sum = hub_sum.reshape(half, 2, 2, 2, 8, kv_width).transpose(3, 0, 2, 1, 4, 5)
        returned = exchange_both(hub_sum.reshape(2 * half, 2, 16, kv_width))
        key_gradient, value_gradient = pl.pallas_call(
            finish_kernel,
            in_specs=[SMEM] + [VMEM] * 5,
            out_specs=[VMEM, VMEM],
            out_shape=[jax.ShapeDtypeStruct(keys.shape, BF16)] * 2,
            compiler_params=PARAMS,
        )(place, returned, self_near[0], near_got, self_far[0], far_got)
        return query_grad, key_gradient, value_gradient
    self_sum = jnp.stack([self_near[0], self_far[0]])
    returned = exchange(hub_sum).transpose(1, 2, 0, 3, 4).reshape(2, 2, rows, kv_width)
    total = (returned.astype(F32) + self_sum.astype(F32)).astype(BF16)
    total = jnp.moveaxis(total.reshape(2, 2, head_count, part_rows, kv_width), 2, 0)
    if head_count > 1:
        total = lax.all_to_all(total, "head", 0, 0, tiled=True)
    total = total.transpose(2, 1, 3, 0, 4).reshape(2, 2, part_rows, kv_all)
    total = jnp.where(upper, total[:, ::-1], total)
    return query_grad, total[0], total[1]


def solution(mesh):
    in_specs = (
        P("leaf", None, "head"),
        P("leaf", "head", None),
        P("leaf", "head", None),
        P("leaf", None, "head"),
        P("leaf"),
    )
    out_specs = (P("leaf", None, "head"), P("leaf", "head", None), P("leaf", "head", None))
    return jax.shard_map(body, mesh=mesh, in_specs=in_specs, out_specs=out_specs, check_vma=False)
```

```python
import functools
import math

import jax
import jax.numpy as jnp
from jax import lax
from jax.experimental import pallas as pl
from jax.experimental.pallas import tpu as pltpu
from jax.sharding import PartitionSpec as P

HEAD_DIM = 128

NT = (((1,), (1,)), ((), ()))
NN = (((1,), (0,)), ((), ()))
F32 = jnp.float32
BF16 = jnp.bfloat16
SMEM = pl.BlockSpec(memory_space=pltpu.SMEM)
PARAMS = pltpu.CompilerParams(vmem_limit_bytes=40 * 1024 * 1024)


def dot(a, b, dims=NN):
    return lax.dot_general(a, b, dims, preferred_element_type=F32)


def attend_kernel(parts, place, parents, q_ref, do_ref, *refs):
    own_refs, anc_ref, dq_ref = refs[:parts], refs[parts], refs[parts + 1]
    dself_refs, danc_ref = refs[parts + 2 : 2 * parts + 2], refs[2 * parts + 2]
    hubs, depth, _, pieces, _ = anc_ref.shape
    rows = q_ref.shape[1]
    heads = q_ref.shape[2] // HEAD_DIM
    scale = HEAD_DIM ** (-0.5)
    c = scale * math.log2(math.e)
    block = 2 * place[0] + pl.program_id(0)
    valid = []
    for _ in range(depth):
        block = above(parents, block)
        valid.append(block >= 0)

    def seen(which):
        tiles = [anc_ref[:, k, which].reshape(rows, HEAD_DIM) for k in range(depth)]
        return jnp.concatenate([ref[which, 0] for ref in own_refs] + tiles, 0)

    keys, values = seen(0), seen(1)
    keys_t = keys.T
    token = lax.rem(lax.broadcasted_iota(jnp.int32, (rows, rows), 0) + place[2], rows)
    hidden = token > lax.broadcasted_iota(jnp.int32, (rows, rows), 1)

    def products(h):
        q, do = (
            jnp.concatenate([ref[0, :, i * HEAD_DIM : (i + 1) * HEAD_DIM] for i in range(h, h + 2)], 0)
            for ref in (q_ref, do_ref)
        )
        return h, q, do, dot(keys, q, NT), dot(values, do, NT)

    def soften(scores, slopes):
        s = [scores[k * rows : (k + 1) * rows] for k in range(depth + 1)]
        d = [slopes[k * rows : (k + 1) * rows] for k in range(depth + 1)]
        s[0] = jnp.where(hidden, -1e30, s[0])
        peak = jnp.max(s[0], 0, keepdims=True)
        for k in range(depth):
            peak = jnp.maximum(peak, jnp.where(valid[k], jnp.max(s[k + 1], 0, keepdims=True), -1e30))
        peak = peak * c
        e = [jnp.exp2(s[0] * c - peak)]
        for k in range(depth):
            e.append(jnp.exp2(s[k + 1] * c - jnp.where(valid[k], peak, 1e30)))
        total = functools.reduce(jnp.add, [jnp.sum(x, 0, keepdims=True) for x in e])
        weighted = functools.reduce(jnp.add, [jnp.sum(x * y, 0, keepdims=True) for x, y in zip(e, d)])
        inverse = 1.0 / total
        mean = weighted * inverse
        p = [x * inverse for x in e]
        ds = [(x * (y - mean)).astype(BF16) for x, y in zip(p, d)]
        return jnp.concatenate([x.astype(BF16) for x in p], 0), jnp.concatenate(ds, 0)

    def gradients(h, q, do, ps, ds):
        dq_t = dot(keys_t, ds) * scale
        for i in range(2):
            lanes = slice((h + i) * HEAD_DIM, (h + i + 1) * HEAD_DIM)
            dq_ref[0, :, lanes] = dq_t[:, i * rows : (i + 1) * rows].T.astype(BF16)
        return dot(ds, q), dot(ps, do)

    grads = None
    stage = products(0)
    ready = None
    for h in range(0, heads + 2, 2):
        following = products(h + 2) if h + 2 < heads else None
        soft = None
        if stage is not None:
            i, q, do, scores, slopes = stage
            halves = [soften(scores[:, x * rows : (x + 1) * rows], slopes[:, x * rows : (x + 1) * rows]) for x in range(2)]
            soft = (i, q, do, jnp.concatenate([x[0] for x in halves], 1), jnp.concatenate([x[1] for x in halves], 1))
        if ready is not None:
            more = gradients(*ready)
            grads = more if grads is None else (grads[0] + more[0], grads[1] + more[1])
        stage, ready = following, soft
    grads = (grads[0] * scale, grads[1])
    for which in range(2):
        start = 0
        for ref in dself_refs:
            ref[which, 0] = grads[which][start : start + ref.shape[2]].astype(BF16)
            start += ref.shape[2]
        for k in range(depth):
            grad = grads[which][(k + 1) * rows : (k + 2) * rows].astype(BF16)
            danc_ref[:, k, which] = grad.reshape(hubs, pieces, HEAD_DIM)


def attend(place, parents, queries, output_gradient, owns, foreign):
    trees, rows, width = queries.shape
    hubs, slots, _, pieces, kv_width = foreign.shape
    depth = slots // trees
    groups = kv_width // HEAD_DIM
    heads = width // groups // HEAD_DIM
    q_spec = pl.BlockSpec((1, rows, heads * HEAD_DIM), lambda t, g: (t, 0, g))
    own_specs = [pl.BlockSpec((2, 1, x.shape[2], HEAD_DIM), lambda t, g: (0, t, 0, g)) for x in owns]
    anc_spec = pl.BlockSpec((hubs, depth, 2, pieces, HEAD_DIM), lambda t, g: (0, t, 0, 0, g))
    return pl.pallas_call(
        functools.partial(attend_kernel, len(owns)),
        grid=(trees, groups),
        in_specs=[SMEM, SMEM, q_spec, q_spec, *own_specs, anc_spec],
        out_specs=[q_spec, *own_specs, anc_spec],
        out_shape=[jax.ShapeDtypeStruct(x.shape, BF16) for x in (queries, *owns, foreign)],
        compiler_params=pltpu.CompilerParams(vmem_limit_bytes=56 * 1024 * 1024),
        cost_estimate=pl.CostEstimate(
            flops=10 * trees * groups * heads * (depth + 1) * rows * rows * HEAD_DIM,
            bytes_accessed=12 * rows * width,
            transcendentals=trees * groups * heads * (depth + 1) * rows * rows,
        ),
    )(place, parents, queries, output_gradient, *owns, foreign)


def pack_kernel(place, parents, keys_ref, values_ref, send_ref, keep_ref, give_ref, table_ref):
    heads, width = send_ref.shape[0] // (keys_ref.shape[1] // 8), keep_ref.shape[3]
    leaves = send_ref.shape[0] // heads
    for kv, ref in enumerate((keys_ref, values_ref)):
        for h in range(heads):
            for j in range(0, leaves, 2):
                tiles = [ref[t, 8 * j : 8 * j + 16, h * width : (h + 1) * width] for t in range(2)]
                send_ref[h * leaves + j, kv] = jnp.concatenate([x[:8] for x in tiles], 0)
                send_ref[h * leaves + j + 1, kv] = jnp.concatenate([x[8:] for x in tiles], 0)
        keep_ref[kv] = ref[:, :, pl.ds(pl.multiple_of(place[1] * width, width), width)]
        give_ref[kv] = ref[:, :, pl.ds(pl.multiple_of((1 - place[1]) * width, width), width)]
    block = lax.broadcasted_iota(jnp.int32, table_ref.shape, 1)
    table = jnp.zeros(table_ref.shape, jnp.int32)
    for t in range(2):
        table = jnp.where(block == 2 * place[0] + t, parents[t], table)
    table_ref[...] = table


def above(parents, block):
    return jnp.where(block >= 0, parents[0, jnp.maximum(block, 0)], -1)


def far_slots(place, parents, half, depth, sending, slots):
    base = (place[0] // half) * half
    source = base if sending else half - base
    target = half - source
    t = jnp.where(source == 0, 0, 1)

    def clear(p, _):
        slots[p] = -1
        return 0

    def mark(d, _):
        block = 2 * (target + d) + t
        for _ in range(depth):
            block = above(parents, block)
            p = block // 2 - source

            @pl.when((block >= 0) & (p >= 0) & (p < half))
            def _():
                slots[p] = 0

        return 0

    def number(p, count):
        needed = slots[p] >= 0
        slots[p] = jnp.where(needed, count, -1)
        return count + needed.astype(jnp.int32)

    lax.fori_loop(0, half, clear, 0)
    lax.fori_loop(0, half, mark, 0)
    return lax.fori_loop(0, half, number, 0)


def each_need(place, parents, half, depth, act):
    base = (place[0] // half) * half

    def leaf(d, _):
        for t in range(2):
            block = 2 * (base + d) + t
            for k in range(depth):
                block = above(parents, block)
                p = block // 2
                act(d, t * depth + k, block >= 0, (p >= base) & (p < base + half), p % half, t)
        return 0

    lax.fori_loop(0, half, leaf, 0)


def cross_kernel(depth, place, parents, own_ref, cross_ref, count_ref, slots):
    half = own_ref.shape[0]
    other = far_slots(place, parents, half, depth, False, slots)
    mine = far_slots(place, parents, half, depth, True, slots)
    count_ref[0] = jnp.maximum(mine, other)
    t = place[0] // half

    def copy(p, _):
        @pl.when(slots[p] >= 0)
        def _():
            cross_ref[slots[p]] = own_ref[p, :, t]

        return 0

    lax.fori_loop(0, half, copy, 0)


def pick_kernel(depth, place, parents, own_ref, cross_ref, out_ref, slots):
    half = own_ref.shape[0]
    far_slots(place, parents, half, depth, False, slots)

    def act(d, slot, valid, here, p, t):
        @pl.when(here | ~valid)
        def _():
            out_ref[d, slot] = own_ref[p, :, t]

        @pl.when(valid & ~here)
        def _():
            out_ref[d, slot] = cross_ref[slots[p]]

    each_need(place, parents, half, depth, act)


def collect_kernel(depth, place, parents, in_ref, own_ref, cross_ref, sums, slots):
    half = own_ref.shape[0]
    far_slots(place, parents, half, depth, False, slots)
    own_ref[...] = jnp.zeros_like(own_ref)
    sums[...] = jnp.zeros_like(sums)

    def act(d, slot, valid, here, p, t):
        @pl.when(valid & here)
        def _():
            own_ref[p, :, t] += in_ref[d, slot].astype(F32)

        @pl.when(valid & ~here)
        def _():
            sums[slots[p]] += in_ref[d, slot].astype(F32)

    each_need(place, parents, half, depth, act)
    cross_ref[...] = sums[...].astype(BF16)


def merge_kernel(depth, spread, place, parents, own_ref, cross_ref, out_ref, slots):
    half = own_ref.shape[0]
    far_slots(place, parents, half, depth, True, slots)
    t = place[0] // half

    def add(p, _):
        needed = slots[p] >= 0
        far = cross_ref[jnp.maximum(slots[p], 0)].astype(F32)
        for kv in range(2):
            sums = [own_ref[p, kv, i] + jnp.where(needed & (i == t), far[kv], 0.0) for i in range(2)]
            if spread:
                for h in range(2):
                    tiles = [x[8 * h : 8 * h + 8] for x in sums]
                    out_ref[h * half + p, kv] = jnp.concatenate(tiles, 0).astype(BF16)
            else:
                for i in range(2):
                    out_ref[p, kv, i] = sums[i].astype(BF16)
        return 0

    lax.fori_loop(0, half, add, 0)


def finish_kernel(place, got_ref, own_ref, own_got_ref, keys_ref, values_ref):
    width = own_ref.shape[3]
    leaves = own_ref.shape[2] // 8
    for kv, out_ref in enumerate((keys_ref, values_ref)):
        for own in range(2):
            h = place[1] if own else 1 - place[1]
            ref = own_ref if own else own_got_ref
            lanes = pl.ds(pl.multiple_of(h * width, width), width)
            for j in range(0, leaves, 2):
                rows = slice(8 * j, 8 * j + 16)
                a, b = (got_ref[h * leaves + j + i, kv].astype(F32) for i in range(2))
                for t in range(2):
                    part = slice(8 * t, 8 * t + 8)
                    total = jnp.concatenate([a[part], b[part]], 0) + ref[kv, t, rows].astype(F32)
                    out_ref[t, rows, lanes] = total.astype(BF16)


def whole(shape):
    return pl.BlockSpec(shape, lambda i: (0,) * len(shape))


def simple(kernel, place, parents, arrays, outs, scratch=(), count=False):
    out_specs = [whole(x.shape) for x in outs] + ([SMEM] if count else [])
    outs = list(outs) + ([jax.ShapeDtypeStruct((1,), jnp.int32)] if count else [])
    return pl.pallas_call(
        kernel,
        grid=(1,),
        in_specs=[SMEM, SMEM] + [whole(x.shape) for x in arrays],
        out_specs=out_specs,
        out_shape=outs,
        scratch_shapes=list(scratch),
        compiler_params=PARAMS,
    )(place, parents, *arrays)


def body(queries, keys, values, output_gradient, parents):
    leaf_count = lax.axis_size("leaf")
    head_count = lax.axis_size("head")
    half = leaf_count // 2
    depth = leaf_count // 4 - 2
    leaf_rank = lax.axis_index("leaf")
    head_rank = lax.axis_index("head")
    token = head_rank * keys.shape[1] if head_count == 2 else 0
    place = jnp.stack([leaf_rank, head_rank, token]).astype(jnp.int32)
    sides = [[half * i + j for j in range(half)] for i in range(2)]
    both = [[leaf_count * h + j for h in range(head_count) for j in side] for side in sides]
    swap = [(i, (i + half) % leaf_count) for i in range(leaf_count)]
    trees, part_rows, kv_all = keys.shape
    kv_width = kv_all // head_count
    rows = part_rows * head_count
    pieces = rows // half
    merged = head_count == 2 and part_rows == 8 * half and half % 2 == 0

    def exchange(x):
        return lax.all_to_all(x, "leaf", 0, 0, tiled=True, axis_index_groups=sides)

    def exchange_both(x):
        return lax.all_to_all(x, ("head", "leaf"), 0, 0, tiled=True, axis_index_groups=both)

    def to_other_head(x):
        return lax.ppermute(x, "head", [(0, 1), (1, 0)])

    def like(*shape, dtype=BF16):
        return jax.ShapeDtypeStruct(shape, dtype)

    blocks = trees * leaf_count
    if merged:
        send, keep, give, table = simple(
            pack_kernel,
            place,
            parents,
            (keys, values),
            [
                like(2 * half, 2, 16, kv_width),
                like(2, trees, part_rows, kv_width),
                like(2, trees, part_rows, kv_width),
                like(1, blocks, dtype=jnp.int32),
            ],
        )
        arrived, all_parents, give = lax.optimization_barrier((exchange_both(send), lax.psum(table, "leaf"), give))
        arrived = arrived.reshape(2, half, 2, trees, 8, kv_width).transpose(1, 2, 3, 0, 4, 5)
        hub_own = arrived.reshape(half, 2, trees, pieces, kv_width)
    else:
        all_parents = lax.all_gather(parents, "leaf", axis=0, tiled=True).reshape(1, blocks)
        pair = jnp.stack([keys, values]).reshape(2, trees, part_rows, head_count, kv_width)
        pair = jnp.moveaxis(pair, 3, 0)
        if head_count > 1:
            pair = lax.all_to_all(pair, "head", 0, 0, tiled=True)
        mine = pair.transpose(1, 2, 0, 3, 4).reshape(2, trees, rows, kv_width)
        hub_own = exchange(mine.reshape(2, trees, half, pieces, kv_width).transpose(2, 0, 1, 3, 4))

    piece = (2, pieces, kv_width)
    slots = pltpu.SMEM((half,), jnp.int32)
    few = min(2, half)

    def cross(x, count):
        def short():
            return jnp.concatenate([lax.ppermute(x[:few], "leaf", swap), x[few:]])

        return lax.cond(count[0] <= few, short, lambda: lax.ppermute(x, "leaf", swap))

    crossing, count = simple(
        functools.partial(cross_kernel, depth),
        place,
        all_parents,
        (hub_own,),
        [like(half, *piece)],
        [slots],
        count=True,
    )
    hub_cross = cross(crossing, count)
    (picked,) = simple(
        functools.partial(pick_kernel, depth),
        place,
        all_parents,
        (hub_own, hub_cross),
        [like(half, trees * depth, *piece)],
        [slots],
    )
    if merged:
        foreign, theirs = lax.optimization_barrier((exchange(picked), to_other_head(give)))
        owns = [keep, theirs]
    else:
        foreign = exchange(picked)
        owns = [mine]
    if pieces % 16:
        foreign = foreign.transpose(1, 2, 0, 3, 4).reshape(1, trees * depth, 2, rows, kv_width)

    query_grad, *self_grads, foreign_grad = attend(place, all_parents, queries, output_gradient, owns, foreign)
    if pieces % 16:
        foreign_grad = foreign_grad.reshape(trees * depth, 2, half, pieces, kv_width).transpose(2, 0, 1, 3, 4)
    back = exchange(foreign_grad)
    if merged:
        back, own_got = lax.optimization_barrier((back, to_other_head(self_grads[1])))

    own_sum, cross_sum = simple(
        functools.partial(collect_kernel, depth),
        place,
        all_parents,
        (back,),
        [like(half, 2, trees, pieces, kv_width, dtype=F32), like(half, *piece)],
        [pltpu.VMEM((half,) + piece, F32), slots],
    )
    (hub_sum,) = simple(
        functools.partial(merge_kernel, depth, merged),
        place,
        all_parents,
        (own_sum, cross(cross_sum, count)),
        [like(2 * half, 2, 16, kv_width) if merged else like(half, 2, trees, pieces, kv_width)],
        [slots],
    )
    if merged:
        returned = exchange_both(hub_sum)
        return query_grad, *pl.pallas_call(
            finish_kernel,
            grid=(1,),
            in_specs=[SMEM] + [whole(x.shape) for x in (returned, self_grads[0], own_got)],
            out_specs=[whole(keys.shape)] * 2,
            out_shape=[like(*keys.shape)] * 2,
            compiler_params=PARAMS,
        )(place, returned, self_grads[0], own_got)
    returned = exchange(hub_sum).transpose(1, 2, 0, 3, 4).reshape(2, trees, rows, kv_width)
    total = (returned.astype(F32) + self_grads[0].astype(F32)).astype(BF16)
    total = jnp.moveaxis(total.reshape(2, trees, head_count, part_rows, kv_width), 2, 0)
    if head_count > 1:
        total = lax.all_to_all(total, "head", 0, 0, tiled=True)
    total = total.transpose(1, 2, 3, 0, 4).reshape(2, trees, part_rows, kv_all)
    return query_grad, total[0], total[1]


def solution(mesh):
    in_specs = (
        P("leaf", None, "head"),
        P("leaf", "head", None),
        P("leaf", "head", None),
        P("leaf", None, "head"),
        P("leaf"),
    )
    out_specs = (P("leaf", None, "head"), P("leaf", "head", None), P("leaf", "head", None))
    return jax.shard_map(body, mesh=mesh, in_specs=in_specs, out_specs=out_specs, check_vma=False)
```

```python
import functools
import math

import jax
import jax.numpy as jnp
from jax import lax
from jax.experimental import pallas as pl
from jax.experimental.pallas import tpu as pltpu
from jax.sharding import PartitionSpec as P

HEAD_DIM = 128

NT = (((1,), (1,)), ((), ()))
NN = (((1,), (0,)), ((), ()))
F32 = jnp.float32
BF16 = jnp.bfloat16
SMEM = pl.BlockSpec(memory_space=pltpu.SMEM)
PARAMS = pltpu.CompilerParams(vmem_limit_bytes=40 * 1024 * 1024)
WIDE = pltpu.CompilerParams(vmem_limit_bytes=60 * 1024 * 1024)


def dot(a, b, dims=NN):
    return lax.dot_general(a, b, dims, preferred_element_type=F32)


def attend_kernel(parts, place, parents, q_ref, do_ref, *refs):
    own_refs, anc_ref, dq_ref = refs[:parts], refs[parts], refs[parts + 1]
    dself_refs, danc_ref = refs[parts + 2 : 2 * parts + 2], refs[2 * parts + 2]
    hubs, depth, _, pieces, _ = anc_ref.shape
    rows = q_ref.shape[1]
    heads = q_ref.shape[2] // HEAD_DIM
    scale = HEAD_DIM ** (-0.5)
    c = scale * math.log2(math.e)
    block = 2 * place[0] + pl.program_id(0)
    valid = []
    for _ in range(depth):
        block = above(parents, block)
        valid.append(block >= 0)

    def seen(which):
        tiles = [anc_ref[:, k, which].reshape(rows, HEAD_DIM) for k in range(depth)]
        return jnp.concatenate([ref[which, 0] for ref in own_refs] + tiles, 0)

    keys, values = seen(0), seen(1)
    keys_t = keys.T
    token = lax.rem(lax.broadcasted_iota(jnp.int32, (rows, rows), 0) + place[2], rows)
    hidden = token > lax.broadcasted_iota(jnp.int32, (rows, rows), 1)

    def products(h):
        q, do = (
            jnp.concatenate([ref[0, :, i * HEAD_DIM : (i + 1) * HEAD_DIM] for i in range(h, h + 2)], 0)
            for ref in (q_ref, do_ref)
        )
        return h, q, do, dot(keys, q, NT), dot(values, do, NT)

    def soften(scores, slopes):
        s = [scores[k * rows : (k + 1) * rows] for k in range(depth + 1)]
        d = [slopes[k * rows : (k + 1) * rows] for k in range(depth + 1)]
        s[0] = jnp.where(hidden, -1e30, s[0])
        peak = jnp.max(s[0], 0, keepdims=True)
        for k in range(depth):
            peak = jnp.maximum(peak, jnp.where(valid[k], jnp.max(s[k + 1], 0, keepdims=True), -1e30))
        peak = peak * c
        e = [jnp.exp2(s[0] * c - peak)]
        for k in range(depth):
            e.append(jnp.exp2(s[k + 1] * c - jnp.where(valid[k], peak, 1e30)))
        total = functools.reduce(jnp.add, [jnp.sum(x, 0, keepdims=True) for x in e])
        weighted = functools.reduce(jnp.add, [jnp.sum(x * y, 0, keepdims=True) for x, y in zip(e, d)])
        inverse = 1.0 / total
        mean = weighted * inverse
        p = [x * inverse for x in e]
        ds = [(x * (y - mean)).astype(BF16) for x, y in zip(p, d)]
        return jnp.concatenate([x.astype(BF16) for x in p], 0), jnp.concatenate(ds, 0)

    def gradients(h, q, do, ps, ds):
        dq_t = dot(keys_t, ds) * scale
        for i in range(2):
            lanes = slice((h + i) * HEAD_DIM, (h + i + 1) * HEAD_DIM)
            dq_ref[0, :, lanes] = dq_t[:, i * rows : (i + 1) * rows].T.astype(BF16)
        return dot(ds, q), dot(ps, do)

    grads = None
    stage = products(0)
    ready = None
    for h in range(0, heads + 2, 2):
        following = products(h + 2) if h + 2 < heads else None
        soft = None
        if stage is not None:
            i, q, do, scores, slopes = stage
            halves = [soften(scores[:, x * rows : (x + 1) * rows], slopes[:, x * rows : (x + 1) * rows]) for x in range(2)]
            soft = (i, q, do, jnp.concatenate([x[0] for x in halves], 1), jnp.concatenate([x[1] for x in halves], 1))
        if ready is not None:
            more = gradients(*ready)
            grads = more if grads is None else (grads[0] + more[0], grads[1] + more[1])
        stage, ready = following, soft
    grads = (grads[0] * scale, grads[1])
    for which in range(2):
        start = 0
        for ref in dself_refs:
            ref[which, 0] = grads[which][start : start + ref.shape[2]].astype(BF16)
            start += ref.shape[2]
        for k in range(depth):
            grad = grads[which][(k + 1) * rows : (k + 2) * rows].astype(BF16)
            danc_ref[:, k, which] = grad.reshape(hubs, pieces, HEAD_DIM)


def attend(place, parents, queries, output_gradient, owns, foreign):
    trees, rows, width = queries.shape
    hubs, slots, _, pieces, kv_width = foreign.shape
    depth = slots // trees
    groups = kv_width // HEAD_DIM
    heads = width // groups // HEAD_DIM
    q_spec = pl.BlockSpec((1, rows, heads * HEAD_DIM), lambda t, g: (t, 0, g))
    own_specs = [pl.BlockSpec((2, 1, x.shape[2], HEAD_DIM), lambda t, g: (0, t, 0, g)) for x in owns]
    anc_spec = pl.BlockSpec((hubs, depth, 2, pieces, HEAD_DIM), lambda t, g: (0, t, 0, 0, g))
    return pl.pallas_call(
        functools.partial(attend_kernel, len(owns)),
        grid=(trees, groups),
        in_specs=[SMEM, SMEM, q_spec, q_spec, *own_specs, anc_spec],
        out_specs=[q_spec, *own_specs, anc_spec],
        out_shape=[jax.ShapeDtypeStruct(x.shape, BF16) for x in (queries, *owns, foreign)],
        compiler_params=pltpu.CompilerParams(vmem_limit_bytes=24 * 1024 * 1024),
        cost_estimate=pl.CostEstimate(
            flops=10 * trees * groups * heads * (depth + 1) * rows * rows * HEAD_DIM,
            bytes_accessed=12 * rows * width,
            transcendentals=trees * groups * heads * (depth + 1) * rows * rows,
        ),
    )(place, parents, queries, output_gradient, *owns, foreign)


def pack_kernel(place, parents, keys_ref, values_ref, send_ref, keep_ref, give_ref, table_ref):
    heads, width = send_ref.shape[0] // (keys_ref.shape[1] // 8), keep_ref.shape[3]
    leaves = send_ref.shape[0] // heads
    for kv, ref in enumerate((keys_ref, values_ref)):
        for h in range(heads):
            for j in range(0, leaves, 2):
                tiles = [ref[t, 8 * j : 8 * j + 16, h * width : (h + 1) * width] for t in range(2)]
                send_ref[h * leaves + j, kv] = jnp.concatenate([x[:8] for x in tiles], 0)
                send_ref[h * leaves + j + 1, kv] = jnp.concatenate([x[8:] for x in tiles], 0)
        keep_ref[kv] = ref[:, :, pl.ds(pl.multiple_of(place[1] * width, width), width)]
        give_ref[kv] = ref[:, :, pl.ds(pl.multiple_of((1 - place[1]) * width, width), width)]
    block = lax.broadcasted_iota(jnp.int32, table_ref.shape, 1)
    table = jnp.zeros(table_ref.shape, jnp.int32)
    for t in range(2):
        table = jnp.where(block == 2 * place[0] + t, parents[t], table)
    table_ref[...] = table


def above(parents, block):
    return jnp.where(block >= 0, parents[0, jnp.maximum(block, 0)], -1)


def far_slots(place, parents, half, depth, sending, slots, start):
    base = (place[0] // half) * half
    source = base if sending else half - base
    target = half - source
    t = jnp.where(source == 0, 0, 1)

    def clear(p, _):
        slots[start + p] = -1
        return 0

    def mark(d, _):
        block = 2 * (target + d) + t
        for _ in range(depth):
            block = above(parents, block)
            p = block // 2 - source

            @pl.when((block >= 0) & (p >= 0) & (p < half))
            def _():
                slots[start + p] = 0

        return 0

    def number(p, count):
        needed = slots[start + p] >= 0
        slots[start + p] = jnp.where(needed, count, -1)
        return count + needed.astype(jnp.int32)

    lax.fori_loop(0, half, clear, 0)
    lax.fori_loop(0, half, mark, 0)
    return lax.fori_loop(0, half, number, 0)


def each_need(place, parents, half, depth, act):
    base = (place[0] // half) * half

    def leaf(d, _):
        for t in range(2):
            block = 2 * (base + d) + t
            for k in range(depth):
                block = above(parents, block)
                p = block // 2
                act(d, t * depth + k, block >= 0, (p >= base) & (p < base + half), p % half, t)
        return 0

    lax.fori_loop(0, half, leaf, 0)


def cross_kernel(depth, place, parents, own_ref, cross_ref, slots):
    half = own_ref.shape[0]
    other = far_slots(place, parents, half, depth, False, slots, 0)
    mine = far_slots(place, parents, half, depth, True, slots, half)
    slots[2 * half] = jnp.maximum(mine, other)
    t = place[0] // half

    def copy(p, _):
        slot = slots[half + p]

        @pl.when(slot >= 0)
        def _():
            cross_ref[slot] = own_ref[p, :, t]

        return 0

    lax.fori_loop(0, half, copy, 0)


def pick_kernel(depth, place, parents, slots, own_ref, cross_ref, out_ref):
    half = own_ref.shape[0]

    def act(d, slot, valid, here, p, t):
        @pl.when(here | ~valid)
        def _():
            out_ref[d, slot] = own_ref[p, :, t]

        @pl.when(valid & ~here)
        def _():
            out_ref[d, slot] = cross_ref[slots[p]]

    each_need(place, parents, half, depth, act)


def collect_kernel(depth, place, parents, slots, in_ref, own_ref, cross_ref, sums):
    half = own_ref.shape[0]
    own_ref[...] = jnp.zeros_like(own_ref)
    sums[...] = jnp.zeros_like(sums)

    def act(d, slot, valid, here, p, t):
        @pl.when(valid & here)
        def _():
            own_ref[p, :, t] += in_ref[d, slot].astype(F32)

        @pl.when(valid & ~here)
        def _():
            sums[slots[p]] += in_ref[d, slot].astype(F32)

    each_need(place, parents, half, depth, act)
    cross_ref[...] = sums[...].astype(BF16)


def merge_kernel(spread, place, slots, own_ref, cross_ref, out_ref):
    half = own_ref.shape[0]
    t = place[0] // half

    def add(p, _):
        slot = slots[half + p]
        far = cross_ref[jnp.maximum(slot, 0)].astype(F32)
        for kv in range(2):
            sums = [own_ref[p, kv, i] + jnp.where((slot >= 0) & (i == t), far[kv], 0.0) for i in range(2)]
            if spread:
                for h in range(2):
                    tiles = [x[8 * h : 8 * h + 8] for x in sums]
                    out_ref[h * half + p, kv] = jnp.concatenate(tiles, 0).astype(BF16)
            else:
                for i in range(2):
                    out_ref[p, kv, i] = sums[i].astype(BF16)
        return 0

    lax.fori_loop(0, half, add, 0)


def finish_kernel(place, got_ref, own_ref, own_got_ref, keys_ref, values_ref):
    width = own_ref.shape[3]
    leaves = own_ref.shape[2] // 8
    for kv, out_ref in enumerate((keys_ref, values_ref)):
        for own in range(2):
            h = place[1] if own else 1 - place[1]
            ref = own_ref if own else own_got_ref
            lanes = pl.ds(pl.multiple_of(h * width, width), width)
            for j in range(0, leaves, 2):
                rows = slice(8 * j, 8 * j + 16)
                a, b = (got_ref[h * leaves + j + i, kv].astype(F32) for i in range(2))
                for t in range(2):
                    part = slice(8 * t, 8 * t + 8)
                    total = jnp.concatenate([a[part], b[part]], 0) + ref[kv, t, rows].astype(F32)
                    out_ref[t, rows, lanes] = total.astype(BF16)


def whole(shape):
    return pl.BlockSpec(shape, lambda i: (0,) * len(shape))


def simple(kernel, scalars, arrays, outs, scratch=(), slots=0, params=PARAMS):
    out_specs = [whole(x.shape) for x in outs] + ([SMEM] if slots else [])
    outs = list(outs) + ([jax.ShapeDtypeStruct((slots,), jnp.int32)] if slots else [])
    return pl.pallas_call(
        kernel,
        grid=(1,),
        in_specs=[SMEM] * len(scalars) + [whole(x.shape) for x in arrays],
        out_specs=out_specs,
        out_shape=outs,
        scratch_shapes=list(scratch),
        compiler_params=params,
    )(*scalars, *arrays)


def body(queries, keys, values, output_gradient, parents):
    leaf_count = lax.axis_size("leaf")
    head_count = lax.axis_size("head")
    half = leaf_count // 2
    depth = leaf_count // 4 - 2
    leaf_rank = lax.axis_index("leaf")
    head_rank = lax.axis_index("head")
    token = head_rank * keys.shape[1] if head_count == 2 else 0
    place = jnp.stack([leaf_rank, head_rank, token]).astype(jnp.int32)
    sides = [[half * i + j for j in range(half)] for i in range(2)]
    both = [[leaf_count * h + j for h in range(head_count) for j in side] for side in sides]
    swap = [(i, (i + half) % leaf_count) for i in range(leaf_count)]
    trees, part_rows, kv_all = keys.shape
    kv_width = kv_all // head_count
    rows = part_rows * head_count
    pieces = rows // half
    merged = head_count == 2 and part_rows == 8 * half and half % 2 == 0

    def exchange(x):
        return lax.all_to_all(x, "leaf", 0, 0, tiled=True, axis_index_groups=sides)

    def exchange_both(x):
        return lax.all_to_all(x, ("head", "leaf"), 0, 0, tiled=True, axis_index_groups=both)

    def to_other_head(x):
        return lax.ppermute(x, "head", [(0, 1), (1, 0)])

    def like(*shape, dtype=BF16):
        return jax.ShapeDtypeStruct(shape, dtype)

    blocks = trees * leaf_count
    if merged:
        send, keep, give, table = simple(
            pack_kernel,
            (place, parents),
            (keys, values),
            [
                like(2 * half, 2, 16, kv_width),
                like(2, trees, part_rows, kv_width),
                like(2, trees, part_rows, kv_width),
                like(1, blocks, dtype=jnp.int32),
            ],
            params=WIDE,
        )
        arrived, all_parents, theirs = lax.optimization_barrier(
            (exchange_both(send), lax.psum(table, "leaf"), to_other_head(give))
        )
        owns = [keep, theirs]
        arrived = arrived.reshape(2, half, 2, trees, 8, kv_width).transpose(1, 2, 3, 0, 4, 5)
        hub_own = arrived.reshape(half, 2, trees, pieces, kv_width)
    else:
        all_parents = lax.all_gather(parents, "leaf", axis=0, tiled=True).reshape(1, blocks)
        pair = jnp.stack([keys, values]).reshape(2, trees, part_rows, head_count, kv_width)
        pair = jnp.moveaxis(pair, 3, 0)
        if head_count > 1:
            pair = lax.all_to_all(pair, "head", 0, 0, tiled=True)
        mine = pair.transpose(1, 2, 0, 3, 4).reshape(2, trees, rows, kv_width)
        hub_own = exchange(mine.reshape(2, trees, half, pieces, kv_width).transpose(2, 0, 1, 3, 4))
        owns = [mine]

    piece = (2, pieces, kv_width)
    few = min(2, half)

    def cross(x):
        def short():
            return jnp.concatenate([lax.ppermute(x[:few], "leaf", swap), x[few:]])

        return lax.cond(slots[2 * half] <= few, short, lambda: lax.ppermute(x, "leaf", swap))

    crossing, slots = simple(
        functools.partial(cross_kernel, depth),
        (place, all_parents),
        (hub_own,),
        [like(half, *piece)],
        slots=2 * half + 1,
    )
    (picked,) = simple(
        functools.partial(pick_kernel, depth),
        (place, all_parents, slots),
        (hub_own, cross(crossing)),
        [like(half, trees * depth, *piece)],
    )
    foreign = exchange(picked)
    if pieces % 16:
        foreign = foreign.transpose(1, 2, 0, 3, 4).reshape(1, trees * depth, 2, rows, kv_width)

    query_grad, *self_grads, foreign_grad = attend(place, all_parents, queries, output_gradient, owns, foreign)
    if pieces % 16:
        foreign_grad = foreign_grad.reshape(trees * depth, 2, half, pieces, kv_width).transpose(2, 0, 1, 3, 4)
    back = exchange(foreign_grad)
    if merged:
        back, own_got = lax.optimization_barrier((back, to_other_head(self_grads[1])))

    own_sum, cross_sum = simple(
        functools.partial(collect_kernel, depth),
        (place, all_parents, slots),
        (back,),
        [like(half, 2, trees, pieces, kv_width, dtype=F32), like(half, *piece)],
        [pltpu.VMEM((half,) + piece, F32)],
    )
    (hub_sum,) = simple(
        functools.partial(merge_kernel, merged),
        (place, slots),
        (own_sum, cross(cross_sum)),
        [like(2 * half, 2, 16, kv_width) if merged else like(half, 2, trees, pieces, kv_width)],
    )
    if merged:
        returned = exchange_both(hub_sum)
        return query_grad, *simple(
            finish_kernel, (place,), (returned, self_grads[0], own_got), [like(*keys.shape)] * 2
        )
    returned = exchange(hub_sum).transpose(1, 2, 0, 3, 4).reshape(2, trees, rows, kv_width)
    total = (returned.astype(F32) + self_grads[0].astype(F32)).astype(BF16)
    total = jnp.moveaxis(total.reshape(2, trees, head_count, part_rows, kv_width), 2, 0)
    if head_count > 1:
        total = lax.all_to_all(total, "head", 0, 0, tiled=True)
    total = total.transpose(1, 2, 3, 0, 4).reshape(2, trees, part_rows, kv_all)
    return query_grad, total[0], total[1]


def solution(mesh):
    in_specs = (
        P("leaf", None, "head"),
        P("leaf", "head", None),
        P("leaf", "head", None),
        P("leaf", None, "head"),
        P("leaf"),
    )
    out_specs = (P("leaf", None, "head"), P("leaf", "head", None), P("leaf", "head", None))
    return jax.shard_map(body, mesh=mesh, in_specs=in_specs, out_specs=out_specs, check_vma=False)
```

```python
import functools
import math

import jax
import jax.numpy as jnp
from jax import lax
from jax.experimental import pallas as pl
from jax.experimental.pallas import tpu as pltpu
from jax.sharding import PartitionSpec as P

HEAD_DIM = 128

NT = (((1,), (1,)), ((), ()))
NN = (((1,), (0,)), ((), ()))
F32 = jnp.float32
BF16 = jnp.bfloat16
SMEM = pl.BlockSpec(memory_space=pltpu.SMEM)
PARAMS = pltpu.CompilerParams(vmem_limit_bytes=40 * 1024 * 1024)
WIDE = pltpu.CompilerParams(vmem_limit_bytes=60 * 1024 * 1024)


def dot(a, b, dims=NN):
    return lax.dot_general(a, b, dims, preferred_element_type=F32)


def attend_kernel(parts, place, parents, q_ref, do_ref, *refs):
    own_refs, anc_ref, dq_ref = refs[:parts], refs[parts], refs[parts + 1]
    dself_refs, danc_ref = refs[parts + 2 : 2 * parts + 2], refs[2 * parts + 2]
    hubs, depth, _, pieces, _ = anc_ref.shape
    rows = q_ref.shape[1]
    step_groups = anc_ref.shape[4] // HEAD_DIM
    heads = q_ref.shape[2] // HEAD_DIM // step_groups
    scale = HEAD_DIM ** (-0.5)
    c = scale * math.log2(math.e)
    block = 2 * place[0] + pl.program_id(0)
    valid = []
    for _ in range(depth):
        block = above(parents, block)
        valid.append(block >= 0)

    def lanes(group, count=1):
        return slice(group * HEAD_DIM, (group + count) * HEAD_DIM)

    def seen(which, group):
        tiles = [anc_ref[:, k, which, :, lanes(group)].reshape(rows, HEAD_DIM) for k in range(depth)]
        return jnp.concatenate([ref[which, 0, :, lanes(group)] for ref in own_refs] + tiles, 0)

    held = [(seen(0, group), seen(1, group)) for group in range(step_groups)]
    held = [(keys, values, keys.T) for keys, values in held]
    token = lax.rem(lax.broadcasted_iota(jnp.int32, (rows, rows), 0) + place[2], rows)
    hidden = token > lax.broadcasted_iota(jnp.int32, (rows, rows), 1)

    def products(group, h):
        q, do = (
            jnp.concatenate([ref[0, :, lanes(group * heads + i)] for i in range(h, h + 2)], 0)
            for ref in (q_ref, do_ref)
        )
        return group, h, q, do, dot(held[group][0], q, NT), dot(held[group][1], do, NT)

    def soften(scores, slopes):
        s = [scores[k * rows : (k + 1) * rows] for k in range(depth + 1)]
        d = [slopes[k * rows : (k + 1) * rows] for k in range(depth + 1)]
        s[0] = jnp.where(hidden, -1e30, s[0])
        peak = jnp.max(s[0], 0, keepdims=True)
        for k in range(depth):
            peak = jnp.maximum(peak, jnp.where(valid[k], jnp.max(s[k + 1], 0, keepdims=True), -1e30))
        peak = peak * c
        e = [jnp.exp2(s[0] * c - peak)]
        for k in range(depth):
            e.append(jnp.exp2(s[k + 1] * c - jnp.where(valid[k], peak, 1e30)))
        total = functools.reduce(jnp.add, [jnp.sum(x, 0, keepdims=True) for x in e])
        weighted = functools.reduce(jnp.add, [jnp.sum(x * y, 0, keepdims=True) for x, y in zip(e, d)])
        inverse = 1.0 / total
        mean = weighted * inverse
        p = [x * inverse for x in e]
        ds = [(x * (y - mean)).astype(BF16) for x, y in zip(p, d)]
        return jnp.concatenate([x.astype(BF16) for x in p], 0), jnp.concatenate(ds, 0)

    def gradients(group, h, q, do, ps, ds):
        dq_t = dot(held[group][2], ds) * scale
        for i in range(2):
            dq_ref[0, :, lanes(group * heads + h + i)] = dq_t[:, i * rows : (i + 1) * rows].T.astype(BF16)
        return dot(ds, q), dot(ps, do)

    def store(group, grads):
        for which in range(2):
            start = 0
            for ref in dself_refs:
                ref[which, 0, :, lanes(group)] = grads[which][start : start + ref.shape[2]].astype(BF16)
                start += ref.shape[2]
            for k in range(depth):
                grad = grads[which][(k + 1) * rows : (k + 2) * rows].astype(BF16)
                danc_ref[:, k, which, :, lanes(group)] = grad.reshape(hubs, pieces, HEAD_DIM)

    pairs = [(group, h) for group in range(step_groups) for h in range(0, heads, 2)]
    stage, ready, grads = products(*pairs[0]), None, None
    for i in range(len(pairs) + 1):
        following = products(*pairs[i + 1]) if i + 1 < len(pairs) else None
        soft = None
        if stage is not None:
            group, h, q, do, scores, slopes = stage
            halves = [soften(scores[:, x * rows : (x + 1) * rows], slopes[:, x * rows : (x + 1) * rows]) for x in range(2)]
            soft = (group, h, q, do, *[jnp.concatenate(x, 1) for x in zip(*halves)])
        if ready is not None:
            more = gradients(*ready)
            grads = more if grads is None else (grads[0] + more[0], grads[1] + more[1])
            if ready[1] == heads - 2:
                store(ready[0], (grads[0] * scale, grads[1]))
                grads = None
        stage, ready = following, soft


def attend(place, parents, queries, output_gradient, owns, foreign):
    trees, rows, width = queries.shape
    hubs, slots, _, pieces, kv_width = foreign.shape
    depth = slots // trees
    groups = kv_width // HEAD_DIM
    heads = width // groups // HEAD_DIM
    step = 2 - groups % 2
    lanes = step * HEAD_DIM
    q_spec = pl.BlockSpec((1, rows, heads * lanes), lambda t, g: (t, 0, g))
    own_specs = [pl.BlockSpec((2, 1, x.shape[2], lanes), lambda t, g: (0, t, 0, g)) for x in owns]
    anc_spec = pl.BlockSpec((hubs, depth, 2, pieces, lanes), lambda t, g: (0, t, 0, 0, g))
    return pl.pallas_call(
        functools.partial(attend_kernel, len(owns)),
        grid=(trees, groups // step),
        in_specs=[SMEM, SMEM, q_spec, q_spec, *own_specs, anc_spec],
        out_specs=[q_spec, *own_specs, anc_spec],
        out_shape=[jax.ShapeDtypeStruct(x.shape, BF16) for x in (queries, *owns, foreign)],
        compiler_params=pltpu.CompilerParams(vmem_limit_bytes=50 * 1024 * 1024),
        cost_estimate=pl.CostEstimate(
            flops=10 * trees * groups * heads * (depth + 1) * rows * rows * HEAD_DIM,
            bytes_accessed=12 * rows * width,
            transcendentals=trees * groups * heads * (depth + 1) * rows * rows,
        ),
    )(place, parents, queries, output_gradient, *owns, foreign)


def pack_kernel(place, keys_ref, values_ref, send_ref, keep_ref, give_ref):
    heads, width = send_ref.shape[0] // (keys_ref.shape[1] // 8), keep_ref.shape[3]
    leaves = send_ref.shape[0] // heads
    for kv, ref in enumerate((keys_ref, values_ref)):
        for h in range(heads):
            for j in range(0, leaves, 2):
                tiles = [ref[t, 8 * j : 8 * j + 16, h * width : (h + 1) * width] for t in range(2)]
                send_ref[h * leaves + j, kv] = jnp.concatenate([x[:8] for x in tiles], 0)
                send_ref[h * leaves + j + 1, kv] = jnp.concatenate([x[8:] for x in tiles], 0)
        keep_ref[kv] = ref[:, :, pl.ds(pl.multiple_of(place[1] * width, width), width)]
        give_ref[kv] = ref[:, :, pl.ds(pl.multiple_of((1 - place[1]) * width, width), width)]


def table_kernel(place, parents, partner_parents, table_ref):
    blocks = table_ref.shape[1]
    block = lax.broadcasted_iota(jnp.int32, table_ref.shape, 1)
    table = jnp.zeros(table_ref.shape, jnp.int32)
    for t in range(2):
        own = 2 * place[0] + t
        table = jnp.where(block == own, parents[t], table)
        table = jnp.where(block == lax.rem(own + blocks // 2, blocks), partner_parents[t], table)
    table_ref[...] = table


def above(parents, block):
    return jnp.where(block >= 0, parents[0, jnp.maximum(block, 0)], -1)


def far_slots(place, parents, half, depth, sending, slots, start):
    base = (place[0] // half) * half
    source = base if sending else half - base
    target = half - source
    t = jnp.where(source == 0, 0, 1)

    def clear(p, _):
        slots[start + p] = -1
        return 0

    def mark(d, _):
        block = 2 * (target + d) + t
        for _ in range(depth):
            block = above(parents, block)
            p = block // 2 - source

            @pl.when((block >= 0) & (p >= 0) & (p < half))
            def _():
                slots[start + p] = 0

        return 0

    def number(p, count):
        needed = slots[start + p] >= 0
        slots[start + p] = jnp.where(needed, count, -1)
        return count + needed.astype(jnp.int32)

    lax.fori_loop(0, half, clear, 0)
    lax.fori_loop(0, half, mark, 0)
    return lax.fori_loop(0, half, number, 0)


def each_need(place, parents, half, depth, act):
    base = (place[0] // half) * half

    def leaf(d, _):
        for t in range(2):
            block = 2 * (base + d) + t
            for k in range(depth):
                block = above(parents, block)
                p = block // 2
                act(d, t * depth + k, block >= 0, (p >= base) & (p < base + half), p % half, t)
        return 0

    lax.fori_loop(0, half, leaf, 0)


def cross_kernel(depth, place, parents, own_ref, cross_ref, slots, count):
    half = own_ref.shape[0]
    other = far_slots(place, parents, half, depth, False, slots, 0)
    mine = far_slots(place, parents, half, depth, True, slots, half)
    count[0] = jnp.maximum(mine, other)
    t = place[0] // half

    def copy(p, _):
        slot = slots[half + p]

        @pl.when(slot >= 0)
        def _():
            cross_ref[slot] = own_ref[p, :, t]

        return 0

    lax.fori_loop(0, half, copy, 0)


def pick_kernel(depth, place, parents, slots, own_ref, cross_ref, out_ref):
    half = own_ref.shape[0]

    def act(d, slot, valid, here, p, t):
        @pl.when(here | ~valid)
        def _():
            out_ref[d, slot] = own_ref[p, :, t]

        @pl.when(valid & ~here)
        def _():
            out_ref[d, slot] = cross_ref[slots[p]]

    each_need(place, parents, half, depth, act)


def collect_kernel(depth, place, parents, slots, in_ref, own_ref, cross_ref, sums):
    half = own_ref.shape[0]
    own_ref[...] = jnp.zeros_like(own_ref)
    sums[...] = jnp.zeros_like(sums)

    def act(d, slot, valid, here, p, t):
        @pl.when(valid & here)
        def _():
            own_ref[p, :, t] += in_ref[d, slot].astype(F32)

        @pl.when(valid & ~here)
        def _():
            sums[slots[p]] += in_ref[d, slot].astype(F32)

    each_need(place, parents, half, depth, act)
    cross_ref[...] = sums[...].astype(BF16)


def merge_kernel(spread, place, slots, own_ref, cross_ref, out_ref):
    half = own_ref.shape[0]
    t = place[0] // half

    def add(p, _):
        slot = slots[half + p]
        far = cross_ref[jnp.maximum(slot, 0)].astype(F32)
        for kv in range(2):
            sums = [own_ref[p, kv, i] + jnp.where((slot >= 0) & (i == t), far[kv], 0.0) for i in range(2)]
            if spread:
                for h in range(2):
                    tiles = [x[8 * h : 8 * h + 8] for x in sums]
                    out_ref[h * half + p, kv] = jnp.concatenate(tiles, 0).astype(BF16)
            else:
                for i in range(2):
                    out_ref[p, kv, i] = sums[i].astype(BF16)
        return 0

    lax.fori_loop(0, half, add, 0)


def finish_kernel(place, got_ref, own_ref, own_got_ref, keys_ref, values_ref):
    width = own_ref.shape[3]
    leaves = own_ref.shape[2] // 8
    for kv, out_ref in enumerate((keys_ref, values_ref)):
        for own in range(2):
            h = place[1] if own else 1 - place[1]
            ref = own_ref if own else own_got_ref
            lanes = pl.ds(pl.multiple_of(h * width, width), width)
            for j in range(0, leaves, 2):
                rows = slice(8 * j, 8 * j + 16)
                a, b = (got_ref[h * leaves + j + i, kv].astype(F32) for i in range(2))
                for t in range(2):
                    part = slice(8 * t, 8 * t + 8)
                    total = jnp.concatenate([a[part], b[part]], 0) + ref[kv, t, rows].astype(F32)
                    out_ref[t, rows, lanes] = total.astype(BF16)


def whole(shape):
    return pl.BlockSpec(shape, lambda i: (0,) * len(shape))


def simple(kernel, scalars, arrays, outs, scratch=(), slots=(), params=PARAMS):
    out_specs = [whole(x.shape) for x in outs] + [SMEM] * len(slots)
    outs = list(outs) + [jax.ShapeDtypeStruct((x,), jnp.int32) for x in slots]
    return pl.pallas_call(
        kernel,
        grid=(1,),
        in_specs=[SMEM] * len(scalars) + [whole(x.shape) for x in arrays],
        out_specs=out_specs,
        out_shape=outs,
        scratch_shapes=list(scratch),
        compiler_params=params,
    )(*scalars, *arrays)


def body(queries, keys, values, output_gradient, parents):
    leaf_count = lax.axis_size("leaf")
    head_count = lax.axis_size("head")
    half = leaf_count // 2
    depth = leaf_count // 4 - 2
    leaf_rank = lax.axis_index("leaf")
    head_rank = lax.axis_index("head")
    token = head_rank * keys.shape[1] if head_count == 2 else 0
    place = jnp.stack([leaf_rank, head_rank, token]).astype(jnp.int32)
    sides = [[half * i + j for j in range(half)] for i in range(2)]
    both = [[leaf_count * h + j for h in range(head_count) for j in side] for side in sides]
    swap = [(i, (i + half) % leaf_count) for i in range(leaf_count)]
    trees, part_rows, kv_all = keys.shape
    kv_width = kv_all // head_count
    rows = part_rows * head_count
    pieces = rows // half
    merged = head_count == 2 and part_rows == 8 * half and half % 2 == 0

    def exchange(x):
        return lax.all_to_all(x, "leaf", 0, 0, tiled=True, axis_index_groups=sides)

    def exchange_both(x):
        return lax.all_to_all(x, ("head", "leaf"), 0, 0, tiled=True, axis_index_groups=both)

    def gather_parents(x):
        return lax.psum(x, "leaf", axis_index_groups=sides)

    def to_other_head(x):
        return lax.ppermute(x, "head", [(0, 1), (1, 0)])

    def like(*shape, dtype=BF16):
        return jax.ShapeDtypeStruct(shape, dtype)

    (table,) = simple(
        table_kernel,
        (place, parents, lax.ppermute(parents, "leaf", swap)),
        (),
        [like(1, trees * leaf_count, dtype=jnp.int32)],
    )
    if merged:
        send, keep, give = simple(
            pack_kernel,
            (place,),
            (keys, values),
            [
                like(2 * half, 2, 16, kv_width),
                like(2, trees, part_rows, kv_width),
                like(2, trees, part_rows, kv_width),
            ],
            params=WIDE,
        )
        send, give, table = lax.optimization_barrier((send, give, table))
        arrived, all_parents, theirs = lax.optimization_barrier(
            (exchange_both(send), gather_parents(table), to_other_head(give))
        )
        owns = [keep, theirs]
        arrived = arrived.reshape(2, half, 2, trees, 8, kv_width).transpose(1, 2, 3, 0, 4, 5)
        hub_own = arrived.reshape(half, 2, trees, pieces, kv_width)
    else:
        all_parents = gather_parents(table)
        pair = jnp.stack([keys, values]).reshape(2, trees, part_rows, head_count, kv_width)
        pair = jnp.moveaxis(pair, 3, 0)
        if head_count > 1:
            pair = lax.all_to_all(pair, "head", 0, 0, tiled=True)
        mine = pair.transpose(1, 2, 0, 3, 4).reshape(2, trees, rows, kv_width)
        hub_own = exchange(mine.reshape(2, trees, half, pieces, kv_width).transpose(2, 0, 1, 3, 4))
        owns = [mine]

    piece = (2, pieces, kv_width)
    few = min(2, half)

    def cross(x):
        def short():
            return jnp.concatenate([lax.ppermute(x[:few], "leaf", swap), x[few:]])

        return lax.cond(count[0] <= few, short, lambda: lax.ppermute(x, "leaf", swap))

    crossing, slots, count = simple(
        functools.partial(cross_kernel, depth),
        (place, all_parents),
        (hub_own,),
        [like(half, *piece)],
        slots=(2 * half, 1),
    )
    (picked,) = simple(
        functools.partial(pick_kernel, depth),
        (place, all_parents, slots),
        (hub_own, cross(crossing)),
        [like(half, trees * depth, *piece)],
    )
    foreign = exchange(picked)
    if pieces % 16:
        foreign = foreign.transpose(1, 2, 0, 3, 4).reshape(1, trees * depth, 2, rows, kv_width)

    query_grad, *self_grads, foreign_grad = attend(place, all_parents, queries, output_gradient, owns, foreign)
    if pieces % 16:
        foreign_grad = foreign_grad.reshape(trees * depth, 2, half, pieces, kv_width).transpose(2, 0, 1, 3, 4)
    back = exchange(foreign_grad)
    if merged:
        back, own_got = lax.optimization_barrier((back, to_other_head(self_grads[1])))

    own_sum, cross_sum = simple(
        functools.partial(collect_kernel, depth),
        (place, all_parents, slots),
        (back,),
        [like(half, 2, trees, pieces, kv_width, dtype=F32), like(half, *piece)],
        [pltpu.VMEM((half,) + piece, F32)],
    )
    (hub_sum,) = simple(
        functools.partial(merge_kernel, merged),
        (place, slots),
        (own_sum, cross(cross_sum)),
        [like(2 * half, 2, 16, kv_width) if merged else like(half, 2, trees, pieces, kv_width)],
    )
    if merged:
        returned = exchange_both(hub_sum)
        return query_grad, *simple(
            finish_kernel, (place,), (returned, self_grads[0], own_got), [like(*keys.shape)] * 2
        )
    returned = exchange(hub_sum).transpose(1, 2, 0, 3, 4).reshape(2, trees, rows, kv_width)
    total = (returned.astype(F32) + self_grads[0].astype(F32)).astype(BF16)
    total = jnp.moveaxis(total.reshape(2, trees, head_count, part_rows, kv_width), 2, 0)
    if head_count > 1:
        total = lax.all_to_all(total, "head", 0, 0, tiled=True)
    total = total.transpose(1, 2, 3, 0, 4).reshape(2, trees, part_rows, kv_all)
    return query_grad, total[0], total[1]


def solution(mesh):
    in_specs = (
        P("leaf", None, "head"),
        P("leaf", "head", None),
        P("leaf", "head", None),
        P("leaf", None, "head"),
        P("leaf"),
    )
    out_specs = (P("leaf", None, "head"), P("leaf", "head", None), P("leaf", "head", None))
    return jax.shard_map(body, mesh=mesh, in_specs=in_specs, out_specs=out_specs, check_vma=False)
```

```python
import functools
import math

import jax
import jax.numpy as jnp
from jax import lax
from jax.experimental import pallas as pl
from jax.experimental.pallas import tpu as pltpu
from jax.sharding import PartitionSpec as P

HEAD_DIM = 128

NT = (((1,), (1,)), ((), ()))
NN = (((1,), (0,)), ((), ()))
F32 = jnp.float32
BF16 = jnp.bfloat16
SMEM = pl.BlockSpec(memory_space=pltpu.SMEM)
PARAMS = pltpu.CompilerParams(vmem_limit_bytes=40 * 1024 * 1024)
WIDE = pltpu.CompilerParams(vmem_limit_bytes=60 * 1024 * 1024)


def dot(a, b, dims=NN):
    return lax.dot_general(a, b, dims, preferred_element_type=F32)


def attend_kernel(parts, parents, q_ref, do_ref, *refs):
    own_refs, anc_ref, dq_ref = refs[:parts], refs[parts], refs[parts + 1]
    dself_refs, danc_ref = refs[parts + 2 : 2 * parts + 2], refs[2 * parts + 2]
    hubs, depth, _, pieces, _ = anc_ref.shape
    rows = q_ref.shape[1]
    step_groups = anc_ref.shape[4] // HEAD_DIM
    heads = q_ref.shape[2] // HEAD_DIM // step_groups
    scale = HEAD_DIM ** (-0.5)
    c = scale * math.log2(math.e)
    block = 2 * leaf_rank() + pl.program_id(0)
    valid = []
    for _ in range(depth):
        block = above(parents, block)
        valid.append(block >= 0)

    def lanes(group, count=1):
        return slice(group * HEAD_DIM, (group + count) * HEAD_DIM)

    def seen(which, group):
        tiles = [anc_ref[:, k, which, :, lanes(group)].reshape(rows, HEAD_DIM) for k in range(depth)]
        return jnp.concatenate([ref[which, 0, :, lanes(group)] for ref in own_refs] + tiles, 0)

    held = [(seen(0, group), seen(1, group)) for group in range(step_groups)]
    held = [(keys, values, keys.T) for keys, values in held]
    first_token = lax.axis_index("head") * own_refs[0].shape[2] if parts == 2 else 0
    token = lax.rem(lax.broadcasted_iota(jnp.int32, (rows, rows), 0) + first_token, rows)
    hidden = token > lax.broadcasted_iota(jnp.int32, (rows, rows), 1)

    def products(group, h):
        q, do = (
            jnp.concatenate([ref[0, :, lanes(group * heads + i)] for i in range(h, h + 2)], 0)
            for ref in (q_ref, do_ref)
        )
        return group, h, q, do, dot(held[group][0], q, NT), dot(held[group][1], do, NT)

    def soften(scores, slopes):
        s = [scores[k * rows : (k + 1) * rows] for k in range(depth + 1)]
        d = [slopes[k * rows : (k + 1) * rows] for k in range(depth + 1)]
        s[0] = jnp.where(hidden, -1e30, s[0])
        peak = jnp.max(s[0], 0, keepdims=True)
        for k in range(depth):
            peak = jnp.maximum(peak, jnp.where(valid[k], jnp.max(s[k + 1], 0, keepdims=True), -1e30))
        peak = peak * c
        e = [jnp.exp2(s[0] * c - peak)]
        for k in range(depth):
            e.append(jnp.exp2(s[k + 1] * c - jnp.where(valid[k], peak, 1e30)))
        total = functools.reduce(jnp.add, [jnp.sum(x, 0, keepdims=True) for x in e])
        weighted = functools.reduce(jnp.add, [jnp.sum(x * y, 0, keepdims=True) for x, y in zip(e, d)])
        inverse = 1.0 / total
        mean = weighted * inverse
        p = [x * inverse for x in e]
        ds = [(x * (y - mean)).astype(BF16) for x, y in zip(p, d)]
        return jnp.concatenate([x.astype(BF16) for x in p], 0), jnp.concatenate(ds, 0)

    def gradients(group, h, q, do, ps, ds):
        dq_t = dot(held[group][2], ds) * scale
        for i in range(2):
            dq_ref[0, :, lanes(group * heads + h + i)] = dq_t[:, i * rows : (i + 1) * rows].T.astype(BF16)
        return dot(ds, q), dot(ps, do)

    def store(group, grads):
        for which in range(2):
            start = 0
            for ref in dself_refs:
                ref[which, 0, :, lanes(group)] = grads[which][start : start + ref.shape[2]].astype(BF16)
                start += ref.shape[2]
            for k in range(depth):
                grad = grads[which][(k + 1) * rows : (k + 2) * rows].astype(BF16)
                danc_ref[:, k, which, :, lanes(group)] = grad.reshape(hubs, pieces, HEAD_DIM)

    pairs = [(group, h) for group in range(step_groups) for h in range(0, heads, 2)]
    stage, ready, grads = products(*pairs[0]), None, None
    for i in range(len(pairs) + 1):
        following = products(*pairs[i + 1]) if i + 1 < len(pairs) else None
        soft = None
        if stage is not None:
            group, h, q, do, scores, slopes = stage
            halves = [soften(scores[:, x * rows : (x + 1) * rows], slopes[:, x * rows : (x + 1) * rows]) for x in range(2)]
            soft = (group, h, q, do, *[jnp.concatenate(x, 1) for x in zip(*halves)])
        if ready is not None:
            more = gradients(*ready)
            grads = more if grads is None else (grads[0] + more[0], grads[1] + more[1])
            if ready[1] == heads - 2:
                store(ready[0], (grads[0] * scale, grads[1]))
                grads = None
        stage, ready = following, soft


def attend(parents, queries, output_gradient, owns, foreign):
    trees, rows, width = queries.shape
    hubs, slots, _, pieces, kv_width = foreign.shape
    depth = slots // trees
    groups = kv_width // HEAD_DIM
    heads = width // groups // HEAD_DIM
    step = 2 - groups % 2
    lanes = step * HEAD_DIM
    q_spec = pl.BlockSpec((1, rows, heads * lanes), lambda t, g: (t, 0, g))
    own_specs = [pl.BlockSpec((2, 1, x.shape[2], lanes), lambda t, g: (0, t, 0, g)) for x in owns]
    anc_spec = pl.BlockSpec((hubs, depth, 2, pieces, lanes), lambda t, g: (0, t, 0, 0, g))
    return pl.pallas_call(
        functools.partial(attend_kernel, len(owns)),
        grid=(trees, groups // step),
        in_specs=[SMEM, q_spec, q_spec, *own_specs, anc_spec],
        out_specs=[q_spec, *own_specs, anc_spec],
        out_shape=[jax.ShapeDtypeStruct(x.shape, BF16) for x in (queries, *owns, foreign)],
        compiler_params=pltpu.CompilerParams(vmem_limit_bytes=50 * 1024 * 1024),
        cost_estimate=pl.CostEstimate(
            flops=10 * trees * groups * heads * (depth + 1) * rows * rows * HEAD_DIM,
            bytes_accessed=12 * rows * width,
            transcendentals=trees * groups * heads * (depth + 1) * rows * rows,
        ),
    )(parents, queries, output_gradient, *owns, foreign)


def pack_kernel(parents, keys_ref, values_ref, send_ref, keep_ref, give_ref, table_ref):
    heads, width = send_ref.shape[0] // (keys_ref.shape[1] // 8), keep_ref.shape[3]
    leaves = send_ref.shape[0] // heads
    for kv, ref in enumerate((keys_ref, values_ref)):
        for h in range(heads):
            for j in range(0, leaves, 2):
                tiles = [ref[t, 8 * j : 8 * j + 16, h * width : (h + 1) * width] for t in range(2)]
                send_ref[h * leaves + j, kv] = jnp.concatenate([x[:8] for x in tiles], 0)
                send_ref[h * leaves + j + 1, kv] = jnp.concatenate([x[8:] for x in tiles], 0)
        keep_ref[kv] = ref[:, :, pl.ds(pl.multiple_of(lax.axis_index("head") * width, width), width)]
        give_ref[kv] = ref[:, :, pl.ds(pl.multiple_of((1 - lax.axis_index("head")) * width, width), width)]
    block = lax.broadcasted_iota(jnp.int32, table_ref.shape, 1)
    table = jnp.zeros(table_ref.shape, jnp.int32)
    for t in range(2):
        table = jnp.where(block == 2 * leaf_rank() + t, parents[t], table)
    table_ref[...] = table


def leaf_rank():
    return lax.axis_index("leaf")


def above(parents, block):
    return jnp.where(block >= 0, parents[0, jnp.maximum(block, 0)], -1)


def far_slots(parents, half, depth, sending, slots, start):
    base = (leaf_rank() // half) * half
    source = base if sending else half - base
    target = half - source
    t = jnp.where(source == 0, 0, 1)

    def clear(p, _):
        slots[start + p] = -1
        return 0

    def mark(d, _):
        block = 2 * (target + d) + t
        for _ in range(depth):
            block = above(parents, block)
            p = block // 2 - source

            @pl.when((block >= 0) & (p >= 0) & (p < half))
            def _():
                slots[start + p] = 0

        return 0

    def number(p, count):
        needed = slots[start + p] >= 0
        slots[start + p] = jnp.where(needed, count, -1)
        return count + needed.astype(jnp.int32)

    lax.fori_loop(0, half, clear, 0)
    lax.fori_loop(0, half, mark, 0)
    return lax.fori_loop(0, half, number, 0)


def each_need(parents, half, depth, act):
    base = (leaf_rank() // half) * half

    def leaf(d, _):
        for t in range(2):
            block = 2 * (base + d) + t
            for k in range(depth):
                block = above(parents, block)
                p = block // 2
                act(d, t * depth + k, block >= 0, (p >= base) & (p < base + half), p % half, t)
        return 0

    lax.fori_loop(0, half, leaf, 0)


def cross_kernel(depth, parents, own_ref, cross_ref, slots, count):
    half = own_ref.shape[0]
    other = far_slots(parents, half, depth, False, slots, 0)
    mine = far_slots(parents, half, depth, True, slots, half)
    count[0] = jnp.maximum(mine, other)
    t = leaf_rank() // half

    def copy(p, _):
        slot = slots[half + p]

        @pl.when(slot >= 0)
        def _():
            cross_ref[slot] = own_ref[p, :, t]

        return 0

    lax.fori_loop(0, half, copy, 0)


def pick_kernel(depth, parents, slots, own_ref, cross_ref, out_ref):
    half = own_ref.shape[0]

    def act(d, slot, valid, here, p, t):
        @pl.when(here | ~valid)
        def _():
            out_ref[d, slot] = own_ref[p, :, t]

        @pl.when(valid & ~here)
        def _():
            out_ref[d, slot] = cross_ref[slots[p]]

    each_need(parents, half, depth, act)


def collect_kernel(depth, parents, slots, in_ref, own_ref, cross_ref, sums):
    half = own_ref.shape[0]
    own_ref[...] = jnp.zeros_like(own_ref)
    sums[...] = jnp.zeros_like(sums)

    def act(d, slot, valid, here, p, t):
        @pl.when(valid & here)
        def _():
            own_ref[p, :, t] += in_ref[d, slot].astype(F32)

        @pl.when(valid & ~here)
        def _():
            sums[slots[p]] += in_ref[d, slot].astype(F32)

    each_need(parents, half, depth, act)
    cross_ref[...] = sums[...].astype(BF16)


def merge_kernel(spread, slots, own_ref, cross_ref, out_ref):
    half = own_ref.shape[0]
    t = leaf_rank() // half

    def add(p, _):
        slot = slots[half + p]
        far = cross_ref[jnp.maximum(slot, 0)].astype(F32)
        for kv in range(2):
            sums = [own_ref[p, kv, i] + jnp.where((slot >= 0) & (i == t), far[kv], 0.0) for i in range(2)]
            if spread:
                for h in range(2):
                    tiles = [x[8 * h : 8 * h + 8] for x in sums]
                    out_ref[h * half + p, kv] = jnp.concatenate(tiles, 0).astype(BF16)
            else:
                for i in range(2):
                    out_ref[p, kv, i] = sums[i].astype(BF16)
        return 0

    lax.fori_loop(0, half, add, 0)


def finish_kernel(got_ref, own_ref, own_got_ref, keys_ref, values_ref):
    width = own_ref.shape[3]
    leaves = own_ref.shape[2] // 8
    for kv, out_ref in enumerate((keys_ref, values_ref)):
        for own in range(2):
            h = lax.axis_index("head") if own else 1 - lax.axis_index("head")
            ref = own_ref if own else own_got_ref
            lanes = pl.ds(pl.multiple_of(h * width, width), width)
            for j in range(0, leaves, 2):
                rows = slice(8 * j, 8 * j + 16)
                a, b = (got_ref[h * leaves + j + i, kv].astype(F32) for i in range(2))
                for t in range(2):
                    part = slice(8 * t, 8 * t + 8)
                    total = jnp.concatenate([a[part], b[part]], 0) + ref[kv, t, rows].astype(F32)
                    out_ref[t, rows, lanes] = total.astype(BF16)


def whole(shape):
    return pl.BlockSpec(shape, lambda i: (0,) * len(shape))


def simple(kernel, scalars, arrays, outs, scratch=(), slots=(), params=PARAMS):
    out_specs = [whole(x.shape) for x in outs] + [SMEM] * len(slots)
    outs = list(outs) + [jax.ShapeDtypeStruct((x,), jnp.int32) for x in slots]
    return pl.pallas_call(
        kernel,
        grid=(1,),
        in_specs=[SMEM] * len(scalars) + [whole(x.shape) for x in arrays],
        out_specs=out_specs,
        out_shape=outs,
        scratch_shapes=list(scratch),
        compiler_params=params,
    )(*scalars, *arrays)


def body(queries, keys, values, output_gradient, parents):
    leaf_count = lax.axis_size("leaf")
    head_count = lax.axis_size("head")
    half = leaf_count // 2
    depth = leaf_count // 4 - 2
    sides = [[half * i + j for j in range(half)] for i in range(2)]
    both = [[leaf_count * h + j for h in range(head_count) for j in side] for side in sides]
    swap = [(i, (i + half) % leaf_count) for i in range(leaf_count)]
    trees, part_rows, kv_all = keys.shape
    kv_width = kv_all // head_count
    rows = part_rows * head_count
    pieces = rows // half
    merged = head_count == 2 and part_rows == 8 * half and half % 2 == 0

    def exchange(x):
        return lax.all_to_all(x, "leaf", 0, 0, tiled=True, axis_index_groups=sides)

    def exchange_both(x):
        return lax.all_to_all(x, ("head", "leaf"), 0, 0, tiled=True, axis_index_groups=both)

    def to_other_head(x):
        return lax.ppermute(x, "head", [(0, 1), (1, 0)])

    def like(*shape, dtype=BF16):
        return jax.ShapeDtypeStruct(shape, dtype)

    if merged:
        send, keep, give, table = simple(
            pack_kernel,
            (parents,),
            (keys, values),
            [
                like(2 * half, 2, 16, kv_width),
                like(2, trees, part_rows, kv_width),
                like(2, trees, part_rows, kv_width),
                like(1, trees * leaf_count, dtype=jnp.int32),
            ],
            params=WIDE,
        )
        arrived, all_parents, theirs = lax.optimization_barrier(
            (exchange_both(send), lax.psum(table, "leaf"), to_other_head(give))
        )
        owns = [keep, theirs]
        arrived = arrived.reshape(2, half, 2, trees, 8, kv_width).transpose(1, 2, 3, 0, 4, 5)
        hub_own = arrived.reshape(half, 2, trees, pieces, kv_width)
    else:
        all_parents = lax.all_gather(parents, "leaf", axis=0, tiled=True).reshape(1, trees * leaf_count)
        pair = jnp.stack([keys, values]).reshape(2, trees, part_rows, head_count, kv_width)
        pair = jnp.moveaxis(pair, 3, 0)
        if head_count > 1:
            pair = lax.all_to_all(pair, "head", 0, 0, tiled=True)
        mine = pair.transpose(1, 2, 0, 3, 4).reshape(2, trees, rows, kv_width)
        hub_own = exchange(mine.reshape(2, trees, half, pieces, kv_width).transpose(2, 0, 1, 3, 4))
        owns = [mine]

    piece = (2, pieces, kv_width)
    few = min(2, half)

    def cross(x):
        def short():
            return jnp.concatenate([lax.ppermute(x[:few], "leaf", swap), x[few:]])

        return lax.cond(count[0] <= few, short, lambda: lax.ppermute(x, "leaf", swap))

    crossing, slots, count = simple(
        functools.partial(cross_kernel, depth),
        (all_parents,),
        (hub_own,),
        [like(half, *piece)],
        slots=(2 * half, 1),
    )
    (picked,) = simple(
        functools.partial(pick_kernel, depth),
        (all_parents, slots),
        (hub_own, cross(crossing)),
        [like(half, trees * depth, *piece)],
    )
    foreign = exchange(picked)
    if pieces % 16:
        foreign = foreign.transpose(1, 2, 0, 3, 4).reshape(1, trees * depth, 2, rows, kv_width)

    query_grad, *self_grads, foreign_grad = attend(all_parents, queries, output_gradient, owns, foreign)
    if pieces % 16:
        foreign_grad = foreign_grad.reshape(trees * depth, 2, half, pieces, kv_width).transpose(2, 0, 1, 3, 4)
    back = exchange(foreign_grad)
    if merged:
        back, own_got = lax.optimization_barrier((back, to_other_head(self_grads[1])))

    own_sum, cross_sum = simple(
        functools.partial(collect_kernel, depth),
        (all_parents, slots),
        (back,),
        [like(half, 2, trees, pieces, kv_width, dtype=F32), like(half, *piece)],
        [pltpu.VMEM((half,) + piece, F32)],
    )
    (hub_sum,) = simple(
        functools.partial(merge_kernel, merged),
        (slots,),
        (own_sum, cross(cross_sum)),
        [like(2 * half, 2, 16, kv_width) if merged else like(half, 2, trees, pieces, kv_width)],
    )
    if merged:
        returned = exchange_both(hub_sum)
        return query_grad, *simple(
            finish_kernel, (), (returned, self_grads[0], own_got), [like(*keys.shape)] * 2
        )
    returned = exchange(hub_sum).transpose(1, 2, 0, 3, 4).reshape(2, trees, rows, kv_width)
    total = (returned.astype(F32) + self_grads[0].astype(F32)).astype(BF16)
    total = jnp.moveaxis(total.reshape(2, trees, head_count, part_rows, kv_width), 2, 0)
    if head_count > 1:
        total = lax.all_to_all(total, "head", 0, 0, tiled=True)
    total = total.transpose(1, 2, 3, 0, 4).reshape(2, trees, part_rows, kv_all)
    return query_grad, total[0], total[1]


def solution(mesh):
    in_specs = (
        P("leaf", None, "head"),
        P("leaf", "head", None),
        P("leaf", "head", None),
        P("leaf", None, "head"),
        P("leaf"),
    )
    out_specs = (P("leaf", None, "head"), P("leaf", "head", None), P("leaf", "head", None))
    return jax.shard_map(body, mesh=mesh, in_specs=in_specs, out_specs=out_specs, check_vma=False)
```

```python
import functools
import math

import jax
import jax.numpy as jnp
from jax import lax
from jax.experimental import pallas as pl
from jax.experimental.pallas import tpu as pltpu
from jax.sharding import PartitionSpec as P

HEAD_DIM = 128

NT = (((1,), (1,)), ((), ()))
NN = (((1,), (0,)), ((), ()))
F32 = jnp.float32
BF16 = jnp.bfloat16
SMEM = pl.BlockSpec(memory_space=pltpu.SMEM)
PARAMS = pltpu.CompilerParams(vmem_limit_bytes=40 * 1024 * 1024)
WIDE = pltpu.CompilerParams(vmem_limit_bytes=60 * 1024 * 1024)


def dot(a, b, dims=NN):
    return lax.dot_general(a, b, dims, preferred_element_type=F32)


def attend_kernel(parts, parents, q_ref, do_ref, *refs):
    own_refs, anc_ref, dq_ref = refs[:parts], refs[parts], refs[parts + 1]
    dself_refs, danc_ref = refs[parts + 2 : 2 * parts + 2], refs[2 * parts + 2]
    hubs, depth, _, pieces, _ = anc_ref.shape
    rows = q_ref.shape[1]
    step_groups = anc_ref.shape[4] // HEAD_DIM
    heads = q_ref.shape[2] // HEAD_DIM // step_groups
    scale = HEAD_DIM ** (-0.5)
    c = scale * math.log2(math.e)
    block = 2 * leaf_rank() + pl.program_id(0)
    valid = []
    for _ in range(depth):
        block = above(parents, block)
        valid.append(block >= 0)

    def lanes(group, count=1):
        return slice(group * HEAD_DIM, (group + count) * HEAD_DIM)

    def seen(which, group):
        tiles = [anc_ref[:, k, which, :, lanes(group)].reshape(rows, HEAD_DIM) for k in range(depth)]
        return jnp.concatenate([ref[which, 0, :, lanes(group)] for ref in own_refs] + tiles, 0)

    held = [(seen(0, group), seen(1, group)) for group in range(step_groups)]
    held = [(keys, values, keys.T) for keys, values in held]
    first_token = lax.axis_index("head") * own_refs[0].shape[2] if parts == 2 else 0
    token = lax.rem(lax.broadcasted_iota(jnp.int32, (rows, rows), 0) + first_token, rows)
    hidden = token > lax.broadcasted_iota(jnp.int32, (rows, rows), 1)

    def products(group, h):
        q, do = (
            jnp.concatenate([ref[0, :, lanes(group * heads + i)] for i in range(h, h + 2)], 0)
            for ref in (q_ref, do_ref)
        )
        return group, h, q, do, dot(held[group][0], q, NT), dot(held[group][1], do, NT)

    def soften(scores, slopes):
        s = [scores[k * rows : (k + 1) * rows] for k in range(depth + 1)]
        d = [slopes[k * rows : (k + 1) * rows] for k in range(depth + 1)]
        s[0] = jnp.where(hidden, -1e30, s[0])
        peak = jnp.max(s[0], 0, keepdims=True)
        for k in range(depth):
            peak = jnp.maximum(peak, jnp.where(valid[k], jnp.max(s[k + 1], 0, keepdims=True), -1e30))
        peak = peak * c
        e = [jnp.exp2(s[0] * c - peak)]
        for k in range(depth):
            e.append(jnp.exp2(s[k + 1] * c - jnp.where(valid[k], peak, 1e30)))
        total = functools.reduce(jnp.add, [jnp.sum(x, 0, keepdims=True) for x in e])
        weighted = functools.reduce(jnp.add, [jnp.sum(x * y, 0, keepdims=True) for x, y in zip(e, d)])
        inverse = 1.0 / total
        mean = weighted * inverse
        p = [x * inverse for x in e]
        ds = [(x * (y - mean)).astype(BF16) for x, y in zip(p, d)]
        return jnp.concatenate([x.astype(BF16) for x in p], 0), jnp.concatenate(ds, 0)

    def gradients(group, h, q, do, ps, ds):
        dq_t = dot(held[group][2], ds) * scale
        for i in range(2):
            dq_ref[0, :, lanes(group * heads + h + i)] = dq_t[:, i * rows : (i + 1) * rows].T.astype(BF16)
        return dot(ds, q), dot(ps, do)

    def store(group, grads):
        for which in range(2):
            start = 0
            for ref in dself_refs:
                ref[which, 0, :, lanes(group)] = grads[which][start : start + ref.shape[2]].astype(BF16)
                start += ref.shape[2]
            for k in range(depth):
                grad = grads[which][(k + 1) * rows : (k + 2) * rows].astype(BF16)
                danc_ref[:, k, which, :, lanes(group)] = grad.reshape(hubs, pieces, HEAD_DIM)

    pairs = [(group, h) for group in range(step_groups) for h in range(0, heads, 2)]
    stage, ready, grads = products(*pairs[0]), None, None
    for i in range(len(pairs) + 1):
        following = products(*pairs[i + 1]) if i + 1 < len(pairs) else None
        soft = None
        if stage is not None:
            group, h, q, do, scores, slopes = stage
            halves = [soften(scores[:, x * rows : (x + 1) * rows], slopes[:, x * rows : (x + 1) * rows]) for x in range(2)]
            soft = (group, h, q, do, *[jnp.concatenate(x, 1) for x in zip(*halves)])
        if ready is not None:
            more = gradients(*ready)
            grads = more if grads is None else (grads[0] + more[0], grads[1] + more[1])
            if ready[1] == heads - 2:
                store(ready[0], (grads[0] * scale, grads[1]))
                grads = None
        stage, ready = following, soft


def attend(parents, queries, output_gradient, owns, foreign):
    trees, rows, width = queries.shape
    hubs, slots, _, pieces, kv_width = foreign.shape
    depth = slots // trees
    groups = kv_width // HEAD_DIM
    heads = width // groups // HEAD_DIM
    step = 2 - groups % 2
    lanes = step * HEAD_DIM
    q_spec = pl.BlockSpec((1, rows, heads * lanes), lambda t, g: (t, 0, g))
    own_specs = [pl.BlockSpec((2, 1, x.shape[2], lanes), lambda t, g: (0, t, 0, g)) for x in owns]
    anc_spec = pl.BlockSpec((hubs, depth, 2, pieces, lanes), lambda t, g: (0, t, 0, 0, g))
    return pl.pallas_call(
        functools.partial(attend_kernel, len(owns)),
        grid=(trees, groups // step),
        in_specs=[SMEM, q_spec, q_spec, *own_specs, anc_spec],
        out_specs=[q_spec, *own_specs, anc_spec],
        out_shape=[jax.ShapeDtypeStruct(x.shape, BF16) for x in (queries, *owns, foreign)],
        compiler_params=pltpu.CompilerParams(vmem_limit_bytes=50 * 1024 * 1024),
        cost_estimate=pl.CostEstimate(
            flops=10 * trees * groups * heads * (depth + 1) * rows * rows * HEAD_DIM,
            bytes_accessed=12 * rows * width,
            transcendentals=trees * groups * heads * (depth + 1) * rows * rows,
        ),
    )(parents, queries, output_gradient, *owns, foreign)


def pack_kernel(parents, keys_ref, values_ref, send_ref, keep_ref, give_ref, table_ref):
    heads, width = send_ref.shape[0] // (keys_ref.shape[1] // 8), keep_ref.shape[3]
    leaves = send_ref.shape[0] // heads
    for kv, ref in enumerate((keys_ref, values_ref)):
        for h in range(heads):
            for j in range(0, leaves, 2):
                tiles = [ref[t, 8 * j : 8 * j + 16, h * width : (h + 1) * width] for t in range(2)]
                send_ref[h * leaves + j, kv] = jnp.concatenate([x[:8] for x in tiles], 0)
                send_ref[h * leaves + j + 1, kv] = jnp.concatenate([x[8:] for x in tiles], 0)
        keep_ref[kv] = ref[:, :, pl.ds(pl.multiple_of(lax.axis_index("head") * width, width), width)]
        give_ref[kv] = ref[:, :, pl.ds(pl.multiple_of((1 - lax.axis_index("head")) * width, width), width)]
    block = lax.broadcasted_iota(jnp.int32, table_ref.shape, 1)
    table = jnp.zeros(table_ref.shape, jnp.int32)
    for t in range(2):
        table = jnp.where(block == 2 * leaf_rank() + t, parents[t], table)
    table_ref[...] = table


def leaf_rank():
    return lax.axis_index("leaf")


def above(parents, block):
    return jnp.where(block >= 0, parents[0, jnp.maximum(block, 0)], -1)


def far_slots(parents, half, depth, sending, slots, start):
    base = (leaf_rank() // half) * half
    source = base if sending else half - base
    target = half - source
    t = jnp.where(source == 0, 0, 1)

    def clear(p):
        slots[start + p] = -1

    def mark(d):
        block = 2 * (target + d) + t
        for _ in range(depth):
            block = above(parents, block)
            p = block // 2 - source

            @pl.when((block >= 0) & (p >= 0) & (p < half))
            def _():
                slots[start + p] = 0

    def number(p, count):
        needed = slots[start + p] >= 0
        slots[start + p] = jnp.where(needed, count, -1)
        return count + needed.astype(jnp.int32)

    each(half, clear)
    each(half, mark)
    return lax.fori_loop(0, half, number, 0, unroll=half <= 8)


def each(count, act):
    def step(i, _):
        act(i)
        return 0

    lax.fori_loop(0, count, step, 0, unroll=count <= 8)


def each_need(parents, half, depth, act):
    base = (leaf_rank() // half) * half

    def leaf(d):
        for t in range(2):
            block = 2 * (base + d) + t
            for k in range(depth):
                block = above(parents, block)
                p = jnp.maximum(block, 0) // 2
                here = (p >= base) & (p < base + half)
                act(d, t * depth + k, block >= 0, here, lax.rem(p, half), t)

    each(half, leaf)


def cross_kernel(depth, parents, own_ref, cross_ref, slots, count):
    half = own_ref.shape[0]
    other = far_slots(parents, half, depth, False, slots, 0)
    mine = far_slots(parents, half, depth, True, slots, half)
    count[0] = jnp.maximum(mine, other)
    t = leaf_rank() // half

    def copy(p):
        slot = slots[half + p]

        @pl.when(slot >= 0)
        def _():
            cross_ref[slot] = own_ref[p, :, t]

    each(half, copy)


def pick_kernel(depth, parents, slots, own_ref, cross_ref, out_ref):
    def act(d, slot, valid, here, p, t):
        far = cross_ref[jnp.maximum(slots[p], 0)]
        out_ref[d, slot] = jnp.where(here | ~valid, own_ref[p, :, t], far)

    each_need(parents, own_ref.shape[0], depth, act)


def collect_kernel(depth, parents, slots, in_ref, sums, cross_ref):
    half = cross_ref.shape[0]
    sums[...] = jnp.zeros_like(sums)

    def act(d, slot, valid, here, p, t):
        row = jnp.where(here, t * half + p, 2 * half + jnp.maximum(slots[p], 0))
        sums[jnp.where(valid, row, 3 * half)] += in_ref[d, slot].astype(F32)

    each_need(parents, half, depth, act)
    cross_ref[...] = sums[2 * half : 3 * half].astype(BF16)


def merge_kernel(spread, slots, sums_ref, cross_ref, out_ref):
    half = cross_ref.shape[0]
    t = leaf_rank() // half

    def add(p):
        slot = slots[half + p]
        far = cross_ref[jnp.maximum(slot, 0)].astype(F32)
        for kv in range(2):
            sums = [sums_ref[i * half + p, kv] + jnp.where((slot >= 0) & (i == t), far[kv], 0.0) for i in range(2)]
            if spread:
                for h in range(2):
                    tiles = [x[8 * h : 8 * h + 8] for x in sums]
                    out_ref[h * half + p, kv] = jnp.concatenate(tiles, 0).astype(BF16)
            else:
                for i in range(2):
                    out_ref[p, kv, i] = sums[i].astype(BF16)

    each(half, add)


def finish_kernel(got_ref, own_ref, own_got_ref, keys_ref, values_ref):
    width = own_ref.shape[3]
    leaves = own_ref.shape[2] // 8
    for kv, out_ref in enumerate((keys_ref, values_ref)):
        for own in range(2):
            h = lax.axis_index("head") if own else 1 - lax.axis_index("head")
            ref = own_ref if own else own_got_ref
            lanes = pl.ds(pl.multiple_of(h * width, width), width)
            for j in range(0, leaves, 2):
                rows = slice(8 * j, 8 * j + 16)
                a, b = (got_ref[h * leaves + j + i, kv].astype(F32) for i in range(2))
                for t in range(2):
                    part = slice(8 * t, 8 * t + 8)
                    total = jnp.concatenate([a[part], b[part]], 0) + ref[kv, t, rows].astype(F32)
                    out_ref[t, rows, lanes] = total.astype(BF16)


def whole(shape):
    return pl.BlockSpec(shape, lambda i: (0,) * len(shape))


def simple(kernel, scalars, arrays, outs, slots=(), params=PARAMS):
    out_specs = [whole(x.shape) for x in outs] + [SMEM] * len(slots)
    outs = list(outs) + [jax.ShapeDtypeStruct((x,), jnp.int32) for x in slots]
    return pl.pallas_call(
        kernel,
        grid=(1,),
        in_specs=[SMEM] * len(scalars) + [whole(x.shape) for x in arrays],
        out_specs=out_specs,
        out_shape=outs,
        compiler_params=params,
    )(*scalars, *arrays)


def body(queries, keys, values, output_gradient, parents):
    leaf_count = lax.axis_size("leaf")
    head_count = lax.axis_size("head")
    half = leaf_count // 2
    depth = leaf_count // 4 - 2
    sides = [[half * i + j for j in range(half)] for i in range(2)]
    both = [[leaf_count * h + j for h in range(head_count) for j in side] for side in sides]
    swap = [(i, (i + half) % leaf_count) for i in range(leaf_count)]
    trees, part_rows, kv_all = keys.shape
    kv_width = kv_all // head_count
    rows = part_rows * head_count
    pieces = rows // half
    merged = head_count == 2 and part_rows == 8 * half and half % 2 == 0

    def exchange(x):
        return lax.all_to_all(x, "leaf", 0, 0, tiled=True, axis_index_groups=sides)

    def exchange_both(x):
        return lax.all_to_all(x, ("head", "leaf"), 0, 0, tiled=True, axis_index_groups=both)

    def to_other_head(x):
        return lax.ppermute(x, "head", [(0, 1), (1, 0)])

    def like(*shape, dtype=BF16):
        return jax.ShapeDtypeStruct(shape, dtype)

    if merged:
        send, keep, give, table = simple(
            pack_kernel,
            (parents,),
            (keys, values),
            [
                like(2 * half, 2, 16, kv_width),
                like(2, trees, part_rows, kv_width),
                like(2, trees, part_rows, kv_width),
                like(1, trees * leaf_count, dtype=jnp.int32),
            ],
            params=WIDE,
        )
        arrived, all_parents, theirs = lax.optimization_barrier(
            (exchange_both(send), lax.psum(table, "leaf"), to_other_head(give))
        )
        owns = [keep, theirs]
        arrived = arrived.reshape(2, half, 2, trees, 8, kv_width).transpose(1, 2, 3, 0, 4, 5)
        hub_own = arrived.reshape(half, 2, trees, pieces, kv_width)
    else:
        all_parents = lax.all_gather(parents, "leaf", axis=0, tiled=True).reshape(1, trees * leaf_count)
        pair = jnp.stack([keys, values]).reshape(2, trees, part_rows, head_count, kv_width)
        pair = jnp.moveaxis(pair, 3, 0)
        if head_count > 1:
            pair = lax.all_to_all(pair, "head", 0, 0, tiled=True)
        mine = pair.transpose(1, 2, 0, 3, 4).reshape(2, trees, rows, kv_width)
        hub_own = exchange(mine.reshape(2, trees, half, pieces, kv_width).transpose(2, 0, 1, 3, 4))
        owns = [mine]

    piece = (2, pieces, kv_width)
    few = min(2, half)

    def cross(x):
        def short():
            return jnp.concatenate([lax.ppermute(x[:few], "leaf", swap), x[few:]])

        return lax.cond(count[0] <= few, short, lambda: lax.ppermute(x, "leaf", swap))

    crossing, slots, count = simple(
        functools.partial(cross_kernel, depth),
        (all_parents,),
        (hub_own,),
        [like(half, *piece)],
        slots=(2 * half, 1),
    )
    (picked,) = simple(
        functools.partial(pick_kernel, depth),
        (all_parents, slots),
        (hub_own, cross(crossing)),
        [like(half, trees * depth, *piece)],
    )
    foreign = exchange(picked)
    if pieces % 16:
        foreign = foreign.transpose(1, 2, 0, 3, 4).reshape(1, trees * depth, 2, rows, kv_width)

    query_grad, *self_grads, foreign_grad = attend(all_parents, queries, output_gradient, owns, foreign)
    if pieces % 16:
        foreign_grad = foreign_grad.reshape(trees * depth, 2, half, pieces, kv_width).transpose(2, 0, 1, 3, 4)
    back = exchange(foreign_grad)
    if merged:
        back, own_got = lax.optimization_barrier((back, to_other_head(self_grads[1])))

    sums, cross_sum = simple(
        functools.partial(collect_kernel, depth),
        (all_parents, slots),
        (back,),
        [like(3 * half + 1, *piece, dtype=F32), like(half, *piece)],
    )
    (hub_sum,) = simple(
        functools.partial(merge_kernel, merged),
        (slots,),
        (sums, cross(cross_sum)),
        [like(2 * half, 2, 16, kv_width) if merged else like(half, 2, trees, pieces, kv_width)],
    )
    if merged:
        returned = exchange_both(hub_sum)
        return query_grad, *simple(
            finish_kernel, (), (returned, self_grads[0], own_got), [like(*keys.shape)] * 2
        )
    returned = exchange(hub_sum).transpose(1, 2, 0, 3, 4).reshape(2, trees, rows, kv_width)
    total = (returned.astype(F32) + self_grads[0].astype(F32)).astype(BF16)
    total = jnp.moveaxis(total.reshape(2, trees, head_count, part_rows, kv_width), 2, 0)
    if head_count > 1:
        total = lax.all_to_all(total, "head", 0, 0, tiled=True)
    total = total.transpose(1, 2, 3, 0, 4).reshape(2, trees, part_rows, kv_all)
    return query_grad, total[0], total[1]


def solution(mesh):
    in_specs = (
        P("leaf", None, "head"),
        P("leaf", "head", None),
        P("leaf", "head", None),
        P("leaf", None, "head"),
        P("leaf"),
    )
    out_specs = (P("leaf", None, "head"), P("leaf", "head", None), P("leaf", "head", None))
    return jax.shard_map(body, mesh=mesh, in_specs=in_specs, out_specs=out_specs, check_vma=False)
```

```python
import functools
import math

import jax
import jax.numpy as jnp
from jax import lax
from jax.experimental import pallas as pl
from jax.experimental.pallas import tpu as pltpu
from jax.sharding import PartitionSpec as P

HEAD_DIM = 128

NT = (((1,), (1,)), ((), ()))
NN = (((1,), (0,)), ((), ()))
F32 = jnp.float32
BF16 = jnp.bfloat16
SMEM = pl.BlockSpec(memory_space=pltpu.SMEM)
PARAMS = pltpu.CompilerParams(vmem_limit_bytes=40 * 1024 * 1024)
WIDE = pltpu.CompilerParams(vmem_limit_bytes=60 * 1024 * 1024)


def dot(a, b, dims=NN):
    return lax.dot_general(a, b, dims, preferred_element_type=F32)


def attend_kernel(parts, tree, parents, q_ref, do_ref, *refs):
    own_refs, anc_ref = refs[:parts], refs[parts]
    dq_ref, *dself_refs, danc_ref = refs[-parts - 2 :]
    hubs, depth, _, pieces, _ = anc_ref.shape
    rows = q_ref.shape[1]
    step_groups = anc_ref.shape[4] // HEAD_DIM
    heads = q_ref.shape[2] // HEAD_DIM // step_groups
    scale = HEAD_DIM ** (-0.5)
    c = scale * math.log2(math.e)
    block = 2 * leaf_rank() + tree()
    valid = []
    for _ in range(depth):
        block = above(parents, block)
        valid.append(block >= 0)

    def lanes(group, count=1):
        return slice(group * HEAD_DIM, (group + count) * HEAD_DIM)

    def seen(which, group):
        tiles = [anc_ref[:, k, which, :, lanes(group)].reshape(rows, HEAD_DIM) for k in range(depth)]
        return jnp.concatenate([ref[which, 0, :, lanes(group)] for ref in own_refs] + tiles, 0)

    held = [(seen(0, group), seen(1, group)) for group in range(step_groups)]
    held = [(keys, values, keys.T) for keys, values in held]
    first_token = lax.axis_index("head") * own_refs[0].shape[2] if parts == 2 else 0
    token = lax.rem(lax.broadcasted_iota(jnp.int32, (rows, rows), 0) + first_token, rows)
    hidden = token > lax.broadcasted_iota(jnp.int32, (rows, rows), 1)

    def products(group, h):
        q, do = (
            jnp.concatenate([ref[0, :, lanes(group * heads + i)] for i in range(h, h + 2)], 0)
            for ref in (q_ref, do_ref)
        )
        return group, h, q, do, dot(held[group][0], q, NT), dot(held[group][1], do, NT)

    def soften(scores, slopes):
        s = [scores[k * rows : (k + 1) * rows] for k in range(depth + 1)]
        d = [slopes[k * rows : (k + 1) * rows] for k in range(depth + 1)]
        s[0] = jnp.where(hidden, -1e30, s[0])
        peak = jnp.max(s[0], 0, keepdims=True)
        for k in range(depth):
            peak = jnp.maximum(peak, jnp.where(valid[k], jnp.max(s[k + 1], 0, keepdims=True), -1e30))
        peak = peak * c
        e = [jnp.exp2(s[0] * c - peak)]
        for k in range(depth):
            e.append(jnp.exp2(s[k + 1] * c - jnp.where(valid[k], peak, 1e30)))
        total = functools.reduce(jnp.add, [jnp.sum(x, 0, keepdims=True) for x in e])
        weighted = functools.reduce(jnp.add, [jnp.sum(x * y, 0, keepdims=True) for x, y in zip(e, d)])
        inverse = 1.0 / total
        mean = weighted * inverse
        p = [x * inverse for x in e]
        ds = [(x * (y - mean)).astype(BF16) for x, y in zip(p, d)]
        return jnp.concatenate([x.astype(BF16) for x in p], 0), jnp.concatenate(ds, 0)

    def gradients(group, h, q, do, ps, ds):
        dq_t = dot(held[group][2], ds) * scale
        for i in range(2):
            dq_ref[0, :, lanes(group * heads + h + i)] = dq_t[:, i * rows : (i + 1) * rows].T.astype(BF16)
        return dot(ds, q), dot(ps, do)

    def store(group, grads):
        for which in range(2):
            start = 0
            for ref in dself_refs:
                ref[which, 0, :, lanes(group)] = grads[which][start : start + ref.shape[2]].astype(BF16)
                start += ref.shape[2]
            for k in range(depth):
                grad = grads[which][(k + 1) * rows : (k + 2) * rows].astype(BF16)
                danc_ref[:, k, which, :, lanes(group)] = grad.reshape(hubs, pieces, HEAD_DIM)

    pairs = [(group, h) for group in range(step_groups) for h in range(0, heads, 2)]
    stage, ready, grads = products(*pairs[0]), None, None
    for i in range(len(pairs) + 1):
        following = products(*pairs[i + 1]) if i + 1 < len(pairs) else None
        soft = None
        if stage is not None:
            group, h, q, do, scores, slopes = stage
            halves = [soften(scores[:, x * rows : (x + 1) * rows], slopes[:, x * rows : (x + 1) * rows]) for x in range(2)]
            soft = (group, h, q, do, *[jnp.concatenate(x, 1) for x in zip(*halves)])
        if ready is not None:
            more = gradients(*ready)
            grads = more if grads is None else (grads[0] + more[0], grads[1] + more[1])
            if ready[1] == heads - 2:
                store(ready[0], (grads[0] * scale, grads[1]))
                grads = None
        stage, ready = following, soft


def attend(parents, queries, output_gradient, owns, foreign, near, half, before):
    trees, rows, width = queries.shape
    hubs, depth, _, pieces, kv_width = foreign.shape
    groups = kv_width // HEAD_DIM
    heads = width // groups // HEAD_DIM
    step = 2 - groups % 2
    lanes = step * HEAD_DIM

    def tree():
        return leaf_rank() // half if near else 1 - leaf_rank() // half

    q_spec = pl.BlockSpec((1, rows, heads * lanes), lambda g: (tree(), 0, g))
    own_specs = [pl.BlockSpec((2, 1, x.shape[2], lanes), lambda g: (0, tree(), 0, g)) for x in owns]
    got_spec = pl.BlockSpec((hubs, depth, 2, pieces, lanes), lambda g: (0, 0, 0, 0, g))
    give_spec = pl.BlockSpec((hubs, depth, 2, pieces, lanes), lambda g: (0, tree(), 0, 0, g))
    out_shape = [jax.ShapeDtypeStruct(x.shape, BF16) for x in (queries, *owns)]
    out_shape.append(jax.ShapeDtypeStruct((hubs, trees * depth, 2, pieces, kv_width), BF16))
    return pl.pallas_call(
        functools.partial(attend_kernel, len(owns), tree),
        grid=(groups // step,),
        in_specs=[SMEM, q_spec, q_spec, *own_specs, got_spec] + [pl.BlockSpec(memory_space=pl.ANY)] * len(before),
        out_specs=[q_spec, *own_specs, give_spec],
        out_shape=out_shape,
        input_output_aliases={4 + len(owns) + i: i for i in range(len(before))},
        compiler_params=pltpu.CompilerParams(vmem_limit_bytes=50 * 1024 * 1024),
        cost_estimate=pl.CostEstimate(
            flops=10 * groups * heads * (depth + 1) * rows * rows * HEAD_DIM,
            bytes_accessed=6 * rows * width,
            transcendentals=groups * heads * (depth + 1) * rows * rows,
        ),
    )(parents, queries, output_gradient, *owns, foreign, *before)


def pack_kernel(parents, keys_ref, values_ref, send_ref, keep_ref, give_ref, table_ref):
    heads, width = send_ref.shape[0] // (keys_ref.shape[1] // 8), keep_ref.shape[3]
    leaves = send_ref.shape[0] // heads
    for kv, ref in enumerate((keys_ref, values_ref)):
        for h in range(heads):
            for j in range(0, leaves, 2):
                tiles = [ref[t, 8 * j : 8 * j + 16, h * width : (h + 1) * width] for t in range(2)]
                send_ref[h * leaves + j, kv] = jnp.concatenate([x[:8] for x in tiles], 0)
                send_ref[h * leaves + j + 1, kv] = jnp.concatenate([x[8:] for x in tiles], 0)
        keep_ref[kv] = ref[:, :, pl.ds(pl.multiple_of(lax.axis_index("head") * width, width), width)]
        give_ref[kv] = ref[:, :, pl.ds(pl.multiple_of((1 - lax.axis_index("head")) * width, width), width)]
    block = lax.broadcasted_iota(jnp.int32, table_ref.shape, 1)
    table = jnp.zeros(table_ref.shape, jnp.int32)
    for t in range(2):
        table = jnp.where(block == 2 * leaf_rank() + t, parents[t], table)
    table_ref[...] = table


def leaf_rank():
    return lax.axis_index("leaf")


def above(parents, block):
    return jnp.where(block >= 0, parents[0, jnp.maximum(block, 0)], -1)


def far_slots(parents, half, depth, sending, slots, start):
    base = (leaf_rank() // half) * half
    source = base if sending else half - base
    target = half - source
    t = jnp.where(source == 0, 0, 1)

    def clear(p):
        slots[start + p] = -1

    def mark(d):
        block = 2 * (target + d) + t
        for _ in range(depth):
            block = above(parents, block)
            p = block // 2 - source

            @pl.when((block >= 0) & (p >= 0) & (p < half))
            def _():
                slots[start + p] = 0

    def number(p, count):
        needed = slots[start + p] >= 0
        slots[start + p] = jnp.where(needed, count, -1)
        return count + needed.astype(jnp.int32)

    each(half, clear)
    each(half, mark)
    return lax.fori_loop(0, half, number, 0, unroll=half <= 8)


def each(count, act):
    def step(i, _):
        act(i)
        return 0

    lax.fori_loop(0, count, step, 0, unroll=count <= 8)


def each_need(parents, half, depth, trees, act):
    base = (leaf_rank() // half) * half

    def leaf(d):
        for i, t in enumerate(trees):
            block = 2 * (base + d) + t
            for k in range(depth):
                block = above(parents, block)
                p = jnp.maximum(block, 0) // 2
                here = (p >= base) & (p < base + half)
                act(d, i * depth + k, block >= 0, here, lax.rem(p, half), t)

    each(half, leaf)


def cross_kernel(depth, parents, own_ref, cross_ref, slots, count):
    half = own_ref.shape[0]
    other = far_slots(parents, half, depth, False, slots, 0)
    mine = far_slots(parents, half, depth, True, slots, half)
    count[0] = jnp.maximum(mine, other)
    t = leaf_rank() // half

    def copy(p):
        slot = slots[half + p]

        @pl.when(slot >= 0)
        def _():
            cross_ref[slot] = own_ref[p, :, t]

    each(half, copy)


def pick_near_kernel(depth, parents, own_ref, out_ref):
    half = own_ref.shape[0]
    near = leaf_rank() // half

    def act(d, k, valid, here, p, t):
        out_ref[d, k] = own_ref[p, :, t]

    each_need(parents, half, depth, (near,), act)


def pick_far_kernel(depth, parents, slots, own_ref, cross_ref, out_ref):
    half = own_ref.shape[0]
    far = 1 - leaf_rank() // half

    def act(d, k, valid, here, p, t):
        crossed = cross_ref[jnp.maximum(slots[p], 0)]
        out_ref[d, k] = jnp.where(here | ~valid, own_ref[p, :, t], crossed)

    each_need(parents, half, depth, (far,), act)


def collect_kernel(depth, parents, slots, in_ref, sums, cross_ref):
    half = cross_ref.shape[0]
    sums[...] = jnp.zeros_like(sums)

    def act(d, slot, valid, here, p, t):
        row = jnp.where(here, t * half + p, 2 * half + jnp.maximum(slots[p], 0))
        sums[jnp.where(valid, row, 3 * half)] += in_ref[d, slot].astype(F32)

    each_need(parents, half, depth, (0, 1), act)
    cross_ref[...] = sums[2 * half : 3 * half].astype(BF16)


def merge_kernel(spread, slots, sums_ref, cross_ref, out_ref):
    half = cross_ref.shape[0]
    t = leaf_rank() // half

    def add(p):
        slot = slots[half + p]
        far = cross_ref[jnp.maximum(slot, 0)].astype(F32)
        for kv in range(2):
            sums = [sums_ref[i * half + p, kv] + jnp.where((slot >= 0) & (i == t), far[kv], 0.0) for i in range(2)]
            if spread:
                for h in range(2):
                    tiles = [x[8 * h : 8 * h + 8] for x in sums]
                    out_ref[h * half + p, kv] = jnp.concatenate(tiles, 0).astype(BF16)
            else:
                for i in range(2):
                    out_ref[p, kv, i] = sums[i].astype(BF16)

    each(half, add)


def finish_kernel(got_ref, own_ref, own_got_ref, keys_ref, values_ref):
    width = own_ref.shape[3]
    leaves = own_ref.shape[2] // 8
    for kv, out_ref in enumerate((keys_ref, values_ref)):
        for own in range(2):
            h = lax.axis_index("head") if own else 1 - lax.axis_index("head")
            ref = own_ref if own else own_got_ref
            lanes = pl.ds(pl.multiple_of(h * width, width), width)
            for j in range(0, leaves, 2):
                rows = slice(8 * j, 8 * j + 16)
                a, b = (got_ref[h * leaves + j + i, kv].astype(F32) for i in range(2))
                for t in range(2):
                    part = slice(8 * t, 8 * t + 8)
                    total = jnp.concatenate([a[part], b[part]], 0) + ref[kv, t, rows].astype(F32)
                    out_ref[t, rows, lanes] = total.astype(BF16)


def whole(shape):
    return pl.BlockSpec(shape, lambda i: (0,) * len(shape))


def simple(kernel, scalars, arrays, outs, slots=(), params=PARAMS):
    out_specs = [whole(x.shape) for x in outs] + [SMEM] * len(slots)
    outs = list(outs) + [jax.ShapeDtypeStruct((x,), jnp.int32) for x in slots]
    return pl.pallas_call(
        kernel,
        grid=(1,),
        in_specs=[SMEM] * len(scalars) + [whole(x.shape) for x in arrays],
        out_specs=out_specs,
        out_shape=outs,
        compiler_params=params,
    )(*scalars, *arrays)


def body(queries, keys, values, output_gradient, parents):
    leaf_count = lax.axis_size("leaf")
    head_count = lax.axis_size("head")
    half = leaf_count // 2
    depth = leaf_count // 4 - 2
    sides = [[half * i + j for j in range(half)] for i in range(2)]
    both = [[leaf_count * h + j for h in range(head_count) for j in side] for side in sides]
    swap = [(i, (i + half) % leaf_count) for i in range(leaf_count)]
    trees, part_rows, kv_all = keys.shape
    kv_width = kv_all // head_count
    rows = part_rows * head_count
    pieces = rows // half
    merged = head_count == 2 and part_rows == 8 * half and half % 2 == 0

    def exchange(x):
        return lax.all_to_all(x, "leaf", 0, 0, tiled=True, axis_index_groups=sides)

    def exchange_both(x):
        return lax.all_to_all(x, ("head", "leaf"), 0, 0, tiled=True, axis_index_groups=both)

    def to_other_head(x):
        return lax.ppermute(x, "head", [(0, 1), (1, 0)])

    def like(*shape, dtype=BF16):
        return jax.ShapeDtypeStruct(shape, dtype)

    if merged:
        send, keep, give, table = simple(
            pack_kernel,
            (parents,),
            (keys, values),
            [
                like(2 * half, 2, 16, kv_width),
                like(2, trees, part_rows, kv_width),
                like(2, trees, part_rows, kv_width),
                like(1, trees * leaf_count, dtype=jnp.int32),
            ],
            params=WIDE,
        )
        arrived, all_parents, theirs = lax.optimization_barrier(
            (exchange_both(send), lax.psum(table, "leaf"), to_other_head(give))
        )
        owns = [keep, theirs]
        arrived = arrived.reshape(2, half, 2, trees, 8, kv_width).transpose(1, 2, 3, 0, 4, 5)
        hub_own = arrived.reshape(half, 2, trees, pieces, kv_width)
    else:
        all_parents = lax.all_gather(parents, "leaf", axis=0, tiled=True).reshape(1, trees * leaf_count)
        pair = jnp.stack([keys, values]).reshape(2, trees, part_rows, head_count, kv_width)
        pair = jnp.moveaxis(pair, 3, 0)
        if head_count > 1:
            pair = lax.all_to_all(pair, "head", 0, 0, tiled=True)
        mine = pair.transpose(1, 2, 0, 3, 4).reshape(2, trees, rows, kv_width)
        hub_own = exchange(mine.reshape(2, trees, half, pieces, kv_width).transpose(2, 0, 1, 3, 4))
        owns = [mine]

    piece = (2, pieces, kv_width)
    few = min(2, half)

    def cross(x):
        def short():
            return jnp.concatenate([lax.ppermute(x[:few], "leaf", swap), x[few:]])

        return lax.cond(count[0] <= few, short, lambda: lax.ppermute(x, "leaf", swap))

    picked_shape = [like(half, depth, *piece)]
    (picked_near,) = simple(functools.partial(pick_near_kernel, depth), (all_parents,), (hub_own,), picked_shape)
    foreign_near = exchange(picked_near)
    crossing, slots, count = simple(
        functools.partial(cross_kernel, depth),
        (all_parents,),
        (hub_own,),
        [like(half, *piece)],
        slots=(2 * half, 1),
    )
    (picked_far,) = simple(
        functools.partial(pick_far_kernel, depth), (all_parents, slots), (hub_own, cross(crossing)), picked_shape
    )
    foreign_near, picked_far = lax.optimization_barrier((foreign_near, picked_far))
    foreign_far = exchange(picked_far)

    results = ()
    for near, foreign in ((True, foreign_near), (False, foreign_far)):
        if pieces % 16:
            foreign = foreign.transpose(1, 2, 0, 3, 4).reshape(1, depth, 2, rows, kv_width)
        results = attend(all_parents, queries, output_gradient, owns, foreign, near, half, results)
    query_grad, *self_grads, foreign_grad = results
    if pieces % 16:
        foreign_grad = foreign_grad.reshape(trees * depth, 2, half, pieces, kv_width).transpose(2, 0, 1, 3, 4)
    back = exchange(foreign_grad)
    if merged:
        back, own_got = lax.optimization_barrier((back, to_other_head(self_grads[1])))

    sums, cross_sum = simple(
        functools.partial(collect_kernel, depth),
        (all_parents, slots),
        (back,),
        [like(3 * half + 1, *piece, dtype=F32), like(half, *piece)],
    )
    (hub_sum,) = simple(
        functools.partial(merge_kernel, merged),
        (slots,),
        (sums, cross(cross_sum)),
        [like(2 * half, 2, 16, kv_width) if merged else like(half, 2, trees, pieces, kv_width)],
    )
    if merged:
        returned = exchange_both(hub_sum)
        return query_grad, *simple(
            finish_kernel, (), (returned, self_grads[0], own_got), [like(*keys.shape)] * 2
        )
    returned = exchange(hub_sum).transpose(1, 2, 0, 3, 4).reshape(2, trees, rows, kv_width)
    total = (returned.astype(F32) + self_grads[0].astype(F32)).astype(BF16)
    total = jnp.moveaxis(total.reshape(2, trees, head_count, part_rows, kv_width), 2, 0)
    if head_count > 1:
        total = lax.all_to_all(total, "head", 0, 0, tiled=True)
    total = total.transpose(1, 2, 3, 0, 4).reshape(2, trees, part_rows, kv_all)
    return query_grad, total[0], total[1]


def solution(mesh):
    in_specs = (
        P("leaf", None, "head"),
        P("leaf", "head", None),
        P("leaf", "head", None),
        P("leaf", None, "head"),
        P("leaf"),
    )
    out_specs = (P("leaf", None, "head"), P("leaf", "head", None), P("leaf", "head", None))
    return jax.shard_map(body, mesh=mesh, in_specs=in_specs, out_specs=out_specs, check_vma=False)
```

```python
import functools
import math

import jax
import jax.numpy as jnp
from jax import lax
from jax.experimental import pallas as pl
from jax.experimental.pallas import tpu as pltpu
from jax.sharding import PartitionSpec as P

HEAD_DIM = 128

NT = (((1,), (1,)), ((), ()))
NN = (((1,), (0,)), ((), ()))
F32 = jnp.float32
BF16 = jnp.bfloat16
SMEM = pl.BlockSpec(memory_space=pltpu.SMEM)
PARAMS = pltpu.CompilerParams(vmem_limit_bytes=40 * 1024 * 1024)
WIDE = pltpu.CompilerParams(vmem_limit_bytes=60 * 1024 * 1024)


def dot(a, b, dims=NN):
    return lax.dot_general(a, b, dims, preferred_element_type=F32)


def attend_kernel(parts, tree, parents, q_ref, do_ref, *refs):
    own_refs, anc_ref = refs[:parts], refs[parts]
    dq_ref, *dself_refs, danc_ref = refs[-parts - 2 :]
    hubs, depth, _, pieces, _ = anc_ref.shape
    rows = q_ref.shape[1]
    step_groups = anc_ref.shape[4] // HEAD_DIM
    heads = q_ref.shape[2] // HEAD_DIM // step_groups
    scale = HEAD_DIM ** (-0.5)
    c = scale * math.log2(math.e)
    block = 2 * leaf_rank() + tree()
    valid = []
    for _ in range(depth):
        block = above(parents, block)
        valid.append(block >= 0)

    def lanes(group, count=1):
        return slice(group * HEAD_DIM, (group + count) * HEAD_DIM)

    def seen(which, group):
        tiles = [anc_ref[:, k, which, :, lanes(group)].reshape(rows, HEAD_DIM) for k in range(depth)]
        return jnp.concatenate([ref[which, 0, :, lanes(group)] for ref in own_refs] + tiles, 0)

    held = [(seen(0, group), seen(1, group)) for group in range(step_groups)]
    held = [(keys, values, keys.T) for keys, values in held]
    first_token = lax.axis_index("head") * own_refs[0].shape[2] if parts == 2 else 0
    token = lax.rem(lax.broadcasted_iota(jnp.int32, (rows, rows), 0) + first_token, rows)
    hidden = token > lax.broadcasted_iota(jnp.int32, (rows, rows), 1)

    def products(group, h):
        q, do = (
            jnp.concatenate([ref[0, :, lanes(group * heads + i)] for i in range(h, h + 2)], 0)
            for ref in (q_ref, do_ref)
        )
        return group, h, q, do, dot(held[group][0], q, NT), dot(held[group][1], do, NT)

    def soften(scores, slopes):
        s = [scores[k * rows : (k + 1) * rows] for k in range(depth + 1)]
        d = [slopes[k * rows : (k + 1) * rows] for k in range(depth + 1)]
        s[0] = jnp.where(hidden, -1e30, s[0])
        peak = jnp.max(s[0], 0, keepdims=True)
        for k in range(depth):
            peak = jnp.maximum(peak, jnp.where(valid[k], jnp.max(s[k + 1], 0, keepdims=True), -1e30))
        peak = peak * c
        e = [jnp.exp2(s[0] * c - peak)]
        for k in range(depth):
            e.append(jnp.exp2(s[k + 1] * c - jnp.where(valid[k], peak, 1e30)))
        total = functools.reduce(jnp.add, [jnp.sum(x, 0, keepdims=True) for x in e])
        weighted = functools.reduce(jnp.add, [jnp.sum(x * y, 0, keepdims=True) for x, y in zip(e, d)])
        inverse = 1.0 / total
        mean = weighted * inverse
        p = [x * inverse for x in e]
        ds = [(x * (y - mean)).astype(BF16) for x, y in zip(p, d)]
        return jnp.concatenate([x.astype(BF16) for x in p], 0), jnp.concatenate(ds, 0)

    def gradients(group, h, q, do, ps, ds):
        dq_t = dot(held[group][2], ds) * scale
        for i in range(2):
            dq_ref[0, :, lanes(group * heads + h + i)] = dq_t[:, i * rows : (i + 1) * rows].T.astype(BF16)
        return dot(ds, q), dot(ps, do)

    def store(group, grads):
        for which in range(2):
            start = 0
            for ref in dself_refs:
                ref[which, 0, :, lanes(group)] = grads[which][start : start + ref.shape[2]].astype(BF16)
                start += ref.shape[2]
            for k in range(depth):
                grad = grads[which][(k + 1) * rows : (k + 2) * rows].astype(BF16)
                danc_ref[:, k, which, :, lanes(group)] = grad.reshape(hubs, pieces, HEAD_DIM)

    pairs = [(group, h) for group in range(step_groups) for h in range(0, heads, 2)]
    stage, ready, grads = products(*pairs[0]), None, None
    for i in range(len(pairs) + 1):
        following = products(*pairs[i + 1]) if i + 1 < len(pairs) else None
        soft = None
        if stage is not None:
            group, h, q, do, scores, slopes = stage
            halves = [soften(scores[:, x * rows : (x + 1) * rows], slopes[:, x * rows : (x + 1) * rows]) for x in range(2)]
            soft = (group, h, q, do, *[jnp.concatenate(x, 1) for x in zip(*halves)])
        if ready is not None:
            more = gradients(*ready)
            grads = more if grads is None else (grads[0] + more[0], grads[1] + more[1])
            if ready[1] == heads - 2:
                store(ready[0], (grads[0] * scale, grads[1]))
                grads = None
        stage, ready = following, soft


def attend(parents, queries, output_gradient, owns, foreign, near, half, before):
    _, rows, width = queries.shape
    hubs, depth, _, pieces, kv_width = foreign.shape
    groups = kv_width // HEAD_DIM
    heads = width // groups // HEAD_DIM
    step = 2 - groups % 2
    lanes = step * HEAD_DIM

    def tree():
        return leaf_rank() // half if near else 1 - leaf_rank() // half

    q_spec = pl.BlockSpec((1, rows, heads * lanes), lambda g: (tree(), 0, g))
    own_specs = [pl.BlockSpec((2, 1, x.shape[2], lanes), lambda g: (0, tree(), 0, g)) for x in owns]
    got_spec = pl.BlockSpec((hubs, depth, 2, pieces, lanes), lambda g: (0, 0, 0, 0, g))
    out_shape = [jax.ShapeDtypeStruct(x.shape, BF16) for x in (queries, *owns, foreign)]
    return pl.pallas_call(
        functools.partial(attend_kernel, len(owns), tree),
        grid=(groups // step,),
        in_specs=[SMEM, q_spec, q_spec, *own_specs, got_spec] + [pl.BlockSpec(memory_space=pl.ANY)] * len(before),
        out_specs=[q_spec, *own_specs, got_spec],
        out_shape=out_shape,
        input_output_aliases={4 + len(owns) + i: i for i in range(len(before))},
        compiler_params=pltpu.CompilerParams(vmem_limit_bytes=50 * 1024 * 1024),
        cost_estimate=pl.CostEstimate(
            flops=10 * groups * heads * (depth + 1) * rows * rows * HEAD_DIM,
            bytes_accessed=6 * rows * width,
            transcendentals=groups * heads * (depth + 1) * rows * rows,
        ),
    )(parents, queries, output_gradient, *owns, foreign, *before)


def pack_kernel(parents, keys_ref, values_ref, send_ref, keep_ref, give_ref, table_ref):
    heads, width = send_ref.shape[0] // (keys_ref.shape[1] // 8), keep_ref.shape[3]
    leaves = send_ref.shape[0] // heads
    for kv, ref in enumerate((keys_ref, values_ref)):
        for h in range(heads):
            for j in range(0, leaves, 2):
                tiles = [ref[t, 8 * j : 8 * j + 16, h * width : (h + 1) * width] for t in range(2)]
                send_ref[h * leaves + j, kv] = jnp.concatenate([x[:8] for x in tiles], 0)
                send_ref[h * leaves + j + 1, kv] = jnp.concatenate([x[8:] for x in tiles], 0)
        keep_ref[kv] = ref[:, :, pl.ds(pl.multiple_of(lax.axis_index("head") * width, width), width)]
        give_ref[kv] = ref[:, :, pl.ds(pl.multiple_of((1 - lax.axis_index("head")) * width, width), width)]
    block = lax.broadcasted_iota(jnp.int32, table_ref.shape, 1)
    table = jnp.zeros(table_ref.shape, jnp.int32)
    for t in range(2):
        table = jnp.where(block == 2 * leaf_rank() + t, parents[t], table)
    table_ref[...] = table


def leaf_rank():
    return lax.axis_index("leaf")


def above(parents, block):
    return jnp.where(block >= 0, parents[0, jnp.maximum(block, 0)], -1)


def far_slots(parents, half, depth, sending, slots, start):
    base = (leaf_rank() // half) * half
    source = base if sending else half - base
    target = half - source
    t = jnp.where(source == 0, 0, 1)

    def clear(p):
        slots[start + p] = -1

    def mark(d):
        block = 2 * (target + d) + t
        for _ in range(depth):
            block = above(parents, block)
            p = block // 2 - source

            @pl.when((block >= 0) & (p >= 0) & (p < half))
            def _():
                slots[start + p] = 0

    def number(p, count):
        needed = slots[start + p] >= 0
        slots[start + p] = jnp.where(needed, count, -1)
        return count + needed.astype(jnp.int32)

    each(half, clear)
    each(half, mark)
    return lax.fori_loop(0, half, number, 0, unroll=half <= 8)


def each(count, act):
    def step(i, _):
        act(i)
        return 0

    lax.fori_loop(0, count, step, 0, unroll=count <= 8)


def each_need(parents, half, depth, trees, act):
    base = (leaf_rank() // half) * half

    def leaf(d):
        for i, t in enumerate(trees):
            block = 2 * (base + d) + t
            for k in range(depth):
                block = above(parents, block)
                p = jnp.maximum(block, 0) // 2
                here = (p >= base) & (p < base + half)
                act(d, i * depth + k, block >= 0, here, lax.rem(p, half), t)

    each(half, leaf)


def cross_kernel(depth, parents, own_ref, cross_ref, slots, count):
    half = own_ref.shape[0]
    other = far_slots(parents, half, depth, False, slots, 0)
    mine = far_slots(parents, half, depth, True, slots, half)
    count[0] = jnp.maximum(mine, other)
    t = leaf_rank() // half

    def copy(p):
        slot = slots[half + p]

        @pl.when(slot >= 0)
        def _():
            cross_ref[slot] = own_ref[p, :, t]

    each(half, copy)


def pick_near_kernel(depth, parents, own_ref, out_ref):
    half = own_ref.shape[0]
    near = leaf_rank() // half

    def act(d, k, valid, here, p, t):
        out_ref[d, k] = own_ref[p, :, t]

    each_need(parents, half, depth, (near,), act)


def pick_far_kernel(depth, parents, slots, own_ref, cross_ref, out_ref):
    half = own_ref.shape[0]
    far = 1 - leaf_rank() // half

    def act(d, k, valid, here, p, t):
        crossed = cross_ref[jnp.maximum(slots[p], 0)]
        out_ref[d, k] = jnp.where(here | ~valid, own_ref[p, :, t], crossed)

    each_need(parents, half, depth, (far,), act)


def collect_near_kernel(depth, parents, in_ref, sums):
    half = in_ref.shape[0]
    sums[...] = jnp.zeros_like(sums)

    def act(d, k, valid, here, p, t):
        sums[jnp.where(valid, p, half)] += in_ref[d, k].astype(F32)

    each_need(parents, half, depth, (leaf_rank() // half,), act)


def collect_far_kernel(depth, parents, slots, in_ref, sums, cross_ref):
    half = cross_ref.shape[0]
    sums[...] = jnp.zeros_like(sums)

    def act(d, k, valid, here, p, t):
        row = jnp.where(here, p, half + jnp.maximum(slots[p], 0))
        sums[jnp.where(valid, row, 2 * half)] += in_ref[d, k].astype(F32)

    each_need(parents, half, depth, (1 - leaf_rank() // half,), act)
    cross_ref[...] = sums[half : 2 * half].astype(BF16)


def merge_kernel(spread, slots, near_ref, far_ref, cross_ref, out_ref):
    half = cross_ref.shape[0]
    even = leaf_rank() < half

    def add(p):
        slot = slots[half + p]
        crossed = cross_ref[jnp.maximum(slot, 0)].astype(F32)
        for kv in range(2):
            near = near_ref[p, kv] + jnp.where(slot >= 0, crossed[kv], 0.0)
            far = far_ref[p, kv]
            sums = [jnp.where(even, near, far), jnp.where(even, far, near)]
            if spread:
                for h in range(2):
                    tiles = [x[8 * h : 8 * h + 8] for x in sums]
                    out_ref[h * half + p, kv] = jnp.concatenate(tiles, 0).astype(BF16)
            else:
                for i in range(2):
                    out_ref[p, kv, i] = sums[i].astype(BF16)

    each(half, add)


def finish_kernel(got_ref, own_ref, own_got_ref, keys_ref, values_ref):
    width = own_ref.shape[3]
    leaves = own_ref.shape[2] // 8
    for kv, out_ref in enumerate((keys_ref, values_ref)):
        for own in range(2):
            h = lax.axis_index("head") if own else 1 - lax.axis_index("head")
            ref = own_ref if own else own_got_ref
            lanes = pl.ds(pl.multiple_of(h * width, width), width)
            for j in range(0, leaves, 2):
                rows = slice(8 * j, 8 * j + 16)
                a, b = (got_ref[h * leaves + j + i, kv].astype(F32) for i in range(2))
                for t in range(2):
                    part = slice(8 * t, 8 * t + 8)
                    total = jnp.concatenate([a[part], b[part]], 0) + ref[kv, t, rows].astype(F32)
                    out_ref[t, rows, lanes] = total.astype(BF16)


def whole(shape):
    return pl.BlockSpec(shape, lambda i: (0,) * len(shape))


def simple(kernel, scalars, arrays, outs, slots=(), params=PARAMS):
    out_specs = [whole(x.shape) for x in outs] + [SMEM] * len(slots)
    outs = list(outs) + [jax.ShapeDtypeStruct((x,), jnp.int32) for x in slots]
    return pl.pallas_call(
        kernel,
        grid=(1,),
        in_specs=[SMEM] * len(scalars) + [whole(x.shape) for x in arrays],
        out_specs=out_specs,
        out_shape=outs,
        compiler_params=params,
    )(*scalars, *arrays)


def body(queries, keys, values, output_gradient, parents):
    leaf_count = lax.axis_size("leaf")
    head_count = lax.axis_size("head")
    half = leaf_count // 2
    depth = leaf_count // 4 - 2
    sides = [[half * i + j for j in range(half)] for i in range(2)]
    both = [[leaf_count * h + j for h in range(head_count) for j in side] for side in sides]
    swap = [(i, (i + half) % leaf_count) for i in range(leaf_count)]
    trees, part_rows, kv_all = keys.shape
    kv_width = kv_all // head_count
    rows = part_rows * head_count
    pieces = rows // half
    merged = head_count == 2 and part_rows == 8 * half and half % 2 == 0

    def exchange(x):
        return lax.all_to_all(x, "leaf", 0, 0, tiled=True, axis_index_groups=sides)

    def exchange_both(x):
        return lax.all_to_all(x, ("head", "leaf"), 0, 0, tiled=True, axis_index_groups=both)

    def to_other_head(x):
        return lax.ppermute(x, "head", [(0, 1), (1, 0)])

    def like(*shape, dtype=BF16):
        return jax.ShapeDtypeStruct(shape, dtype)

    if merged:
        send, keep, give, table = simple(
            pack_kernel,
            (parents,),
            (keys, values),
            [
                like(2 * half, 2, 16, kv_width),
                like(2, trees, part_rows, kv_width),
                like(2, trees, part_rows, kv_width),
                like(1, trees * leaf_count, dtype=jnp.int32),
            ],
            params=WIDE,
        )
        arrived, all_parents, theirs = lax.optimization_barrier(
            (exchange_both(send), lax.psum(table, "leaf"), to_other_head(give))
        )
        owns = [keep, theirs]
        arrived = arrived.reshape(2, half, 2, trees, 8, kv_width).transpose(1, 2, 3, 0, 4, 5)
        hub_own = arrived.reshape(half, 2, trees, pieces, kv_width)
    else:
        all_parents = lax.all_gather(parents, "leaf", axis=0, tiled=True).reshape(1, trees * leaf_count)
        pair = jnp.stack([keys, values]).reshape(2, trees, part_rows, head_count, kv_width)
        pair = jnp.moveaxis(pair, 3, 0)
        if head_count > 1:
            pair = lax.all_to_all(pair, "head", 0, 0, tiled=True)
        mine = pair.transpose(1, 2, 0, 3, 4).reshape(2, trees, rows, kv_width)
        hub_own = exchange(mine.reshape(2, trees, half, pieces, kv_width).transpose(2, 0, 1, 3, 4))
        owns = [mine]

    piece = (2, pieces, kv_width)
    few = min(2, half)

    def cross(x):
        def short():
            return jnp.concatenate([lax.ppermute(x[:few], "leaf", swap), x[few:]])

        return lax.cond(count[0] <= few, short, lambda: lax.ppermute(x, "leaf", swap))

    picked_shape = [like(half, depth, *piece)]
    (picked_near,) = simple(functools.partial(pick_near_kernel, depth), (all_parents,), (hub_own,), picked_shape)
    foreign_near = exchange(picked_near)
    crossing, slots, count = simple(
        functools.partial(cross_kernel, depth),
        (all_parents,),
        (hub_own,),
        [like(half, *piece)],
        slots=(2 * half, 1),
    )
    (picked_far,) = simple(
        functools.partial(pick_far_kernel, depth), (all_parents, slots), (hub_own, cross(crossing)), picked_shape
    )
    foreign_near, picked_far = lax.optimization_barrier((foreign_near, picked_far))
    foreign_far = exchange(picked_far)

    def gather_rows(x):
        if pieces % 16 == 0:
            return x
        return x.transpose(1, 2, 0, 3, 4).reshape(1, depth, 2, rows, kv_width)

    def spread_rows(x):
        if pieces % 16 == 0:
            return x
        return x.reshape(depth, 2, half, pieces, kv_width).transpose(2, 0, 1, 3, 4)

    *results, near_grad = attend(
        all_parents, queries, output_gradient, owns, gather_rows(foreign_near), True, half, ()
    )
    query_grad, *self_grads, far_grad = attend(
        all_parents, queries, output_gradient, owns, gather_rows(foreign_far), False, half, results
    )
    near_back, far_grad = lax.optimization_barrier((exchange(spread_rows(near_grad)), far_grad))
    far_back = exchange(spread_rows(far_grad))
    (near_sum,) = simple(
        functools.partial(collect_near_kernel, depth),
        (all_parents,),
        (near_back,),
        [like(half + 1, *piece, dtype=F32)],
    )
    if merged:
        far_back, near_sum, own_got = lax.optimization_barrier((far_back, near_sum, to_other_head(self_grads[1])))
    else:
        far_back, near_sum = lax.optimization_barrier((far_back, near_sum))
    far_sum, cross_sum = simple(
        functools.partial(collect_far_kernel, depth),
        (all_parents, slots),
        (far_back,),
        [like(2 * half + 1, *piece, dtype=F32), like(half, *piece)],
    )
    (hub_sum,) = simple(
        functools.partial(merge_kernel, merged),
        (slots,),
        (near_sum, far_sum, cross(cross_sum)),
        [like(2 * half, 2, 16, kv_width) if merged else like(half, 2, trees, pieces, kv_width)],
    )
    if merged:
        returned = exchange_both(hub_sum)
        return query_grad, *simple(
            finish_kernel, (), (returned, self_grads[0], own_got), [like(*keys.shape)] * 2
        )
    returned = exchange(hub_sum).transpose(1, 2, 0, 3, 4).reshape(2, trees, rows, kv_width)
    total = (returned.astype(F32) + self_grads[0].astype(F32)).astype(BF16)
    total = jnp.moveaxis(total.reshape(2, trees, head_count, part_rows, kv_width), 2, 0)
    if head_count > 1:
        total = lax.all_to_all(total, "head", 0, 0, tiled=True)
    total = total.transpose(1, 2, 3, 0, 4).reshape(2, trees, part_rows, kv_all)
    return query_grad, total[0], total[1]


def solution(mesh):
    in_specs = (
        P("leaf", None, "head"),
        P("leaf", "head", None),
        P("leaf", "head", None),
        P("leaf", None, "head"),
        P("leaf"),
    )
    out_specs = (P("leaf", None, "head"), P("leaf", "head", None), P("leaf", "head", None))
    return jax.shard_map(body, mesh=mesh, in_specs=in_specs, out_specs=out_specs, check_vma=False)
```

```python
import functools
import math

import jax
import jax.numpy as jnp
from jax import lax
from jax.experimental import pallas as pl
from jax.experimental.pallas import tpu as pltpu
from jax.sharding import PartitionSpec as P

HEAD_DIM = 128

NT = (((1,), (1,)), ((), ()))
NN = (((1,), (0,)), ((), ()))
F32 = jnp.float32
BF16 = jnp.bfloat16
SMEM = pl.BlockSpec(memory_space=pltpu.SMEM)
PARAMS = pltpu.CompilerParams(vmem_limit_bytes=40 * 1024 * 1024)
WIDE = pltpu.CompilerParams(vmem_limit_bytes=60 * 1024 * 1024)


def dot(a, b, dims=NN):
    return lax.dot_general(a, b, dims, preferred_element_type=F32)


def attend_kernel(parts, tree, parents, q_ref, do_ref, *refs):
    own_refs, anc_ref = refs[:parts], refs[parts]
    dq_ref, *dself_refs, danc_ref = refs[-parts - 2 :]
    hubs, depth, _, pieces, _ = anc_ref.shape
    rows = q_ref.shape[1]
    step_groups = anc_ref.shape[4] // HEAD_DIM
    heads = q_ref.shape[2] // HEAD_DIM // step_groups
    scale = HEAD_DIM ** (-0.5)
    c = scale * math.log2(math.e)
    block = 2 * leaf_rank() + tree()
    valid = []
    for _ in range(depth):
        block = above(parents, block)
        valid.append(block >= 0)

    def lanes(group, count=1):
        return slice(group * HEAD_DIM, (group + count) * HEAD_DIM)

    def seen(which, group):
        tiles = [anc_ref[:, k, which, :, lanes(group)].reshape(rows, HEAD_DIM) for k in range(depth)]
        return jnp.concatenate([ref[which, 0, :, lanes(group)] for ref in own_refs] + tiles, 0)

    held = [(seen(0, group), seen(1, group)) for group in range(step_groups)]
    held = [(keys, values, keys.T) for keys, values in held]
    first_token = lax.axis_index("head") * own_refs[0].shape[2] if parts == 2 else 0
    token = lax.rem(lax.broadcasted_iota(jnp.int32, (rows, rows), 0) + first_token, rows)
    hidden = token > lax.broadcasted_iota(jnp.int32, (rows, rows), 1)

    def products(group, h):
        q, do = (
            jnp.concatenate([ref[0, :, lanes(group * heads + i)] for i in range(h, h + 2)], 0)
            for ref in (q_ref, do_ref)
        )
        return group, h, q, do, dot(held[group][0], q, NT), dot(held[group][1], do, NT)

    def soften(scores, slopes):
        s = [scores[k * rows : (k + 1) * rows] for k in range(depth + 1)]
        d = [slopes[k * rows : (k + 1) * rows] for k in range(depth + 1)]
        s[0] = jnp.where(hidden, -1e30, s[0])
        peak = jnp.max(s[0], 0, keepdims=True)
        for k in range(depth):
            peak = jnp.maximum(peak, jnp.where(valid[k], jnp.max(s[k + 1], 0, keepdims=True), -1e30))
        peak = peak * c
        e = [jnp.exp2(s[0] * c - peak)]
        for k in range(depth):
            e.append(jnp.exp2(s[k + 1] * c - jnp.where(valid[k], peak, 1e30)))
        total = functools.reduce(jnp.add, [jnp.sum(x, 0, keepdims=True) for x in e])
        weighted = functools.reduce(jnp.add, [jnp.sum(x * y, 0, keepdims=True) for x, y in zip(e, d)])
        inverse = 1.0 / total
        mean = weighted * inverse
        p = [x * inverse for x in e]
        ds = [(x * (y - mean)).astype(BF16) for x, y in zip(p, d)]
        return jnp.concatenate([x.astype(BF16) for x in p], 0), jnp.concatenate(ds, 0)

    def gradients(group, h, q, do, ps, ds):
        dq_t = dot(held[group][2], ds) * scale
        for i in range(2):
            dq_ref[0, :, lanes(group * heads + h + i)] = dq_t[:, i * rows : (i + 1) * rows].T.astype(BF16)
        return dot(ds, q), dot(ps, do)

    def store(group, grads):
        for which in range(2):
            start = 0
            for ref in dself_refs:
                ref[which, 0, :, lanes(group)] = grads[which][start : start + ref.shape[2]].astype(BF16)
                start += ref.shape[2]
            for k in range(depth):
                grad = grads[which][(k + 1) * rows : (k + 2) * rows].astype(BF16)
                danc_ref[:, k, which, :, lanes(group)] = grad.reshape(hubs, pieces, HEAD_DIM)

    pairs = [(group, h) for group in range(step_groups) for h in range(0, heads, 2)]
    stage, ready, grads = products(*pairs[0]), None, None
    for i in range(len(pairs) + 1):
        following = products(*pairs[i + 1]) if i + 1 < len(pairs) else None
        soft = None
        if stage is not None:
            group, h, q, do, scores, slopes = stage
            halves = [soften(scores[:, x * rows : (x + 1) * rows], slopes[:, x * rows : (x + 1) * rows]) for x in range(2)]
            soft = (group, h, q, do, *[jnp.concatenate(x, 1) for x in zip(*halves)])
        if ready is not None:
            more = gradients(*ready)
            grads = more if grads is None else (grads[0] + more[0], grads[1] + more[1])
            if ready[1] == heads - 2:
                store(ready[0], (grads[0] * scale, grads[1]))
                grads = None
        stage, ready = following, soft


def attend(parents, queries, output_gradient, owns, foreign, near, half, before):
    _, rows, width = queries.shape
    hubs, depth, _, pieces, kv_width = foreign.shape
    groups = kv_width // HEAD_DIM
    heads = width // groups // HEAD_DIM
    step = 2 - groups % 2
    lanes = step * HEAD_DIM

    def tree():
        return leaf_rank() // half if near else 1 - leaf_rank() // half

    q_spec = pl.BlockSpec((1, rows, heads * lanes), lambda g: (tree(), 0, g))
    own_specs = [pl.BlockSpec((2, 1, x.shape[2], lanes), lambda g: (0, tree(), 0, g)) for x in owns]
    got_spec = pl.BlockSpec((hubs, depth, 2, pieces, lanes), lambda g: (0, 0, 0, 0, g))
    out_shape = [jax.ShapeDtypeStruct(x.shape, BF16) for x in (queries, *owns, foreign)]
    return pl.pallas_call(
        functools.partial(attend_kernel, len(owns), tree),
        grid=(groups // step,),
        in_specs=[SMEM, q_spec, q_spec, *own_specs, got_spec] + [pl.BlockSpec(memory_space=pl.ANY)] * len(before),
        out_specs=[q_spec, *own_specs, got_spec],
        out_shape=out_shape,
        input_output_aliases={4 + len(owns) + i: i for i in range(len(before))},
        compiler_params=pltpu.CompilerParams(vmem_limit_bytes=50 * 1024 * 1024),
        cost_estimate=pl.CostEstimate(
            flops=10 * groups * heads * (depth + 1) * rows * rows * HEAD_DIM,
            bytes_accessed=6 * rows * width,
            transcendentals=groups * heads * (depth + 1) * rows * rows,
        ),
    )(parents, queries, output_gradient, *owns, foreign, *before)


def pack_kernel(parents, keys_ref, values_ref, send_ref, keep_ref, give_ref, table_ref):
    heads, width = send_ref.shape[0] // (keys_ref.shape[1] // 8), keep_ref.shape[3]
    leaves = send_ref.shape[0] // heads
    for kv, ref in enumerate((keys_ref, values_ref)):
        for h in range(heads):
            for j in range(0, leaves, 2):
                tiles = [ref[t, 8 * j : 8 * j + 16, h * width : (h + 1) * width] for t in range(2)]
                send_ref[h * leaves + j, kv] = jnp.concatenate([x[:8] for x in tiles], 0)
                send_ref[h * leaves + j + 1, kv] = jnp.concatenate([x[8:] for x in tiles], 0)
        keep_ref[kv] = ref[:, :, pl.ds(pl.multiple_of(lax.axis_index("head") * width, width), width)]
        give_ref[kv] = ref[:, :, pl.ds(pl.multiple_of((1 - lax.axis_index("head")) * width, width), width)]
    block = lax.broadcasted_iota(jnp.int32, table_ref.shape, 1)
    table = jnp.zeros(table_ref.shape, jnp.int32)
    for t in range(2):
        table = jnp.where(block == 2 * leaf_rank() + t, parents[t], table)
    table_ref[...] = table


def leaf_rank():
    return lax.axis_index("leaf")


def above(parents, block):
    return jnp.where(block >= 0, parents[0, jnp.maximum(block, 0)], -1)


def far_slots(parents, half, depth, sending, slots, start):
    base = (leaf_rank() // half) * half
    source = base if sending else half - base
    target = half - source
    t = jnp.where(source == 0, 0, 1)

    def clear(p):
        slots[start + p] = -1

    def mark(d):
        block = 2 * (target + d) + t
        for _ in range(depth):
            block = above(parents, block)
            p = block // 2 - source

            @pl.when((block >= 0) & (p >= 0) & (p < half))
            def _():
                slots[start + p] = 0

    def number(p, count):
        needed = slots[start + p] >= 0
        slots[start + p] = jnp.where(needed, count, -1)
        return count + needed.astype(jnp.int32)

    each(half, clear)
    each(half, mark)
    return lax.fori_loop(0, half, number, 0, unroll=half <= 8)


def each(count, act):
    def step(i, _):
        act(i)
        return 0

    lax.fori_loop(0, count, step, 0, unroll=count <= 8)


def each_need(parents, half, depth, trees, act, first=0, count=None):
    base = (leaf_rank() // half) * half

    def leaf(d):
        for i, t in enumerate(trees):
            block = 2 * (base + first + d) + t
            for k in range(depth):
                block = above(parents, block)
                p = jnp.maximum(block, 0) // 2
                here = (p >= base) & (p < base + half)
                act(d, i * depth + k, block >= 0, here, lax.rem(p, half), t)

    each(count or half, leaf)


def cross_kernel(depth, parents, own_ref, cross_ref, slots, count):
    half = own_ref.shape[0]
    other = far_slots(parents, half, depth, False, slots, 0)
    mine = far_slots(parents, half, depth, True, slots, half)
    count[0] = jnp.maximum(mine, other)
    t = leaf_rank() // half

    def copy(p):
        slot = slots[half + p]

        @pl.when(slot >= 0)
        def _():
            cross_ref[slot] = own_ref[p, :, t]

    each(half, copy)


def pick_near_kernel(depth, parents, own_ref, out_ref):
    half = own_ref.shape[0]
    near = leaf_rank() // half

    def act(d, k, valid, here, p, t):
        out_ref[d, k] = own_ref[p, :, t]

    count = out_ref.shape[0]
    each_need(parents, half, depth, (near,), act, pl.program_id(0) * count, count)


def pick_far_kernel(depth, parents, slots, own_ref, cross_ref, out_ref):
    half = own_ref.shape[0]
    far = 1 - leaf_rank() // half

    def act(d, k, valid, here, p, t):
        crossed = cross_ref[jnp.maximum(slots[p], 0)]
        out_ref[d, k] = jnp.where(here | ~valid, own_ref[p, :, t], crossed)

    count = out_ref.shape[0]
    each_need(parents, half, depth, (far,), act, pl.program_id(0) * count, count)


def collect_near_kernel(depth, parents, in_ref, sums):
    half = in_ref.shape[0]
    sums[...] = jnp.zeros_like(sums)

    def act(d, k, valid, here, p, t):
        sums[jnp.where(valid, p, half)] += in_ref[d, k].astype(F32)

    each_need(parents, half, depth, (leaf_rank() // half,), act)


def collect_far_kernel(depth, parents, slots, in_ref, sums, cross_ref):
    half = cross_ref.shape[0]
    sums[...] = jnp.zeros_like(sums)

    def act(d, k, valid, here, p, t):
        row = jnp.where(here, p, half + jnp.maximum(slots[p], 0))
        sums[jnp.where(valid, row, 2 * half)] += in_ref[d, k].astype(F32)

    each_need(parents, half, depth, (1 - leaf_rank() // half,), act)
    cross_ref[...] = sums[half : 2 * half].astype(BF16)


def merge_kernel(spread, slots, near_ref, far_ref, cross_ref, out_ref):
    half = cross_ref.shape[0]
    even = leaf_rank() < half

    def add(p):
        slot = slots[half + p]
        crossed = cross_ref[jnp.maximum(slot, 0)].astype(F32)
        for kv in range(2):
            near = near_ref[p, kv] + jnp.where(slot >= 0, crossed[kv], 0.0)
            far = far_ref[p, kv]
            sums = [jnp.where(even, near, far), jnp.where(even, far, near)]
            if spread:
                for h in range(2):
                    tiles = [x[8 * h : 8 * h + 8] for x in sums]
                    out_ref[h * half + p, kv] = jnp.concatenate(tiles, 0).astype(BF16)
            else:
                for i in range(2):
                    out_ref[p, kv, i] = sums[i].astype(BF16)

    each(half, add)


def finish_kernel(got_ref, own_ref, own_got_ref, keys_ref, values_ref):
    width = own_ref.shape[3]
    leaves = own_ref.shape[2] // 8
    for kv, out_ref in enumerate((keys_ref, values_ref)):
        for own in range(2):
            h = lax.axis_index("head") if own else 1 - lax.axis_index("head")
            ref = own_ref if own else own_got_ref
            lanes = pl.ds(pl.multiple_of(h * width, width), width)
            for j in range(0, leaves, 2):
                rows = slice(8 * j, 8 * j + 16)
                a, b = (got_ref[h * leaves + j + i, kv].astype(F32) for i in range(2))
                for t in range(2):
                    part = slice(8 * t, 8 * t + 8)
                    total = jnp.concatenate([a[part], b[part]], 0) + ref[kv, t, rows].astype(F32)
                    out_ref[t, rows, lanes] = total.astype(BF16)


def whole(shape):
    return pl.BlockSpec(shape, lambda i: (0,) * len(shape))


def simple(kernel, scalars, arrays, outs, slots=(), steps=1, params=PARAMS):
    out_specs = [
        pl.BlockSpec((x.shape[0] // steps,) + x.shape[1:], lambda i, n=len(x.shape): (i,) + (0,) * (n - 1)) for x in outs
    ] + [SMEM] * len(slots)
    outs = list(outs) + [jax.ShapeDtypeStruct((x,), jnp.int32) for x in slots]
    return pl.pallas_call(
        kernel,
        grid=(steps,),
        in_specs=[SMEM] * len(scalars) + [whole(x.shape) for x in arrays],
        out_specs=out_specs,
        out_shape=outs,
        compiler_params=params,
    )(*scalars, *arrays)


def body(queries, keys, values, output_gradient, parents):
    leaf_count = lax.axis_size("leaf")
    head_count = lax.axis_size("head")
    half = leaf_count // 2
    depth = leaf_count // 4 - 2
    sides = [[half * i + j for j in range(half)] for i in range(2)]
    both = [[leaf_count * h + j for h in range(head_count) for j in side] for side in sides]
    swap = [(i, (i + half) % leaf_count) for i in range(leaf_count)]
    trees, part_rows, kv_all = keys.shape
    kv_width = kv_all // head_count
    rows = part_rows * head_count
    pieces = rows // half
    merged = head_count == 2 and part_rows == 8 * half and half % 2 == 0

    def exchange(x):
        return lax.all_to_all(x, "leaf", 0, 0, tiled=True, axis_index_groups=sides)

    def exchange_both(x):
        return lax.all_to_all(x, ("head", "leaf"), 0, 0, tiled=True, axis_index_groups=both)

    def to_other_head(x):
        return lax.ppermute(x, "head", [(0, 1), (1, 0)])

    def like(*shape, dtype=BF16):
        return jax.ShapeDtypeStruct(shape, dtype)

    if merged:
        send, keep, give, table = simple(
            pack_kernel,
            (parents,),
            (keys, values),
            [
                like(2 * half, 2, 16, kv_width),
                like(2, trees, part_rows, kv_width),
                like(2, trees, part_rows, kv_width),
                like(1, trees * leaf_count, dtype=jnp.int32),
            ],
            params=WIDE,
        )
        arrived, all_parents, theirs = lax.optimization_barrier(
            (exchange_both(send), lax.psum(table, "leaf"), to_other_head(give))
        )
        owns = [keep, theirs]
        arrived = arrived.reshape(2, half, 2, trees, 8, kv_width).transpose(1, 2, 3, 0, 4, 5)
        hub_own = arrived.reshape(half, 2, trees, pieces, kv_width)
    else:
        all_parents = lax.all_gather(parents, "leaf", axis=0, tiled=True).reshape(1, trees * leaf_count)
        pair = jnp.stack([keys, values]).reshape(2, trees, part_rows, head_count, kv_width)
        pair = jnp.moveaxis(pair, 3, 0)
        if head_count > 1:
            pair = lax.all_to_all(pair, "head", 0, 0, tiled=True)
        mine = pair.transpose(1, 2, 0, 3, 4).reshape(2, trees, rows, kv_width)
        hub_own = exchange(mine.reshape(2, trees, half, pieces, kv_width).transpose(2, 0, 1, 3, 4))
        owns = [mine]

    piece = (2, pieces, kv_width)
    few = min(2, half)

    def cross(x):
        def short():
            return jnp.concatenate([lax.ppermute(x[:few], "leaf", swap), x[few:]])

        return lax.cond(count[0] <= few, short, lambda: lax.ppermute(x, "leaf", swap))

    picked_shape = [like(half, depth, *piece)]
    (picked_near,) = simple(functools.partial(pick_near_kernel, depth), (all_parents,), (hub_own,), picked_shape, steps=2)
    foreign_near = exchange(picked_near)
    crossing, slots, count = simple(
        functools.partial(cross_kernel, depth),
        (all_parents,),
        (hub_own,),
        [like(half, *piece)],
        slots=(2 * half, 1),
    )
    (picked_far,) = simple(
        functools.partial(pick_far_kernel, depth), (all_parents, slots), (hub_own, cross(crossing)), picked_shape, steps=2
    )
    foreign_near, picked_far = lax.optimization_barrier((foreign_near, picked_far))
    foreign_far = exchange(picked_far)

    def gather_rows(x):
        if pieces % 16 == 0:
            return x
        return x.transpose(1, 2, 0, 3, 4).reshape(1, depth, 2, rows, kv_width)

    def spread_rows(x):
        if pieces % 16 == 0:
            return x
        return x.reshape(depth, 2, half, pieces, kv_width).transpose(2, 0, 1, 3, 4)

    *results, near_grad = attend(
        all_parents, queries, output_gradient, owns, gather_rows(foreign_near), True, half, ()
    )
    query_grad, *self_grads, far_grad = attend(
        all_parents, queries, output_gradient, owns, gather_rows(foreign_far), False, half, results
    )
    near_back, far_grad = lax.optimization_barrier((exchange(spread_rows(near_grad)), far_grad))
    far_back = exchange(spread_rows(far_grad))
    (near_sum,) = simple(
        functools.partial(collect_near_kernel, depth),
        (all_parents,),
        (near_back,),
        [like(half + 1, *piece, dtype=F32)],
    )
    if merged:
        far_back, near_sum, own_got = lax.optimization_barrier((far_back, near_sum, to_other_head(self_grads[1])))
    else:
        far_back, near_sum = lax.optimization_barrier((far_back, near_sum))
    far_sum, cross_sum = simple(
        functools.partial(collect_far_kernel, depth),
        (all_parents, slots),
        (far_back,),
        [like(2 * half + 1, *piece, dtype=F32), like(half, *piece)],
    )
    (hub_sum,) = simple(
        functools.partial(merge_kernel, merged),
        (slots,),
        (near_sum, far_sum, cross(cross_sum)),
        [like(2 * half, 2, 16, kv_width) if merged else like(half, 2, trees, pieces, kv_width)],
    )
    if merged:
        returned = exchange_both(hub_sum)
        return query_grad, *simple(
            finish_kernel, (), (returned, self_grads[0], own_got), [like(*keys.shape)] * 2
        )
    returned = exchange(hub_sum).transpose(1, 2, 0, 3, 4).reshape(2, trees, rows, kv_width)
    total = (returned.astype(F32) + self_grads[0].astype(F32)).astype(BF16)
    total = jnp.moveaxis(total.reshape(2, trees, head_count, part_rows, kv_width), 2, 0)
    if head_count > 1:
        total = lax.all_to_all(total, "head", 0, 0, tiled=True)
    total = total.transpose(1, 2, 3, 0, 4).reshape(2, trees, part_rows, kv_all)
    return query_grad, total[0], total[1]


def solution(mesh):
    in_specs = (
        P("leaf", None, "head"),
        P("leaf", "head", None),
        P("leaf", "head", None),
        P("leaf", None, "head"),
        P("leaf"),
    )
    out_specs = (P("leaf", None, "head"), P("leaf", "head", None), P("leaf", "head", None))
    return jax.shard_map(body, mesh=mesh, in_specs=in_specs, out_specs=out_specs, check_vma=False)
```
